32 devices in a mesh: dp: 8 (over y, x, core), tensor: 4 (over z).
Axes of the slice: x: 2, y: 2, z: 4, core: 2. Of those that a mesh axis runs over, the one named last changes fastest.
Arguments:
- hidden_in: float32 [8192, 1536], P(('dp', 'tensor')), may hold values from -6 to 6
- norm1_gain: float32 [1536], replicated, may hold values from 0.5 to 1.5
- w_query: bfloat16 [1536, 1536], P('dp', 'tensor'), may hold values from -0.625 to 0.625
- w_keyvalue: bfloat16 [2, 1536, 512], P(None, 'dp', 'tensor'), may hold values from -0.625 to 0.625
- w_output: bfloat16 [1536, 1536], P('tensor', 'dp'), may hold values from -0.625 to 0.625
- norm2_gain: float32 [1536], replicated, may hold values from 0.5 to 1.5
- w_router: bfloat16 [1536, 32], replicated, may hold values from -0.078125 to 0.078125
- w_gate_up: bfloat16 [32, 2, 1536, 512], P(('dp', 'tensor')), may hold values from -0.15625 to 0.15625
- w_down: bfloat16 [32, 512, 1536], P(('dp', 'tensor')), may hold values from -6 to 6
- expert_ids: int32 [8192, 8], P(('dp', 'tensor')), may hold values from 0 to 31, all different within a row; in each aligned block of 256 rows (0 to 255, 256 to 511, ...) at most 88 rows name the same one
- choice_scale: float32 [8192, 8], P(('dp', 'tensor')), may hold values from 0.7 to 1.4
- out_grad: float32 [8192, 1536], P(('dp', 'tensor')), may hold values from -6 to 6
Outputs:
- output: float32 [8192, 1536], P(('dp', 'tensor'))
- grad_hidden: float32 [8192, 1536], P(('dp', 'tensor'))
- grad_norm1_gain: float32 [1536], replicated
- grad_w_query: float32 [1536, 1536], P('dp', 'tensor')
- grad_w_keyvalue: float32 [2, 1536, 512], P(None, 'dp', 'tensor')
- grad_w_output: float32 [1536, 1536], P('tensor', 'dp')
- grad_norm2_gain: float32 [1536], replicated
- grad_w_router: float32 [1536, 32], replicated
- grad_w_gate_up: float32 [32, 2, 1536, 512], P(('dp', 'tensor'))
- grad_w_down: float32 [32, 512, 1536], P(('dp', 'tensor'))
The draws below stay inside these ranges and needn't reach their ends.
Inputs may be any that keep to these rules, and one draw needn't show every extreme that they name: `expert_ids`: each row names 8 different experts. Within the 256 rows of one device no expert is named more than 88 times, a bound that some block reaches.
All inputs are finite; a program needn't handle non-finite values.
Results may differ from the reference program's by a relative error of at most 0.022.
Values may be sent and summed in bfloat16 or wider, within the bound.
No kernel may reach another device: no remote copies, remote signals or barrier semaphores. Data moves between devices by JAX's collectives and lax.ppermute only.
A program may use at most 256 MiB of HBM per device.

```python
import math
import jax
import jax.numpy as jnp
import numpy as np
from jax import lax

D = 1536
HEADS = 24
KV_HEADS = 8
HEAD = 64
EXP_FF = 512
TOPK = 8
TOK_DEV = 256
SEQ = 1024
TOKENS = 8192
EXPERTS = 32
CAP = 88
N_DP = 8
N_TENSOR = 4


def shard_levels(stream_key, dims, cuts, least, high):
    factor_of = 1.0
    for position, parts in cuts:
        steps = jax.random.uniform(jax.random.fold_in(jax.random.fold_in(stream_key, 6), position), (parts,), jnp.float32, least / len(cuts), high / len(cuts))
        factor_of = factor_of * jnp.repeat(jnp.exp(steps), dims[position] // parts).reshape((-1,) + (1,) * (len(dims) - 1 - position))
    return factor_of


def deal_out(own_key, own, number, rows, count, top, most, skew):
    sequence = jax.random.permutation(own_key, count)
    heavy_load, ordinary = portions_of(count, rows * top, most, skew, True), portions_of(count, rows * top, most, skew, False)
    places = jnp.arange(count)

    def named(tallies, turn):
        used = int((tallies > 0).sum())
        fixed = max(1, used // 4)
        moved = fixed + (places - fixed + turn * (used - fixed)) % max(1, count - fixed)
        return jnp.zeros((count,), jnp.int32).at[sequence[jnp.where(places < fixed, places, moved)]].set(jnp.asarray(tallies, jnp.int32))

    tallies = jnp.where(number % 4 == 0, named(heavy_load, number // 4), named(ordinary, number - number // 4 - 1))
    mixed = jax.random.permutation(jax.random.fold_in(own, 3), count)
    donor, sink = mixed[0:count // 2 * 2:2], mixed[1:count // 2 * 2:2]
    margin = jnp.minimum(tallies[donor] - 1, most - tallies[sink]) // 2
    margin = jnp.where((donor == sequence[0]) | (sink == sequence[0]) | (tallies[sink] == 0), 0, jnp.maximum(margin, 0))
    moved = jax.random.randint(jax.random.fold_in(own, 4), (count // 2,), 0, 1 << 20) % (margin + 1)
    tallies = tallies.at[donor].add(-moved).at[sink].add(moved)
    labels = jnp.searchsorted(jnp.cumsum(tallies), jnp.arange(rows * top), side="right").astype(jnp.int32)
    grid = labels.reshape(top, rows).T
    grid = grid[jax.random.permutation(jax.random.fold_in(own, 1), rows)]
    turn = jax.random.randint(jax.random.fold_in(own, 2), (rows, 1), 0, top)
    return jnp.take_along_axis(grid, (jnp.arange(top)[None, :] + turn) % top, axis=1)


def portions_of(number_of, total, bound, lean, full):
    portions = [(1 << 20) // math.isqrt(standing ** lean) + 1 for standing in range(1, number_of + 1)]
    largest = bound if full else min(bound, max(-(-total // number_of), total * portions[0] // sum(portions)))
    least = 1 if total - largest >= number_of - 1 else 0
    given, surplus = [largest] + [least] * (number_of - 1), total - largest - least * (number_of - 1)
    while surplus > 0:
        free = [i for i in range(1, number_of) if given[i] < largest] or [i for i in range(1, number_of) if given[i] < bound]
        whole, left = sum([portions[i] for i in free]), surplus
        for i in free:
            more = min(bound - given[i], max(1, left * portions[i] // whole), surplus)
            given[i] = given[i] + more
            surplus = surplus - more
    return np.array(given)


def scatter_about(rng, shape, scale, reach, cuts=(), kind=jnp.bfloat16):
    values = jax.random.normal(rng, shape, jnp.float32) * scale
    if len(cuts) > 0:
        values = shard_levels(rng, shape, cuts, -0.22, 0.18) * values
    return jnp.clip(values, min=-reach, max=reach).astype(kind)


def setup_inputs(seed: int = 0) -> dict:
    arg_keys = jax.random.split(jax.random.key(seed), 13)
    hidden_in = scatter_about(arg_keys[0], (TOKENS, D), 1.0, 6.0, ((0, 32),), jnp.float32)
    norm1_gain = jnp.clip(1.0 + 0.1 * jax.random.normal(arg_keys[1], (D,), jnp.float32), 0.5, 1.5)
    w_query = scatter_about(arg_keys[2], (D, HEADS * HEAD), (D // 16) ** -0.5, 0.625, ((0, 8), (1, 4)))
    w_keyvalue = scatter_about(arg_keys[3], (2, D, KV_HEADS * HEAD), (D // 16) ** -0.5, 0.625, ((1, 8), (2, 4)))
    w_output = scatter_about(arg_keys[4], (HEADS * HEAD, D), (D // 16) ** -0.5, 0.625, ((0, 4), (1, 8)))
    norm2_gain = jnp.clip(1.0 + 0.1 * jax.random.normal(arg_keys[5], (D,), jnp.float32), 0.5, 1.5)
    w_router = scatter_about(arg_keys[6], (D, EXPERTS), (4 * D) ** -0.5, 0.078125)
    w_gate_up = scatter_about(arg_keys[7], (EXPERTS, 2, D, EXP_FF), D ** -0.5, 0.15625, ((0, 32),))
    w_down = scatter_about(arg_keys[8], (EXPERTS, EXP_FF, D), 1 ** -0.5, 6.0, ((0, 32),))
    expert_ids_keys = jax.random.split(jax.random.fold_in(arg_keys[9], 1), TOKENS // TOK_DEV)
    expert_ids_turns = jax.random.permutation(jax.random.fold_in(arg_keys[9], 3), TOKENS // TOK_DEV)
    expert_ids = jax.vmap(lambda own, number: deal_out(jax.random.fold_in(arg_keys[9], 2), own, number, TOK_DEV, EXPERTS, TOPK, CAP, 1))(expert_ids_keys, expert_ids_turns).reshape((TOKENS, TOPK))
    choice_scale = jnp.clip(jnp.exp(math.log(1.4) - 0.6931472 * jax.random.uniform(arg_keys[10], (TOKENS, TOPK), jnp.float32) ** shard_levels(arg_keys[10], (TOKENS, TOPK), ((0, 32),), -0.2, 0.2)), 0.7, 1.4)
    out_grad = scatter_about(arg_keys[11], (TOKENS, D), 1.0, 6.0, ((0, 32),), jnp.float32)
    return {"hidden_in": hidden_in, "norm1_gain": norm1_gain, "w_query": w_query, "w_keyvalue": w_keyvalue, "w_output": w_output, "norm2_gain": norm2_gain, "w_router": w_router, "w_gate_up": w_gate_up, "w_down": w_down, "expert_ids": expert_ids, "choice_scale": choice_scale, "out_grad": out_grad}


EPSILON = 1e-06
ATTN_SCALE = 0.015625
RESIDUAL_SCALE = 0.22
THETA = 10000.0
HIGHEST = lax.Precision.HIGHEST

@jax.custom_vjp
def low(v):
    return lax.optimization_barrier(v.astype(jnp.bfloat16)).astype(jnp.float32)

@jax.custom_vjp
def low_back(v):
    return v

def low_keep(v):
    return (low(v), None)

def low_pass(kept, grad):
    return (grad,)

def back_keep(v):
    return (v, None)

def back_low(kept, grad):
    return (low(grad),)
low.defvjp(low_keep, low_pass)
low_back.defvjp(back_keep, back_low)

def rotary_tables(length, head_width):
    half_width = head_width // 2
    frequency = THETA ** (-2.0 * jnp.arange(half_width, dtype=jnp.float32) / head_width)
    angles = jnp.arange(length, dtype=jnp.float32)[:, None] * frequency[None, :]
    return (jnp.cos(angles), jnp.sin(angles))

def rotate(values, cosine_table, sine_table, direction):
    half_width = values.shape[-1] // 2
    front_half = values[..., :half_width]
    back_half = values[..., half_width:]
    cosine_part = cosine_table[:, None, :]
    sine_part = direction * sine_table[:, None, :]
    return jnp.concatenate([front_half * cosine_part - back_half * sine_part, back_half * cosine_part + front_half * sine_part], axis=-1)

def slot_tables(choice_ids, expert_count, capacity):
    row_count, pick_count = choice_ids.shape
    flat_ids = choice_ids.reshape(row_count * pick_count)
    one_hot = (flat_ids[:, None] == jnp.arange(expert_count, dtype=jnp.int32)[None, :]).astype(jnp.int32)
    earlier = jnp.cumsum(one_hot, axis=0) - one_hot
    ranking = lax.optimization_barrier(jnp.sum(earlier * one_hot, axis=1))
    target = (flat_ids * capacity + ranking).astype(jnp.int32)
    holder = jnp.full((expert_count * capacity,), row_count * pick_count, jnp.int32)
    holder = holder.at[target].set(jnp.arange(row_count * pick_count, dtype=jnp.int32))
    return (target, holder)

def norm_rows(values, gain):
    inverse = lax.rsqrt(lax.optimization_barrier(jnp.mean(values * values, axis=-1, keepdims=True)) + EPSILON)
    return values * inverse * gain

def attend_group(query_group, key_group, value_group):
    scores = jnp.einsum('qrw,kw->rqk', query_group, key_group, precision=HIGHEST) * ATTN_SCALE
    length = key_group.shape[0]
    causal = jnp.arange(length)[:, None] >= jnp.arange(length)[None, :]
    scores = jnp.where(causal[None], low_back(scores), -1e+30)
    weights = low(jax.nn.softmax(scores, axis=-1))
    return jnp.einsum('rqk,kw->qrw', weights, value_group, precision=HIGHEST)

def take_rows(row_table, index_table):
    return jnp.take(row_table, index_table, axis=0)

def sequence_forward(params, hidden_seq, ids_seq, scale_seq):
    norm1_gain, w_query, w_keyvalue, w_output, norm2_gain, w_router, w_gate_up, w_down = params
    length = hidden_seq.shape[0]
    group_size = HEADS // KV_HEADS
    normed = low(norm_rows(hidden_seq, norm1_gain))
    queries = low_back(jnp.dot(normed, w_query, precision=HIGHEST))
    keys = low_back(jnp.dot(normed, w_keyvalue[0], precision=HIGHEST))
    values = low(low_back(jnp.dot(normed, w_keyvalue[1], precision=HIGHEST)))
    cosine_table, sine_table = rotary_tables(length, HEAD)
    queries = low(rotate(queries.reshape(length, HEADS, HEAD), cosine_table, sine_table, 1.0))
    keys = low(rotate(keys.reshape(length, KV_HEADS, HEAD), cosine_table, sine_table, 1.0))
    values = values.reshape(length, KV_HEADS, HEAD)
    grouped = queries.reshape(length, KV_HEADS, group_size, HEAD).transpose(1, 0, 2, 3)
    mixed = lax.map(jax.checkpoint(lambda pieces: attend_group(pieces[0], pieces[1], pieces[2])), (grouped, keys.transpose(1, 0, 2), values.transpose(1, 0, 2)))
    attended = low(low_back(mixed.transpose(1, 0, 2, 3).reshape(length, HEADS * HEAD)))
    branch = low_back(jnp.dot(attended, w_output, precision=HIGHEST))
    middle = hidden_seq + RESIDUAL_SCALE * branch
    normed_two = low(norm_rows(middle, norm2_gain))
    logits = low_back(jnp.dot(normed_two, w_router, precision=HIGHEST))
    chosen = jnp.take_along_axis(logits, ids_seq, axis=1)
    gate_weights = jax.nn.softmax(chosen, axis=-1) * scale_seq
    blocks = ids_seq.reshape(N_TENSOR, TOK_DEV, TOPK)
    target, holder = jax.vmap(lambda block_ids: slot_tables(block_ids, EXPERTS, CAP))(blocks)
    padded = jnp.concatenate([normed_two.reshape(N_TENSOR, TOK_DEV, D), jnp.zeros((N_TENSOR, 1, D), jnp.float32)], axis=1)
    routed = low_back(jax.vmap(take_rows)(padded, holder // TOPK))
    routed = routed.reshape(N_TENSOR, EXPERTS, CAP, D).transpose(1, 0, 2, 3).reshape(EXPERTS, N_TENSOR * CAP, D)
    gate_up = jnp.einsum('emd,ecdf->emcf', routed, w_gate_up, precision=HIGHEST)
    gate_pre = low_back(gate_up[:, :, 0])
    up_pre = low_back(gate_up[:, :, 1])
    activated = low(jax.nn.silu(gate_pre) * up_pre)
    expert_out = low(low_back(jnp.einsum('emf,efd->emd', activated, w_down, precision=HIGHEST)))
    expert_out = expert_out.reshape(EXPERTS, N_TENSOR, CAP, D).transpose(1, 0, 2, 3).reshape(N_TENSOR, EXPERTS * CAP, D)
    picked = jax.vmap(take_rows)(expert_out, target).reshape(length, TOPK, D)
    combined = jnp.einsum('tk,tkd->td', gate_weights, picked, precision=HIGHEST)
    return middle + RESIDUAL_SCALE * combined

def reference(hidden_in, norm1_gain, w_query, w_keyvalue, w_output, norm2_gain, w_router, w_gate_up, w_down, expert_ids, choice_scale, out_grad):
    params = (norm1_gain.astype(jnp.float32), w_query.astype(jnp.float32), w_keyvalue.astype(jnp.float32), w_output.astype(jnp.float32), norm2_gain.astype(jnp.float32), w_router.astype(jnp.float32), w_gate_up.astype(jnp.float32), w_down.astype(jnp.float32))
    hidden_all = hidden_in.astype(jnp.float32)
    ids_all = expert_ids.reshape(N_DP, SEQ, TOPK)
    scale_all = choice_scale.astype(jnp.float32).reshape(N_DP, SEQ, TOPK)

    def forward(params_in, hidden_values):
        per_sequence = lax.map(jax.checkpoint(lambda pieces: sequence_forward(params_in, pieces[0], pieces[1], pieces[2])), (hidden_values.reshape(N_DP, SEQ, D), ids_all, scale_all))
        return per_sequence.reshape(TOKENS, D)
    output, pullback = jax.vjp(forward, params, hidden_all)
    param_grads, grad_hidden = pullback(out_grad.astype(jnp.float32))
    return (output, grad_hidden, param_grads[0], param_grads[1], param_grads[2], param_grads[3], param_grads[4], param_grads[5], param_grads[6], param_grads[7])
```

```python
import functools
import math

import jax
import jax.numpy as jnp
from jax import lax
from jax.experimental import pallas as pl
from jax.experimental.pallas import tpu as pltpu
from jax.sharding import Mesh
from jax.sharding import PartitionSpec as P

HEAD = 64
EPSILON = 1e-06
ATTN_SCALE = 0.015625
RESIDUAL_SCALE = 0.22
THETA = 10000.0
BLOCK_LIMIT = 512
F32 = jnp.float32
BF16 = jnp.bfloat16
SWAP = [(0, 1), (1, 0)]
VMEM_LIMIT = 56 * 1024 * 1024

ROWS = ("yh", "yl", "xh", "xl", "core")
ALL = ROWS + ("z",)


def swap(value, axis):
    return lax.ppermute(value, axis, SWAP)


def dot(a, b, dims):
    return lax.dot_general(a, b, (dims, ((), ())), preferred_element_type=F32)


def rotary_tables(length, head_width):
    half_width = head_width // 2
    frequency = THETA ** (-2.0 * jnp.arange(half_width, dtype=F32) / head_width)
    angles = jnp.arange(length, dtype=F32)[:, None] * frequency[None, :]
    return (jnp.cos(angles), jnp.sin(angles))


def rotate(values, cosine_table, sine_table, direction):
    half_width = values.shape[-1] // 2
    front_half = values[..., :half_width]
    back_half = values[..., half_width:]
    cosine_part = cosine_table[:, None, :]
    sine_part = direction * sine_table[:, None, :]
    return jnp.concatenate(
        [
            front_half * cosine_part - back_half * sine_part,
            back_half * cosine_part + front_half * sine_part,
        ],
        axis=-1,
    )


def norm_rows(values, gain):
    inverse = lax.rsqrt(jnp.mean(values * values, axis=-1, keepdims=True) + EPSILON)
    scaled = values * inverse
    return (scaled * gain, inverse, scaled)


def norm_back(grad_normed, scaled, inverse, gain):
    grad_scaled = grad_normed * gain
    return inverse * (
        grad_scaled - scaled * jnp.mean(grad_scaled * scaled, axis=-1, keepdims=True)
    )


def line_gather(value, size):
    z = lax.axis_index("z")
    whole = jnp.zeros((size,) + value.shape, value.dtype)
    whole = lax.dynamic_update_index_in_dim(whole, value, z, 0)
    for step in range(1, size):
        value = lax.ppermute(value, "z", [(i, (i + 1) % size) for i in range(size)])
        whole = lax.dynamic_update_index_in_dim(whole, value, lax.rem(z + size - step, size), 0)
    return whole


def line_scatter(value, size):
    z = lax.axis_index("z")

    def term(step):
        return lax.dynamic_index_in_dim(value, lax.rem(z + 2 * size - 1 - step, size), 0, False)

    running = term(0)
    for step in range(1, size):
        running = lax.ppermute(running, "z", [(i, (i + 1) % size) for i in range(size)])
        if step < size - 1:
            running = term(step) + running
    return term(size - 1).astype(F32) + running.astype(F32) if size > 1 else value[0].astype(F32)


def rows_scatter(value, high):
    shape = value.shape[1:]
    value = value.reshape((high, 2, high, 4) + shape)
    if high > 1:
        value = lax.psum_scatter(value, "yh", scatter_dimension=0, tiled=True)
        value = lax.psum_scatter(value, "xh", scatter_dimension=2, tiled=True)
    value = value.reshape((2, 2, 2) + shape)
    for dim, axis in ((2, "core"), (1, "xl"), (0, "yl")):
        place = lax.axis_index(axis)
        mine = lax.dynamic_index_in_dim(value, place, dim, False)
        other = lax.dynamic_index_in_dim(value, 1 - place, dim, False)
        value = mine.astype(F32) + swap(other, axis).astype(F32)
        if dim > 0:
            value = value.astype(BF16)
    return value


def total(value, sizes):
    for axis in ALL:
        step = 1
        while step < sizes[axis]:
            pairs = [(i, i ^ step) for i in range(sizes[axis])]
            value = value + lax.ppermute(value, axis, pairs)
            step *= 2
    return value


def tokens_gather(value, sizes):
    line = line_gather(value, sizes["z"])
    both = jnp.concatenate([line, swap(line, "core")], axis=0)
    if sizes["yh"] > 1:
        both = lax.all_gather(both, ("yh", "xh"), axis=0, tiled=True)
    return both


def tokens_scatter(value, sizes):
    if sizes["yh"] > 1:
        value = lax.psum_scatter(value, ("yh", "xh"), scatter_dimension=0, tiled=True)
    size = sizes["z"]
    line = value[:size] + swap(value[size:], "core")
    return line_scatter(line, size)


def dispatch_kernel(experts, slots, place_ref, rows_ref, out_ref):
    rank = lax.broadcasted_iota(jnp.int32, (slots, rows_ref.shape[1]), 0).astype(F32)
    pick = jnp.concatenate(
        [
            jnp.where(rank == place_ref[0, e : e + 1, :], 1.0, 0.0).astype(BF16)
            for e in range(experts)
        ],
        axis=0,
    )
    out = dot(pick, rows_ref[0], ((1,), (0,))).astype(BF16)
    for e in range(experts):
        out_ref[e, 0] = out[e * slots : (e + 1) * slots]


def dispatch(place, rows, slots):
    blocks, experts, tokens = place.shape
    width = rows.shape[-1]
    return pl.pallas_call(
        functools.partial(dispatch_kernel, experts, slots),
        grid=(blocks,),
        in_specs=[
            pl.BlockSpec((1, experts, tokens), lambda b: (b, 0, 0)),
            pl.BlockSpec((1, tokens, width), lambda b: (b, 0, 0)),
        ],
        out_specs=pl.BlockSpec((experts, 1, slots, width), lambda b: (0, b, 0, 0)),
        out_shape=jax.ShapeDtypeStruct((experts, blocks, slots, width), BF16),
        compiler_params=pltpu.CompilerParams(vmem_limit_bytes=VMEM_LIMIT),
        cost_estimate=pl.CostEstimate(
            flops=2 * blocks * experts * slots * tokens * width,
            bytes_accessed=2 * blocks * width * (tokens + experts * slots),
            transcendentals=0,
        ),
        name="dispatch",
    )(place, rows)


def combine_kernel(experts, slots, place_ref, *refs):
    out_ref = refs[-1]
    tokens = out_ref.shape[1]
    lane = lax.broadcasted_iota(jnp.int32, (tokens, experts * slots), 1).astype(F32)
    hit = lane == place_ref[0, :, 0:1]
    for e in range(1, experts):
        hit = hit | (lane == place_ref[0, :, e : e + 1])
    pick = jnp.where(hit, 1.0, 0.0).astype(BF16)
    rows = jnp.concatenate([ref[...] for ref in refs[:-1]], axis=0)
    out_ref[0] = dot(pick, rows, ((1,), (0,))).astype(BF16)


def combine(place, parts, slots):
    blocks, tokens, experts = place.shape
    width = parts[0].shape[-1]
    return pl.pallas_call(
        functools.partial(combine_kernel, experts, slots),
        grid=(blocks,),
        in_specs=[pl.BlockSpec((1, tokens, experts), lambda b: (b, 0, 0))]
        + [pl.BlockSpec((slots, width), lambda b: (b, 0))] * experts,
        out_specs=pl.BlockSpec((1, tokens, width), lambda b: (b, 0, 0)),
        out_shape=jax.ShapeDtypeStruct((blocks, tokens, width), BF16),
        compiler_params=pltpu.CompilerParams(vmem_limit_bytes=VMEM_LIMIT),
        cost_estimate=pl.CostEstimate(
            flops=2 * blocks * experts * slots * tokens * width,
            bytes_accessed=2 * blocks * width * (tokens + experts * slots),
            transcendentals=0,
        ),
        name="combine",
    )(place, *parts)


def expert_kernel(width, x_ref, g_ref, s_ref, wa_ref, wb_ref, y_ref, r_ref, t_ref, da_ref, db_ref, sum_a, sum_b):
    step = pl.program_id(0)
    hidden = wa_ref.shape[1]
    half = hidden // 2
    cuts = width // hidden
    x = x_ref[...]
    weight = s_ref[...]
    grad = g_ref[...].astype(F32) * RESIDUAL_SCALE
    gate = dot(x, wa_ref[:width], ((1,), (0,)))
    up = dot(x, wb_ref[:width], ((1,), (0,)))
    sigmoid = 1.0 / (1.0 + jnp.exp(-gate))
    silu = gate * sigmoid
    active = (silu * up).astype(BF16)

    def down(ref, cut):
        return ref[width + cut * half : width + (cut + 1) * half, :]

    grad_out = (grad * weight).astype(BF16)
    through = 0.0
    grad_a = grad_b = 0.0
    for cut in range(cuts):
        columns = slice(cut * hidden, (cut + 1) * hidden)
        out = dot(active[:, :half], down(wa_ref, cut), ((1,), (0,)))
        out = out + dot(active[:, half:], down(wb_ref, cut), ((1,), (0,)))
        out = out.astype(BF16).astype(F32)
        through = through + jnp.sum(out * grad[:, columns], axis=1, keepdims=True)
        y_ref[:, columns] = (out * weight).astype(BF16)
        grad_a = grad_a + dot(grad_out[:, columns], down(wa_ref, cut), ((1,), (1,)))
        grad_b = grad_b + dot(grad_out[:, columns], down(wb_ref, cut), ((1,), (1,)))
    t_ref[...] = through
    grad_active = jnp.concatenate([grad_a, grad_b], axis=1)
    grad_gate = (grad_active * up * sigmoid * (1.0 + gate * (1.0 - sigmoid))).astype(BF16)
    grad_up = (grad_active * silu).astype(BF16)
    rows = dot(grad_gate, wa_ref[:width], ((1,), (1,)))
    rows = rows + dot(grad_up, wb_ref[:width], ((1,), (1,)))
    r_ref[...] = rows.astype(BF16)

    def add(target, start, left, right):
        part = dot(left, right, ((0,), (0,)))
        place = slice(start, start + part.shape[0])

        @pl.when(step == 0)
        def _():
            target[place] = part

        @pl.when(step > 0)
        def _():
            target[place] += part

    add(sum_a, 0, x, grad_gate)
    add(sum_b, 0, x, grad_up)
    for cut in range(cuts):
        columns = slice(cut * hidden, (cut + 1) * hidden)
        add(sum_a, width + cut * half, active[:, :half], grad_out[:, columns])
        add(sum_b, width + cut * half, active[:, half:], grad_out[:, columns])

    @pl.when(step == pl.num_programs(0) - 1)
    def _():
        da_ref[...] = sum_a[...].astype(BF16)
        db_ref[...] = sum_b[...].astype(BF16)


def expert(which, x, g, weight, half_a, half_b):
    _, slots, width = x.shape
    packed, hidden = half_a.shape[-2:]
    chunk = max(c for c in range(16, 385, 16) if slots % c == 0)

    def at_rows(n):
        return pl.BlockSpec((None, chunk, n), lambda i: (which, i, 0))

    def fixed(array, place):
        if array.ndim == 2:
            return pl.BlockSpec((packed, hidden), lambda i: (0, 0))
        return pl.BlockSpec((None, packed, hidden), lambda i: (place, 0, 0))

    def out_rows(n):
        return pl.BlockSpec((chunk, n), lambda i: (i, 0))

    whole = pl.BlockSpec((packed, hidden), lambda i: (0, 0))
    return pl.pallas_call(
        functools.partial(expert_kernel, width),
        grid=(slots // chunk,),
        in_specs=[at_rows(width), at_rows(width), at_rows(1), fixed(half_a, 0), fixed(half_b, 1)],
        out_specs=[out_rows(width), out_rows(width), out_rows(1), whole, whole],
        out_shape=[
            jax.ShapeDtypeStruct((slots, width), BF16),
            jax.ShapeDtypeStruct((slots, width), BF16),
            jax.ShapeDtypeStruct((slots, 1), F32),
            jax.ShapeDtypeStruct((packed, hidden), BF16),
            jax.ShapeDtypeStruct((packed, hidden), BF16),
        ],
        scratch_shapes=[pltpu.VMEM((packed, hidden), F32), pltpu.VMEM((packed, hidden), F32)],
        compiler_params=pltpu.CompilerParams(vmem_limit_bytes=VMEM_LIMIT),
        cost_estimate=pl.CostEstimate(
            flops=18 * slots * width * hidden,
            bytes_accessed=8 * slots * width + 12 * width * hidden,
            transcendentals=slots * hidden,
        ),
        name="expert",
    )(x, g, weight, half_a, half_b)


def pack_halves(gate_up, down):
    _, width, hidden = gate_up.shape
    blocks = down.reshape(2, hidden // 2, width // hidden, hidden).transpose(0, 2, 1, 3)
    return jnp.concatenate([gate_up, blocks.reshape(2, -1, hidden)], axis=1)


def unpack_halves(packed, width):
    hidden = packed.shape[-1]
    blocks = packed[:, width:].reshape(2, width // hidden, hidden // 2, hidden)
    return packed[:, :width], blocks.transpose(0, 2, 1, 3).reshape(hidden, width)


def attention_scores(query_block, key_prefix, row_start):
    scores = (
        jnp.einsum("qgrw,kgw->grqk", query_block, key_prefix, preferred_element_type=F32)
        * ATTN_SCALE
    )
    row_places = row_start + jnp.arange(query_block.shape[0])
    key_places = jnp.arange(key_prefix.shape[0])
    causal = row_places[:, None] >= key_places[None, :]
    return jnp.where(causal[None, None], scores, -1e30)


def attend(query_grouped, key_rot, value_low):
    length = query_grouped.shape[0]
    block_size = min(BLOCK_LIMIT, length)
    attended_parts, total_parts = [], []
    for row_start in range(0, length, block_size):
        row_stop = row_start + block_size
        scores = attention_scores(query_grouped[row_start:row_stop], key_rot[:row_stop], row_start)
        row_max = jnp.max(scores, axis=-1, keepdims=True)
        exponent = jnp.exp(scores - row_max)
        row_total = jnp.sum(exponent, axis=-1, keepdims=True)
        probs_low = (exponent / row_total).astype(BF16)
        attended_parts.append(
            jnp.einsum(
                "grqk,kgw->qgrw", probs_low, value_low[:row_stop], preferred_element_type=F32
            )
        )
        total_parts.append(row_max + jnp.log(row_total))
    return jnp.concatenate(attended_parts, axis=0), jnp.concatenate(total_parts, axis=2)


def attend_back(query_grouped, key_rot, value_low, log_total, grad_attended):
    length, groups, _, head = query_grouped.shape
    block_size = min(BLOCK_LIMIT, length)
    grad_query_parts = []
    grad_key_rot = jnp.zeros((length, groups, head), F32)
    grad_value = jnp.zeros((length, groups, head), F32)
    for row_start in range(0, length, block_size):
        row_stop = row_start + block_size
        query_block = query_grouped[row_start:row_stop]
        scores = attention_scores(query_block, key_rot[:row_stop], row_start)
        probs = jnp.exp(scores - log_total[:, :, row_start:row_stop])
        grad_block = grad_attended[row_start:row_stop]
        grad_probs = jnp.einsum(
            "qgrw,kgw->grqk", grad_block, value_low[:row_stop], preferred_element_type=F32
        )
        grad_scores = (
            probs * (grad_probs - jnp.sum(probs * grad_probs, axis=-1, keepdims=True))
        ).astype(BF16)
        grad_query_parts.append(
            ATTN_SCALE
            * jnp.einsum(
                "grqk,kgw->qgrw", grad_scores, key_rot[:row_stop], preferred_element_type=F32
            )
        )
        grad_key_rot = grad_key_rot.at[:row_stop].add(
            ATTN_SCALE
            * jnp.einsum("grqk,qgrw->kgw", grad_scores, query_block, preferred_element_type=F32)
        )
        grad_value = grad_value.at[:row_stop].add(
            jnp.einsum(
                "grqk,qgrw->kgw", probs.astype(BF16), grad_block, preferred_element_type=F32
            )
        )
    return jnp.concatenate(grad_query_parts, axis=0), grad_key_rot, grad_value


def chosen_tables(ids, scale, expert_count):
    lead = (1,) * (ids.ndim - 2)
    numbers = jnp.arange(expert_count, dtype=F32).reshape(lead + (1, expert_count, 1))
    hits = ids[..., :, None, :] == numbers
    mask = jnp.any(hits, axis=-3)
    return mask, jnp.sum(jnp.where(hits, scale[..., :, None, :], 0.0), axis=-3)


def masked_softmax(logits, mask, axis):
    top = jnp.max(jnp.where(mask, logits, -jnp.inf), axis=axis, keepdims=True)
    exponent = jnp.where(mask, jnp.exp(jnp.where(mask, logits - top, 0.0)), 0.0)
    return exponent / jnp.sum(exponent, axis=axis, keepdims=True)


def local(
    sizes,
    hidden_in,
    norm1_gain,
    w_query,
    w_keyvalue,
    w_output,
    norm2_gain,
    w_router,
    w_gate_up,
    w_down,
    expert_ids,
    choice_scale,
    out_grad,
):
    tok_rows, model_width = hidden_in.shape
    pick_count = expert_ids.shape[1]
    expert_count = w_router.shape[1]
    capacity = max(2, (tok_rows * pick_count * 11 + 8 * expert_count - 1) // (8 * expert_count))
    slots = -(-capacity // 16) * 16
    zs, high = sizes["z"], sizes["yh"]
    yl, xl, core, z = (lax.axis_index(a) for a in ("yl", "xl", "core", "z"))
    yh, xh = lax.axis_index("yh"), lax.axis_index("xh")

    normed_one, inverse_one, scaled_one = norm_rows(hidden_in, norm1_gain)
    normed_low = normed_one.astype(BF16)
    seq_rows = line_gather(normed_low, zs).reshape(zs * tok_rows, model_width)
    packed = jnp.concatenate([w_query, w_keyvalue[0], w_keyvalue[1]], axis=1)
    w_in = lax.all_gather(packed, ROWS, axis=0, tiled=True)
    query_width = w_query.shape[1]
    kv_width = w_keyvalue.shape[2]
    w_out = lax.all_gather(lax.all_gather(w_output.T, "z", axis=0), ROWS, axis=0)
    w_out = w_out.transpose(1, 0, 2, 3).reshape(zs, model_width, w_output.shape[0])
    meta = jnp.concatenate([expert_ids.astype(F32).T, choice_scale.T], axis=0)
    meta_all = lax.all_gather(meta, ("yh", "xh", "core", "z"), axis=0)
    meta_all = meta_all.reshape((high * high, 2, zs) + meta.shape)
    meta_all = jnp.where(core == 1, meta_all[:, ::-1], meta_all)
    meta_all = meta_all.reshape((-1,) + meta.shape)
    blocks = meta_all.shape[0]

    halves_o = pack_halves(w_gate_up[0], w_down[0])
    halves_x, halves_y = swap(halves_o, "xl"), swap(halves_o, "yl")
    half_da, half_db = swap(halves_x[0], "yl"), swap(halves_y[1], "xl")

    grad_low_all = tokens_gather(out_grad.astype(BF16), sizes)

    length = seq_rows.shape[0]
    local_heads = query_width // HEAD
    local_groups = kv_width // HEAD
    group_size = local_heads // local_groups
    proj = jnp.dot(seq_rows, w_in, preferred_element_type=F32)
    query_proj = proj[:, :query_width]
    key_proj = proj[:, query_width : query_width + kv_width]
    value_low = proj[:, query_width + kv_width :].astype(BF16)
    value_low = value_low.reshape(length, local_groups, HEAD)
    cosine_table, sine_table = rotary_tables(length, HEAD)
    query_rot = rotate(
        query_proj.reshape(length, local_heads, HEAD), cosine_table, sine_table, 1.0
    ).astype(BF16)
    key_rot = rotate(
        key_proj.reshape(length, local_groups, HEAD), cosine_table, sine_table, 1.0
    ).astype(BF16)
    query_grouped = query_rot.reshape(length, local_groups, group_size, HEAD)
    attended, log_total = attend(query_grouped, key_rot, value_low)
    attended = attended.reshape(zs, tok_rows, query_width).astype(BF16)
    attended_own = lax.all_to_all(attended, "z", split_axis=0, concat_axis=0, tiled=True)
    branch = sum(dot(attended_own[i], w_out[i], ((1,), (1,))) for i in range(zs))
    middle = hidden_in + RESIDUAL_SCALE * branch
    normed_two, inverse_two, scaled_two = norm_rows(middle, norm2_gain)
    normed_two_low = normed_two.astype(BF16)

    mask_all, scale_all = chosen_tables(
        meta_all[:, :pick_count], meta_all[:, pick_count:], expert_count
    )
    side = 2 * high
    numbers = []
    for dy, dx in ((0, 0), (0, 1), (1, 0), (1, 1)):
        chip = (yh * 2 + (yl ^ dy)) * side + xh * 2 + (xl ^ dx)
        numbers.append((chip * 2 + core) * zs + z)
    mine = jnp.stack(numbers)[:, None] == jnp.arange(expert_count)[None, :]
    mask_mine = jnp.any(mine[None, :, :, None] & mask_all[:, None], axis=2)
    earlier = (
        jnp.arange(tok_rows)[:, None] < jnp.arange(tok_rows)[None, :]
    ).astype(BF16)
    rank = jnp.einsum(
        "bes,st->bet", mask_mine.astype(BF16), earlier, preferred_element_type=F32
    )
    place = jnp.where(mask_mine, rank, -1.0)
    place_of_token = jnp.where(
        mask_mine, rank + (jnp.arange(4, dtype=F32) * slots)[None, :, None], -1.0
    ).transpose(0, 2, 1)
    grad_slots = dispatch(place, grad_low_all, slots)

    rows_all = tokens_gather(normed_two_low, sizes)
    logits_all = jnp.einsum("de,btd->bet", w_router, rows_all, preferred_element_type=F32)
    gates_all = masked_softmax(logits_all, mask_all, 1) * scale_all
    gates_mine = jnp.sum(jnp.where(mine[None, :, :, None], gates_all[:, None], 0.0), axis=2)
    hits = place[:, :, None, :] == jnp.arange(slots, dtype=F32)[None, None, :, None]
    slot_gates = jnp.sum(jnp.where(hits, gates_mine[:, :, None, :], 0.0), axis=-1)
    slot_gates = slot_gates.transpose(1, 0, 2).reshape(4, blocks * slots, 1)
    row_slots = dispatch(place, rows_all, slots).reshape(4, blocks * slots, model_width)
    grad_slots = grad_slots.reshape(4, blocks * slots, model_width)

    out_d = expert(3, row_slots, grad_slots, slot_gates, half_da, half_db)
    from_y_a, from_x_b = swap(out_d[3], "yl"), swap(out_d[4], "xl")
    out_o = expert(0, row_slots, grad_slots, slot_gates, halves_o, halves_o)
    out_x = expert(1, row_slots, grad_slots, slot_gates, halves_x, halves_x)
    out_y = expert(2, row_slots, grad_slots, slot_gates, halves_y, halves_y)
    outs = (out_o, out_x, out_y, out_d)
    grad_rows_part = combine(place_of_token, [o[1] for o in outs], slots)
    output_part = combine(place_of_token, [o[0] for o in outs], slots)
    expert_x = (swap(out_x[3] + from_y_a, "xl"), swap(out_x[4], "xl"))
    expert_y = (swap(out_y[3], "yl"), swap(out_y[4] + from_x_b, "yl"))
    grad_packed = jnp.stack(
        [
            out_o[3 + i].astype(F32) + expert_x[i].astype(F32) + expert_y[i].astype(F32)
            for i in range(2)
        ]
    )
    grad_w_gate_up, grad_w_down = unpack_halves(grad_packed, model_width)
    grad_w_gate_up, grad_w_down = grad_w_gate_up[None], grad_w_down[None]

    slot_grads = jnp.stack([o[2].reshape(blocks, slots) for o in outs], axis=1)
    token_grads = jnp.sum(jnp.where(hits, slot_grads[:, :, :, None], 0.0), axis=2)
    token_grads = jnp.where(xl == 1, token_grads[:, jnp.array([1, 0, 3, 2])], token_grads)
    token_grads = jnp.where(yl == 1, token_grads[:, jnp.array([2, 3, 0, 1])], token_grads)
    token_grads = token_grads.reshape(high * high, 2, zs, 4, tok_rows)
    token_grads = jnp.where(core == 1, token_grads[:, ::-1], token_grads)
    token_grads = token_grads.reshape(blocks, 4, tok_rows)
    gate_grads = lax.all_to_all(
        token_grads, ("yh", "xh", "core", "z"), split_axis=0, concat_axis=0, tiled=True
    )
    gate_grads = gate_grads.reshape(high, high, 2, zs, 2, 2, tok_rows)
    gate_grads = gate_grads.transpose(0, 4, 1, 5, 2, 3, 6).reshape(expert_count, tok_rows)

    mask_own, scale_own = chosen_tables(meta[:pick_count], meta[pick_count:], expert_count)
    logits_own = dot(w_router, normed_two_low, ((0,), (1,)))
    prob_own = masked_softmax(logits_own, mask_own, 0)
    grad_scaled = gate_grads * scale_own
    grad_chosen = prob_own * (
        grad_scaled - jnp.sum(prob_own * grad_scaled, axis=0, keepdims=True)
    )
    grad_logits = grad_chosen.astype(BF16)
    grad_router_part = dot(grad_logits, normed_two_low, ((1,), (0,)))
    grad_normed_moe = tokens_scatter(grad_rows_part, sizes)
    grad_normed_two = grad_normed_moe + dot(grad_logits, w_router, ((0,), (1,)))
    grad_middle = out_grad + norm_back(grad_normed_two, scaled_two, inverse_two, norm2_gain)
    grad_gain_two = jnp.sum(grad_normed_two * scaled_two, axis=0)
    grad_branch = (RESIDUAL_SCALE * grad_middle).astype(BF16)

    grad_attended = jnp.stack(
        [dot(grad_branch, w_out[i], ((1,), (0,))).astype(BF16) for i in range(zs)]
    )
    grad_attended = lax.all_to_all(grad_attended, "z", split_axis=0, concat_axis=0, tiled=True)
    grad_attended = grad_attended.reshape(length, local_groups, group_size, HEAD)
    grad_query_rot, grad_key_rot, grad_value = attend_back(
        query_grouped, key_rot, value_low, log_total, grad_attended
    )
    grad_query_rot = grad_query_rot.reshape(length, local_heads, HEAD)
    grad_query = rotate(grad_query_rot, cosine_table, sine_table, -1.0)
    grad_key = rotate(grad_key_rot, cosine_table, sine_table, -1.0)
    grad_proj = jnp.concatenate(
        [
            grad_query.reshape(length, query_width),
            grad_key.reshape(length, kv_width),
            grad_value.reshape(length, kv_width),
        ],
        axis=1,
    ).astype(BF16)
    grad_normed_part = dot(grad_proj, w_in, ((1,), (1,))).astype(BF16)
    grad_normed_one = line_scatter(grad_normed_part.reshape(zs, tok_rows, model_width), zs)
    grad_w_in = dot(seq_rows, grad_proj, ((0,), (0,)))
    grad_gain_one = jnp.sum(w_in.astype(F32) * grad_w_in, axis=1) / norm1_gain
    dp_count = 8 * high * high
    shard_in = rows_scatter(grad_w_in.astype(BF16).reshape(dp_count, -1, packed.shape[1]), high)
    shard_query = shard_in[:, :query_width]
    shard_keyvalue = jnp.stack(
        [
            shard_in[:, query_width : query_width + kv_width],
            shard_in[:, query_width + kv_width :],
        ]
    )

    attended_rows = attended_own.transpose(1, 0, 2).reshape(tok_rows, zs * query_width)
    grad_w_out = dot(grad_branch, attended_rows, ((0,), (0,))).astype(BF16)
    shard_out = lax.psum_scatter(grad_w_out, ROWS, scatter_dimension=0, tiled=True)
    shard_out = shard_out.reshape(-1, zs, query_width).transpose(1, 0, 2)
    shard_output = line_scatter(shard_out, zs).T

    normed_back = norm_back(grad_normed_one, scaled_one, inverse_one, norm1_gain)
    grad_hidden = grad_middle + normed_back
    output = middle + RESIDUAL_SCALE * tokens_scatter(output_part, sizes)
    early = total(jnp.concatenate([grad_router_part, grad_gain_two[None]], axis=0), sizes)
    total_gain_one = total(grad_gain_one.reshape(-1, 128), sizes).reshape(-1)
    return (
        output,
        grad_hidden,
        total_gain_one,
        shard_query,
        shard_keyvalue,
        shard_output,
        early[expert_count],
        early[:expert_count].T,
        grad_w_gate_up,
        grad_w_down,
    )


def solution(mesh):
    high = math.isqrt(mesh.shape["dp"] // 2) // 2
    zs = mesh.shape["tensor"]
    inner = Mesh(mesh.devices.reshape(high, 2, high, 2, 2, zs), ALL)
    sizes = dict(inner.shape)
    in_specs = (
        P(ALL, None),
        P(),
        P(ROWS, "z"),
        P(None, ROWS, "z"),
        P("z", ROWS),
        P(),
        P(),
        P(ALL, None, None, None),
        P(ALL, None, None),
        P(ALL, None),
        P(ALL, None),
        P(ALL, None),
    )
    out_specs = (
        P(ALL, None),
        P(ALL, None),
        P(),
        P(ROWS, "z"),
        P(None, ROWS, "z"),
        P("z", ROWS),
        P(),
        P(),
        P(ALL, None, None, None),
        P(ALL, None, None),
    )
    return jax.shard_map(
        functools.partial(local, sizes),
        mesh=inner,
        in_specs=in_specs,
        out_specs=out_specs,
        check_vma=False,
    )
```

```python
import functools
import math

import jax
import jax.numpy as jnp
from jax import lax
from jax.experimental import pallas as pl
from jax.experimental.pallas import tpu as pltpu
from jax.sharding import Mesh
from jax.sharding import PartitionSpec as P

HEAD = 64
EPSILON = 1e-06
ATTN_SCALE = 0.015625
RESIDUAL_SCALE = 0.22
THETA = 10000.0
QUERY_BLOCK = 256
F32 = jnp.float32
BF16 = jnp.bfloat16
SWAP = [(0, 1), (1, 0)]
VMEM_LIMIT = 56 * 1024 * 1024
SMALL = pl.CostEstimate(flops=1, bytes_accessed=1, transcendentals=0)
LARGE = pl.CostEstimate(flops=10**11, bytes_accessed=10**8, transcendentals=0)

ROWS = ("yh", "yl", "xh", "xl", "core")
ALL = ROWS + ("z",)


def swap(value, axis):
    return lax.ppermute(value, axis, SWAP)


def dot(a, b, dims):
    return lax.dot_general(a, b, (dims, ((), ())), preferred_element_type=F32)


def rotary_tables(length):
    half_width = HEAD // 2
    frequency = THETA ** (-2.0 * jnp.arange(half_width, dtype=F32) / HEAD)
    angles = jnp.arange(length, dtype=F32)[:, None] * frequency[None, :]
    cosine, sine = jnp.cos(angles), jnp.sin(angles)
    return jnp.tile(cosine, (1, 4)), jnp.tile(jnp.concatenate([-sine, sine], axis=1), (1, 2))


def norm_rows(values, gain):
    inverse = lax.rsqrt(jnp.mean(values * values, axis=-1, keepdims=True) + EPSILON)
    scaled = values * inverse
    return (scaled * gain, inverse, scaled)


def norm_back(grad_normed, scaled, inverse, gain):
    grad_scaled = grad_normed * gain
    return inverse * (
        grad_scaled - scaled * jnp.mean(grad_scaled * scaled, axis=-1, keepdims=True)
    )


def line_step(value, size):
    return lax.ppermute(value, "z", [(i, (i + 1) % size) for i in range(size)])


def line_pieces(value, size):
    pieces = [value]
    for _ in range(size - 1):
        pieces.append(line_step(pieces[-1], size))
    return pieces


def line_order(pieces):
    size = len(pieces)
    z = lax.axis_index("z")
    whole = jnp.zeros((size,) + pieces[0].shape, pieces[0].dtype)
    for step, piece in enumerate(pieces):
        whole = lax.dynamic_update_index_in_dim(whole, piece, lax.rem(z + size - step, size), 0)
    return whole


def line_sum(terms):
    size = len(terms)
    running = None
    for step in range(1, size):
        running = line_step(terms[step] if running is None else terms[step] + running, size)
    own = terms[0].astype(F32)
    return own if running is None else own + running.astype(F32)


def tie(*values):
    return lax.optimization_barrier(values)


def behind(value, size):
    z = lax.axis_index("z")
    return [
        lax.dynamic_index_in_dim(value, lax.rem(z + size - j, size), 0, False) for j in range(size)
    ]


def spread(pieces, sizes):
    if sizes["yh"] == 1:
        return [piece[None] for piece in pieces]
    return [lax.all_gather(piece, ("yh", "xh"), axis=0, tiled=False) for piece in pieces]


def exchange(value, axes):
    return lax.all_to_all(value, axes, split_axis=0, concat_axis=0, tiled=True)


def share(value, axes, count):
    return exchange(jnp.broadcast_to(value[None], (count,) + value.shape), axes)


def one_hot(place_row, slots):
    rank = lax.broadcasted_iota(jnp.int32, (slots, place_row.shape[1]), 0).astype(F32)
    return jnp.where(rank == place_row, 1.0, 0.0)


def load_weights(sources, buffer, sem):
    number, inner = pl.program_id(0), pl.program_id(1)

    def copies(k):
        for half, ref in enumerate(sources[k]):
            yield pltpu.make_async_copy(ref, buffer.at[k % 2, half], sem.at[k % 2, half])

    for k in range(len(sources)):
        if k == 0:

            @pl.when((number == 0) & (inner == 0))
            def _():
                for copy in copies(0):
                    copy.start()

        @pl.when((number == k) & (inner == 0))
        def _(k=k):
            for copy in copies(k):
                copy.wait()
            if k + 1 < len(sources):
                for copy in copies(k + 1):
                    copy.start()


def halves_of(refs):
    pairs, refs = [], list(refs)
    while refs:
        ref = refs.pop(0)
        pairs.append((ref.at[0], ref.at[1]) if len(ref.shape) == 3 else (ref, refs.pop(0)))
    return pairs


def forward_kernel(pieces, slots, *refs):
    x_refs = refs[:pieces]
    place_ref, mask_ref, scale_ref, mine_ref, router_ref = refs[pieces : pieces + 5]
    weights = halves_of(refs[pieces + 5 : -8])
    y_ref, xs_ref, dg_ref, du_ref, act_ref, gate_ref, buffer, sem = refs[-8:]
    number, group = pl.program_id(0), pl.program_id(1)
    load_weights(weights, buffer, sem)
    width = x_refs[0].shape[-1]
    hidden = buffer.shape[-1]
    half = hidden // 2

    @pl.when(number == 0)
    def _():
        for j in range(pieces):
            mask = mask_ref[group, j]
            logits = dot(router_ref[...], x_refs[j][0], ((1,), (1,)))
            logits = jnp.where(mask > 0.0, logits, -1e30)
            top = jnp.max(logits, axis=0, keepdims=True)
            exponent = jnp.where(mask > 0.0, jnp.exp(logits - top), 0.0)
            gates = exponent / jnp.sum(exponent, axis=0, keepdims=True) * scale_ref[group, j]
            for e in range(gate_ref.shape[2]):
                gate_ref[group, j, e : e + 1] = jnp.sum(
                    gates * mine_ref[:, e : e + 1], axis=0, keepdims=True
                )

    slot_gates = []
    for j in range(pieces):
        pick = one_hot(place_ref[group, j, pl.ds(number, 1), :], slots)
        rows = dot(pick.astype(BF16), x_refs[j][0], ((1,), (0,)))
        xs_ref[0, j * slots : (j + 1) * slots] = rows.astype(BF16)
        slot_gates.append(
            jnp.sum(pick * gate_ref[group, j, pl.ds(number, 1), :], axis=1, keepdims=True)
        )
    slot_gate = jnp.concatenate(slot_gates, axis=0)
    now = lax.rem(number, 2)
    x = xs_ref[0]
    gate = dot(x, buffer[now, 0, :width], ((1,), (0,)))
    up = dot(x, buffer[now, 1, :width], ((1,), (0,)))
    sigmoid = 1.0 / (1.0 + jnp.exp(-gate))
    silu = gate * sigmoid
    active = (silu * up).astype(BF16)
    act_ref[0] = active
    dg_ref[0] = (up * sigmoid * (1.0 + gate * (1.0 - sigmoid))).astype(BF16)
    du_ref[0] = silu.astype(BF16)
    weighted = (active.astype(F32) * slot_gate).astype(BF16)
    for cut in range(width // hidden):
        place = slice(width + cut * half, width + (cut + 1) * half)
        out = dot(weighted[:, :half], buffer[now, 0, place], ((1,), (0,)))
        out = out + dot(weighted[:, half:], buffer[now, 1, place], ((1,), (0,)))
        y_ref[0, :, cut * hidden : (cut + 1) * hidden] = out.astype(BF16)


def backward_kernel(pieces, slots, first, given, *refs):
    g_refs = refs[:pieces]
    place_ref, gate_ref, xs_ref, dg_ref, du_ref, act_ref = refs[pieces : pieces + 6]
    weights, refs = refs[pieces + 6 : pieces + 6 + given], refs[pieces + 6 + given :]
    weights = halves_of(weights)
    experts = len(weights)
    rows_ref, through_ref = refs[:2]
    results = [refs[2 + 4 * k : 6 + 4 * k] for k in range(experts)]
    buffer, sem, gs_ref, stage, out_sem = refs[2 + 4 * experts : 7 + 4 * experts]
    sums = refs[7 + 4 * experts :]
    step, group = pl.program_id(0), pl.program_id(1)
    number = first - 2 * step
    load_weights(weights, buffer, sem)
    width = g_refs[0].shape[-1]
    hidden = buffer.shape[-1]
    half = hidden // 2
    now = lax.rem(step, 2)
    last = pl.num_programs(1) - 1

    def stores(k):
        piece = stage.shape[1] // 2
        return [
            pltpu.make_async_copy(
                stage.at[n // 2, pl.ds(n % 2 * piece, piece)], results[k][n], out_sem.at[n]
            )
            for n in range(4)
        ]

    slot_gates = []
    for j in range(pieces):
        pick = one_hot(place_ref[group, j, pl.ds(number, 1), :], slots)
        rows = dot(pick.astype(BF16), g_refs[j][0], ((1,), (0,)))
        gs_ref[j * slots : (j + 1) * slots] = rows.astype(BF16)
        slot_gates.append(
            jnp.sum(pick * gate_ref[group, j, pl.ds(number, 1), :], axis=1, keepdims=True)
        )
    slot_gate = jnp.concatenate(slot_gates, axis=0) * RESIDUAL_SCALE
    grad_a = grad_b = 0.0
    for cut in range(width // hidden):
        place = slice(width + cut * half, width + (cut + 1) * half)
        grad = gs_ref[:, cut * hidden : (cut + 1) * hidden]
        grad_a = grad_a + dot(grad, buffer[now, 0, place], ((1,), (1,)))
        grad_b = grad_b + dot(grad, buffer[now, 1, place], ((1,), (1,)))
    grad_active = jnp.concatenate([grad_a, grad_b], axis=1)
    active = act_ref[0].astype(F32)
    through = jnp.sum(grad_active * active, axis=1, keepdims=True) * RESIDUAL_SCALE
    for j in range(pieces):
        pick = one_hot(place_ref[group, j, pl.ds(number, 1), :], slots)
        through_ref[0, 0, j : j + 1] = jnp.sum(
            pick * through[j * slots : (j + 1) * slots], axis=0, keepdims=True
        )
    grad_active = grad_active * slot_gate
    grad_gate = (grad_active * dg_ref[0].astype(F32)).astype(BF16)
    grad_up = (grad_active * du_ref[0].astype(F32)).astype(BF16)
    rows = dot(grad_gate, buffer[now, 0, :width], ((1,), (1,)))
    rows = rows + dot(grad_up, buffer[now, 1, :width], ((1,), (1,)))
    rows_ref[0] = rows.astype(BF16)
    weighted = (active * slot_gate).astype(BF16)

    for k in range(1, experts):

        @pl.when((step == k) & (group == last))
        def _(k=k):
            for copy in stores(k - 1):
                copy.wait()

    def add(which, start, left, right):
        part = dot(left, right, ((0,), (0,)))
        place = slice(start, start + part.shape[0])
        if not sums:
            stage[which, place] = part.astype(BF16)
            return

        @pl.when(group == 0)
        def _():
            sums[0][which, place] = part

        @pl.when(group > 0)
        def _():
            sums[0][which, place] += part

        @pl.when(group == last)
        def _():
            stage[which, place] = sums[0][which, place].astype(BF16)

    x = xs_ref[0]
    add(0, 0, x, grad_gate)
    add(1, 0, x, grad_up)
    for cut in range(width // hidden):
        grad = gs_ref[:, cut * hidden : (cut + 1) * hidden]
        add(0, width + cut * half, weighted[:, :half], grad)
        add(1, width + cut * half, weighted[:, half:], grad)
    for k in range(experts):

        @pl.when((step == k) & (group == last))
        def _(k=k):
            for copy in stores(k):
                copy.start()
            if k == experts - 1:
                for copy in stores(k):
                    copy.wait()


def experts_forward(x_pieces, place, mask, scale, mine, router, weights, slots):
    pieces = len(x_pieces)
    groups, tokens, width = x_pieces[0].shape
    experts = place.shape[2]
    packed, hidden = weights[0].shape[-2:]
    rows = pieces * slots
    once = pl.Buffered(1)
    fixed = [
        pl.BlockSpec(a.shape, lambda e, c, n=a.ndim: (0,) * n, pipeline_mode=once)
        for a in (place, mask, scale, mine, router)
    ]
    piece = pl.BlockSpec(
        (1, tokens, width), lambda e, c: (c, 0, 0), pipeline_mode=once if groups == 1 else None
    )

    def by_slot(n):
        return pl.BlockSpec((1, rows, n), lambda e, c: (e, c, 0))

    def shape(n):
        return jax.ShapeDtypeStruct((experts, groups * rows, n), BF16)

    gate_shape = (groups, pieces, experts, tokens)
    return pl.pallas_call(
        functools.partial(forward_kernel, pieces, slots),
        grid=(experts, groups),
        in_specs=[piece] * pieces + fixed + [pl.BlockSpec(memory_space=pl.ANY)] * len(weights),
        out_specs=[by_slot(width), by_slot(width)]
        + [by_slot(hidden)] * 3
        + [pl.BlockSpec(gate_shape, lambda e, c: (0, 0, 0, 0))],
        out_shape=[shape(width), shape(width)]
        + [shape(hidden)] * 3
        + [jax.ShapeDtypeStruct(gate_shape, F32)],
        scratch_shapes=[
            pltpu.VMEM((2, 2, packed, hidden), BF16),
            pltpu.SemaphoreType.DMA((2, 2)),
        ],
        compiler_params=pltpu.CompilerParams(vmem_limit_bytes=VMEM_LIMIT),
        cost_estimate=LARGE,
        name="experts_forward",
    )(*x_pieces, place, mask, scale, mine, router, *weights)


def experts_backward(first, g_pieces, place, gates, saved, weights, slots):
    pieces = len(g_pieces)
    groups, tokens, width = g_pieces[0].shape
    experts = sum(2 if w.ndim == 3 else 1 for w in weights) // 2
    packed, hidden = weights[0].shape[-2:]
    rows = pieces * slots
    once = pl.Buffered(1)
    fixed = [
        pl.BlockSpec(a.shape, lambda e, c, n=a.ndim: (0,) * n, pipeline_mode=once)
        for a in (place, gates)
    ]
    piece = pl.BlockSpec(
        (1, tokens, width), lambda e, c: (c, 0, 0), pipeline_mode=once if groups == 1 else None
    )

    def by_slot(n):
        return pl.BlockSpec((1, rows, n), lambda e, c: (first - 2 * e, c, 0))

    anywhere = pl.BlockSpec(memory_space=pl.ANY)
    return pl.pallas_call(
        functools.partial(backward_kernel, pieces, slots, first, len(weights)),
        grid=(experts, groups),
        in_specs=[piece] * pieces
        + fixed
        + [by_slot(width)]
        + [by_slot(hidden)] * 3
        + [anywhere] * len(weights),
        out_specs=[
            pl.BlockSpec((1, rows, width), lambda e, c: (e, c, 0)),
            pl.BlockSpec((1, 1, pieces, tokens), lambda e, c: (e, c, 0, 0)),
        ]
        + [anywhere] * (4 * experts),
        out_shape=[
            jax.ShapeDtypeStruct((experts, groups * rows, width), BF16),
            jax.ShapeDtypeStruct((experts, groups, pieces, tokens), F32),
        ]
        + [jax.ShapeDtypeStruct((packed // 2, hidden), BF16)] * (4 * experts),
        scratch_shapes=[
            pltpu.VMEM((2, 2, packed, hidden), BF16),
            pltpu.SemaphoreType.DMA((2, 2)),
            pltpu.VMEM((rows, width), BF16),
            pltpu.VMEM((2, packed, hidden), BF16),
            pltpu.SemaphoreType.DMA((4,)),
        ]
        + ([pltpu.VMEM((2, packed, hidden), F32)] if groups > 1 else []),
        compiler_params=pltpu.CompilerParams(vmem_limit_bytes=VMEM_LIMIT),
        cost_estimate=LARGE,
        name="experts_backward",
    )(*g_pieces, place, gates, *saved, *weights)


def extra_rows(expert_count, tokens, width):
    return 16 * -(-(-(-2 * expert_count // 16)) // (width // tokens))


def extra_places(expert_count, tokens, width):
    across = width // tokens
    for block in range(-(-2 * expert_count // 16)):
        yield block, 16 * (block // across), tokens * (block % across)


def combine_kernel(order, slots, extra, place_ref, *refs):
    parts = 1 + max(which for which, _ in order)
    experts = len(order)
    rows_refs, refs = refs[:parts], refs[parts:]
    if extra:
        through_refs, mine_ref, refs = refs[:parts], refs[parts], refs[parts + 1 :]
    pieces = len(refs) - 1
    step = pl.program_id(0)
    tokens = place_ref.shape[1]
    lane = lax.broadcasted_iota(jnp.int32, (tokens, experts * slots), 1).astype(F32)
    hit = lane == place_ref[0, :, 0:1]
    for e in range(1, experts):
        hit = hit | (lane == place_ref[0, :, e : e + 1])
    pick = jnp.where(hit, 1.0, 0.0).astype(BF16)
    rows = jnp.concatenate([rows_refs[which][k] for which, k in order], axis=0)
    out = dot(pick, rows, ((1,), (0,)))
    width = out.shape[1]
    more = None
    if extra:
        dense = 0.0
        for e, (which, k) in enumerate(order):
            dense = dense + mine_ref[:, e : e + 1] * through_refs[which][k, 0]
        high = dense.astype(BF16).astype(F32)
        both = jnp.concatenate([high, dense - high], axis=0)
        across = width // tokens
        lines = []
        for start in range(0, both.shape[0], 16 * across):
            line = [both[i : i + 16] for i in range(start, min(start + 16 * across, both.shape[0]), 16)]
            line += [jnp.zeros((16, tokens), F32)] * (across - len(line))
            lines.append(jnp.concatenate(line, axis=1))
        more = jnp.concatenate(lines, axis=0)

    def store(ref):
        if not pieces:
            ref[0, :tokens] = out.astype(BF16)
            if extra:
                ref[0, tokens:] = more.astype(BF16)
            return
        ref[0, :tokens] = (out + refs[0][0, :tokens].astype(F32)).astype(BF16)
        if extra:
            ref[0, tokens:] = (more + refs[0][0, tokens:].astype(F32)).astype(BF16)

    if not pieces:
        store(refs[0])
        return
    for j in range(pieces):

        @pl.when(lax.rem(step, pieces) == j)
        def _(j=j):
            store(refs[1 + j])


def combine(place, parts, order, slots, half, other=None, through=None, mine=None):
    groups, pieces, tokens, experts = place.shape
    column = pieces // 2
    width = parts[0].shape[-1]
    extra = 0 if through is None else extra_rows(mine.shape[0], tokens, width)

    def at(i):
        return (i // column) * pieces + half * column + i % column

    in_specs = [pl.BlockSpec((1, tokens, experts), lambda i: (at(i), 0, 0))]
    in_specs += [pl.BlockSpec((p.shape[0], slots, width), lambda i: (0, at(i), 0)) for p in parts]
    operands = [place.reshape(groups * pieces, tokens, experts), *parts]
    if extra:
        in_specs += [
            pl.BlockSpec((t.shape[0], 1, 1, tokens), lambda i: (0, at(i), 0, 0)) for t in through
        ]
        in_specs.append(pl.BlockSpec(mine.shape, lambda i: (0, 0)))
        operands += [t.reshape(t.shape[0], groups * pieces, 1, tokens) for t in through] + [mine]
    rows = tokens + extra
    by_step = pl.BlockSpec((1, rows, width), lambda i: (i, 0, 0))
    if other is None:
        out_specs, out_shape = by_step, jax.ShapeDtypeStruct((groups * column, rows, width), BF16)
    else:
        in_specs.append(by_step)
        operands.append(other)
        out_specs = [pl.BlockSpec((1, rows, width), lambda i: (i // column, 0, 0))] * column
        out_shape = [jax.ShapeDtypeStruct((groups, rows, width), BF16)] * column
    return pl.pallas_call(
        functools.partial(combine_kernel, order, slots, extra),
        grid=(groups * column,),
        in_specs=in_specs,
        out_specs=out_specs,
        out_shape=out_shape,
        compiler_params=pltpu.CompilerParams(vmem_limit_bytes=VMEM_LIMIT),
        cost_estimate=SMALL,
        name="combine",
    )(*operands)


def gates_of_extra(rows, expert_count, tokens):
    width = rows.shape[1]
    blocks = [
        rows[row : row + 16, column : column + tokens]
        for _, row, column in extra_places(expert_count, tokens, width)
    ]
    both = jnp.concatenate(blocks, axis=0)
    return both[:expert_count] + both[expert_count : 2 * expert_count]


def to_owners(place, parts, order, slots, sizes, through=None, mine=None):
    other = swap(combine(place, parts, order, slots, 1, None, through, mine), "core")
    terms = combine(place, parts, order, slots, 0, other, through, mine)
    if sizes["yh"] == 1:
        return [term[0] for term in terms]
    return [
        lax.psum_scatter(term, ("yh", "xh"), scatter_dimension=0, tiled=True)[0] for term in terms
    ]


def pack_kernel(gate_up_ref, down_ref, out_ref):
    step = pl.program_id(1)
    half, hidden = down_ref.shape[1], out_ref.shape[2]

    @pl.when(step < 2)
    def _():
        out_ref[0] = gate_up_ref[0, 0]

    @pl.when(step == 2)
    def _():
        for cut in range(down_ref.shape[2] // hidden):
            columns = slice(cut * hidden, (cut + 1) * hidden)
            out_ref[0, cut * half : (cut + 1) * half] = down_ref[0, :, columns]


def packed_specs(width, hidden):
    block = width // 2
    return (
        pl.BlockSpec((1, 1, block, hidden), lambda h, i: (0, h, jnp.minimum(i, 1), 0)),
        pl.BlockSpec((1, hidden // 2, width), lambda h, i: (0, h, 0)),
    )


def pack(gate_up, down):
    _, _, width, hidden = gate_up.shape
    gate_up_spec, down_spec = packed_specs(width, hidden)
    return pl.pallas_call(
        pack_kernel,
        grid=(2, 3),
        in_specs=[gate_up_spec, down_spec],
        out_specs=pl.BlockSpec((1, width // 2, hidden), lambda h, i: (h, i, 0)),
        out_shape=jax.ShapeDtypeStruct((2, 3 * width // 2, hidden), BF16),
        compiler_params=pltpu.CompilerParams(vmem_limit_bytes=VMEM_LIMIT),
        cost_estimate=SMALL,
        name="pack",
    )(gate_up, down)


def unpack_kernel(*refs):
    gate_up_ref, down_ref = refs[-2:]
    which, step = pl.program_id(0), pl.program_id(1)
    half, hidden = down_ref.shape[1], gate_up_ref.shape[3]
    piece = refs[0].shape[0]
    block = gate_up_ref.shape[2]

    def value(terms, start, count):
        return sum(ref[start : start + count].astype(F32) for ref in terms)

    def rows(first, second, start, count):
        parts = []
        if start < piece:
            parts.append(value(first, start, min(count, piece - start)))
        if start + count > piece:
            low = max(start, piece)
            parts.append(value(second, low - piece, start + count - low))
        return jnp.concatenate(parts, axis=0) if len(parts) > 1 else parts[0]

    for k in (0, 1):
        first, second = refs[6 * k : 6 * k + 3], refs[6 * k + 3 : 6 * k + 6]
        for i in (0, 1):

            @pl.when((which == k) & (step == i))
            def _(first=first, second=second, i=i):
                gate_up_ref[0, 0] = rows(first, second, i * block, block)

        @pl.when((which == k) & (step == 2))
        def _(first=first, second=second):
            for cut in range(down_ref.shape[2] // hidden):
                columns = slice(cut * hidden, (cut + 1) * hidden)
                down_ref[0, :, columns] = rows(first, second, 2 * block + cut * half, half)


def unpack(terms, width):
    piece, hidden = terms[0][0][0].shape
    gate_up_spec, down_spec = packed_specs(width, hidden)
    whole = pl.BlockSpec((piece, hidden), lambda h, i: (0, 0), pipeline_mode=pl.Buffered(1))
    return pl.pallas_call(
        unpack_kernel,
        grid=(2, 3),
        in_specs=[whole] * 12,
        out_specs=[gate_up_spec, down_spec],
        out_shape=[
            jax.ShapeDtypeStruct((1, 2, width, hidden), F32),
            jax.ShapeDtypeStruct((1, hidden, width), F32),
        ],
        compiler_params=pltpu.CompilerParams(vmem_limit_bytes=VMEM_LIMIT),
        cost_estimate=SMALL,
        name="unpack",
    )(*[array for half in terms for part in half for array in part])


def causal_mask(scores, start):
    keys, columns = scores.shape
    block = keys - start
    key = lax.broadcasted_iota(jnp.int32, (block, columns), 0)
    query = lax.rem(lax.broadcasted_iota(jnp.int32, (block, columns), 1), block)
    low = jnp.where(key <= query, scores[start:], -1e30)
    return low if start == 0 else jnp.concatenate([scores[:start], low], axis=0)


def head_rows(pair, odd):
    lane = lax.broadcasted_iota(jnp.int32, pair.shape, 1)
    return jnp.where((lane >= HEAD) == odd, pair, jnp.zeros_like(pair))


def both_halves(rows):
    return jnp.concatenate([rows, rows], axis=1)


def attend_kernel(heads, groups, block, qkv_ref, out_ref, lse_ref):
    length = qkv_ref.shape[0]
    each = heads // groups
    at_key = heads * HEAD
    at_value = at_key + groups * HEAD
    for i in range(length // block):
        start, stop = i * block, (i + 1) * block
        parts = []
        for g in range(groups):
            key = both_halves(qkv_ref[:stop, at_key + g * HEAD : at_key + (g + 1) * HEAD])
            value = qkv_ref[:stop, at_value + g * HEAD : at_value + (g + 1) * HEAD]
            query = []
            for h in range(g * each, (g + 1) * each):
                pair = qkv_ref[start:stop, h // 2 * 2 * HEAD : (h // 2 + 1) * 2 * HEAD]
                query.append(head_rows(pair, h % 2 == 1) * ATTN_SCALE)
            query = jnp.concatenate(query, axis=0).astype(BF16)
            scores = causal_mask(dot(key, query, ((1,), (1,))), start)
            top = jnp.max(scores, axis=0, keepdims=True)
            exponent = jnp.exp(scores - top)
            norm = jnp.sum(exponent, axis=0, keepdims=True)
            total = top + jnp.log(norm)
            out = dot(value, exponent.astype(BF16), ((0,), (0,))) / norm
            for k in range(each):
                columns = slice(k * block, (k + 1) * block)
                lse_ref[g * each + k : g * each + k + 1, start:stop] = total[:, columns]
                parts.append(out[:, columns])
        for pair in range(heads // 2):
            rows = jnp.concatenate(parts[2 * pair : 2 * pair + 2], axis=0)
            out_ref[start:stop, pair * 2 * HEAD : (pair + 1) * 2 * HEAD] = rows.T.astype(BF16)


def attend(qkv, heads, groups):
    length = qkv.shape[0]
    return pl.pallas_call(
        functools.partial(attend_kernel, heads, groups, min(QUERY_BLOCK, length)),
        out_shape=[
            jax.ShapeDtypeStruct((length, heads * HEAD), BF16),
            jax.ShapeDtypeStruct((8 * -(-heads // 8), length), F32),
        ],
        compiler_params=pltpu.CompilerParams(vmem_limit_bytes=VMEM_LIMIT),
        cost_estimate=LARGE,
        name="attend",
    )(qkv)


def turn(values, cosine, sine, direction):
    width = values.shape[1]
    lane = lax.broadcasted_iota(jnp.int32, values.shape, 1)
    first = lax.rem(lane, HEAD) < HEAD // 2
    behind_half = pltpu.roll(values, width - HEAD // 2, 1)
    other = jnp.where(first, behind_half, pltpu.roll(values, HEAD // 2, 1))
    repeats = width // cosine.shape[1]
    cosine = jnp.concatenate([cosine] * repeats, axis=1) if repeats > 1 else cosine
    sine = jnp.concatenate([sine] * repeats, axis=1) if repeats > 1 else sine
    return values * cosine + direction * (other * sine)


def attend_back_kernel(
    heads, groups, block, qkv_ref, lse_ref, grad_ref, cos_ref, sin_ref, out_ref, key_sum, value_sum
):
    length = qkv_ref.shape[0]
    each = heads // groups
    at_key = heads * HEAD
    at_value = at_key + groups * HEAD
    for i in reversed(range(length // block)):
        start, stop = i * block, (i + 1) * block
        parts = []
        for g in range(groups):
            key = qkv_ref[:stop, at_key + g * HEAD : at_key + (g + 1) * HEAD]
            value = both_halves(qkv_ref[:stop, at_value + g * HEAD : at_value + (g + 1) * HEAD])
            query, grad, lse = [], [], []
            for h in range(g * each, (g + 1) * each):
                columns = slice(h // 2 * 2 * HEAD, (h // 2 + 1) * 2 * HEAD)
                query.append(head_rows(qkv_ref[start:stop, columns], h % 2 == 1) * ATTN_SCALE)
                grad.append(head_rows(grad_ref[start:stop, columns], h % 2 == 1))
                lse.append(lse_ref[h : h + 1, start:stop])
            query = jnp.concatenate(query, axis=0).astype(BF16)
            grad = jnp.concatenate(grad, axis=0)
            lse = jnp.concatenate(lse, axis=1)
            scores = causal_mask(dot(both_halves(key), query, ((1,), (1,))), start)
            probs = jnp.exp(scores - lse)
            grad_probs = dot(value, grad, ((1,), (1,)))
            weighted = probs * grad_probs
            delta = jnp.sum(weighted, axis=0, keepdims=True)
            grad_scores = (weighted - probs * delta).astype(BF16)
            grad_value = dot(probs.astype(BF16), grad, ((1,), (0,)))
            grad_key = dot(grad_scores, query, ((1,), (0,)))
            if stop == length:
                value_sum[g] = grad_value
                key_sum[g] = grad_key
            else:
                value_sum[g, :stop] += grad_value
                key_sum[g, :stop] += grad_key
            grad_query = dot(key, grad_scores, ((0,), (0,))) * ATTN_SCALE
            for k in range(each):
                parts.append(grad_query[:, k * block : (k + 1) * block])
        cosine, sine = cos_ref[start:stop], sin_ref[start:stop]
        for pair in range(heads // 2):
            rows = jnp.concatenate(parts[2 * pair : 2 * pair + 2], axis=0).T
            rows = turn(rows, cosine, sine, -1.0).astype(BF16)
            out_ref[start:stop, pair * 2 * HEAD : (pair + 1) * 2 * HEAD] = rows
    rows = [key_sum[g][:, :HEAD] + key_sum[g][:, HEAD:] for g in range(groups)]
    rows = turn(jnp.concatenate(rows, axis=1), cos_ref[...], sin_ref[...], -1.0)
    out_ref[:, at_key:at_value] = rows.astype(BF16)
    rows = [value_sum[g][:, :HEAD] + value_sum[g][:, HEAD:] for g in range(groups)]
    out_ref[:, at_value:] = jnp.concatenate(rows, axis=1).astype(BF16)


def attend_back(qkv, lse, grad, cosine, sine, heads, groups):
    length = qkv.shape[0]
    return pl.pallas_call(
        functools.partial(attend_back_kernel, heads, groups, min(QUERY_BLOCK, length)),
        out_shape=jax.ShapeDtypeStruct(qkv.shape, BF16),
        scratch_shapes=[pltpu.VMEM((groups, length, 2 * HEAD), F32)] * 2,
        compiler_params=pltpu.CompilerParams(vmem_limit_bytes=VMEM_LIMIT),
        cost_estimate=LARGE,
        name="attend_back",
    )(qkv, lse, grad, cosine, sine)


def project_kernel(turned, place_ref, x_ref, w_ref, cos_ref, sin_ref, *refs):
    out_ref = refs[-1]
    values = dot(x_ref[...], w_ref[...], ((1,), (0,)))
    out_ref[:, :turned] = turn(values[:, :turned], cos_ref[...], sin_ref[...], 1.0).astype(BF16)
    out_ref[:, turned:] = values[:, turned:].astype(BF16)


def project(place, rows, weights, cosine, sine, turned, before=None):
    tokens, width = rows.shape
    columns = weights.shape[1]
    in_specs = [
        pl.BlockSpec((tokens, width), lambda i, p: (0, 0)),
        pl.BlockSpec((width, columns), lambda i, p: (0, 0)),
        pl.BlockSpec((tokens, cosine.shape[1]), lambda i, p: (p[0], 0)),
        pl.BlockSpec((tokens, sine.shape[1]), lambda i, p: (p[0], 0)),
    ]
    operands = [place.reshape(1), rows, weights, cosine, sine]
    if before is not None:
        in_specs.append(pl.BlockSpec(memory_space=pl.ANY))
        operands.append(before)
    return pl.pallas_call(
        functools.partial(project_kernel, turned),
        grid_spec=pltpu.PrefetchScalarGridSpec(
            num_scalar_prefetch=1,
            grid=(1,),
            in_specs=in_specs,
            out_specs=pl.BlockSpec((tokens, columns), lambda i, p: (p[0], 0)),
        ),
        out_shape=jax.ShapeDtypeStruct((cosine.shape[0], columns), BF16),
        input_output_aliases={} if before is None else {5: 0},
        compiler_params=pltpu.CompilerParams(vmem_limit_bytes=VMEM_LIMIT),
        cost_estimate=SMALL,
        name="project",
    )(*operands)


def project_back_kernel(pieces, place_ref, *refs):
    x_refs = refs[:pieces]
    grad_ref, w_ref, out_ref, gain_ref = refs[pieces:]
    tokens = x_refs[0].shape[0]
    grad = 0.0
    for j in range(pieces):
        start = pl.multiple_of(place_ref[j] * tokens, tokens)
        grad = grad + dot(x_refs[j][...], grad_ref[pl.ds(start, tokens), :], ((0,), (0,)))
    out_ref[...] = grad.astype(BF16)
    ones = jnp.ones((8, w_ref.shape[1]), F32)
    gain_ref[...] = lax.dot_general(
        ones,
        w_ref[...].astype(F32) * grad,
        (((1,), (1,)), ((), ())),
        precision=lax.Precision.HIGHEST,
        preferred_element_type=F32,
    )


def project_back(places, pieces, grad, weights):
    tokens, width = pieces[0].shape
    columns = weights.shape[1]
    cut = width // 3
    return pl.pallas_call(
        functools.partial(project_back_kernel, len(pieces)),
        grid_spec=pltpu.PrefetchScalarGridSpec(
            num_scalar_prefetch=1,
            grid=(3,),
            in_specs=[pl.BlockSpec((tokens, cut), lambda i, p: (0, i))] * len(pieces)
            + [
                pl.BlockSpec(grad.shape, lambda i, p: (0, 0)),
                pl.BlockSpec((cut, columns), lambda i, p: (i, 0)),
            ],
            out_specs=[
                pl.BlockSpec((cut, columns), lambda i, p: (i, 0)),
                pl.BlockSpec((8, cut), lambda i, p: (0, i)),
            ],
        ),
        out_shape=[
            jax.ShapeDtypeStruct((width, columns), BF16),
            jax.ShapeDtypeStruct((8, width), F32),
        ],
        compiler_params=pltpu.CompilerParams(vmem_limit_bytes=VMEM_LIMIT),
        cost_estimate=SMALL,
        name="project_back",
    )(places, *pieces, grad, weights)


def chosen_tables(ids, scale, expert_count):
    lead = (1,) * (ids.ndim - 2)
    numbers = jnp.arange(expert_count, dtype=F32).reshape(lead + (1, expert_count, 1))
    hits = ids[..., :, None, :] == numbers
    mask = jnp.any(hits, axis=-3)
    return mask, jnp.sum(jnp.where(hits, scale[..., :, None, :], 0.0), axis=-3)


def masked_softmax(logits, mask, axis):
    top = jnp.max(jnp.where(mask, logits, -jnp.inf), axis=axis, keepdims=True)
    exponent = jnp.where(mask, jnp.exp(jnp.where(mask, logits - top, 0.0)), 0.0)
    return exponent / jnp.sum(exponent, axis=axis, keepdims=True)


def local(
    sizes,
    hidden_in,
    norm1_gain,
    w_query,
    w_keyvalue,
    w_output,
    norm2_gain,
    w_router,
    w_gate_up,
    w_down,
    expert_ids,
    choice_scale,
    out_grad,
):
    tok_rows, model_width = hidden_in.shape
    pick_count = expert_ids.shape[1]
    expert_count = w_router.shape[1]
    capacity = max(2, (tok_rows * pick_count * 11 + 8 * expert_count - 1) // (8 * expert_count))
    slots = -(-capacity // 16) * 16
    zs, high = sizes["z"], sizes["yh"]
    yl, xl, core, z = (lax.axis_index(a) for a in ("yl", "xl", "core", "z"))
    yh, xh = lax.axis_index("yh"), lax.axis_index("xh")

    packed = jnp.concatenate([w_query, w_keyvalue[0], w_keyvalue[1]], axis=1)
    dp_count = 8 * high * high
    w_in = lax.all_gather(packed, ROWS, axis=0, tiled=True)
    query_width = w_query.shape[1]
    kv_width = w_keyvalue.shape[2]
    normed_one, inverse_one, scaled_one = norm_rows(hidden_in, norm1_gain)
    normed_low = normed_one.astype(BF16)
    normed_low, w_gate_up, w_down = tie(normed_low, w_gate_up, w_down)
    seq_pieces = line_pieces(normed_low, zs)
    halves_o = pack(w_gate_up, w_down)
    halves_x, halves_y = swap(halves_o, "xl"), swap(halves_o, "yl")
    w_out = lax.all_gather(w_output.T, ALL, axis=0)
    w_out = w_out.reshape((-1, zs) + w_out.shape[1:])
    w_out = w_out.transpose(1, 0, 2, 3).reshape(zs, model_width, w_output.shape[0])
    meta = jnp.concatenate([expert_ids.astype(F32).T, choice_scale.T], axis=0)
    meta_all = share(meta, ("yh", "xh", "core", "z"), high * high * 2 * zs)
    meta_all = meta_all.reshape((high * high, 2, zs) + meta.shape)
    meta_all = jnp.where(core == 1, meta_all[:, ::-1], meta_all)
    meta_all = jnp.stack(behind(jnp.moveaxis(meta_all, 2, 0), zs), axis=2)
    meta_all = meta_all.reshape((high * high, 2 * zs) + meta.shape)
    grad_low, seq_pieces[-1] = tie(out_grad.astype(BF16), seq_pieces[-1])
    grad_first = line_step(grad_low, zs)

    length = zs * tok_rows
    heads = query_width // HEAD
    groups = kv_width // HEAD
    places = lax.rem(z + zs - jnp.arange(zs, dtype=jnp.int32), zs)
    cosine, sine = rotary_tables(length)
    qkv = None
    for j, piece in enumerate(seq_pieces):
        qkv = project(places[j], piece, w_in, cosine, sine, query_width + kv_width, qkv)
    attended, lse = attend(qkv, heads, groups)
    attended = attended.reshape(zs, tok_rows, query_width)
    attended_own = exchange(attended, "z")
    attended_own, halves_x, halves_y = tie(attended_own, halves_x, halves_y)
    attended_own, half_da, half_db = tie(attended_own, halves_x[0], halves_y[1])
    half_da, half_db = swap(half_da, "yl"), swap(half_db, "xl")
    mask_all, scale_all = chosen_tables(
        meta_all[:, :, :pick_count], meta_all[:, :, pick_count:], expert_count
    )
    side = 2 * high
    numbers = []
    for dy, dx in ((0, 0), (0, 1), (1, 0), (1, 1)):
        chip = (yh * 2 + (yl ^ dy)) * side + xh * 2 + (xl ^ dx)
        numbers.append((chip * 2 + core) * zs + z)
    mine = jnp.stack(numbers)[None, :] == jnp.arange(expert_count)[:, None]
    mask_mine = jnp.any(mine[:, :, None] & mask_all[:, :, :, None], axis=2)
    earlier = (jnp.arange(tok_rows)[:, None] < jnp.arange(tok_rows)[None, :]).astype(BF16)
    rank = jnp.einsum(
        "gpes,st->gpet", mask_mine.astype(BF16), earlier, preferred_element_type=F32
    )
    place = jnp.where(mask_mine, rank, -1.0)
    place_of_token = jnp.where(
        mask_mine, rank + (jnp.arange(4, dtype=F32) * slots)[:, None], -1.0
    ).swapaxes(2, 3)

    tables = (place, place_of_token, mask_all.astype(F32), scale_all)
    attended_own, tables = tie(attended_own, tables)
    place, place_of_token, mask_low, scale_all = tables
    branch = sum(dot(attended_own[i], w_out[i], ((1,), (1,))) for i in range(zs))
    middle = hidden_in + RESIDUAL_SCALE * branch
    normed_two, inverse_two, scaled_two = norm_rows(middle, norm2_gain)
    normed_two_low = normed_two.astype(BF16)

    rows_pieces = line_pieces(normed_two_low, zs)
    grad_first, rows_pieces[-1] = tie(grad_first, rows_pieces[-1])
    grad_next = line_step(grad_first, zs)
    rows_pieces = rows_pieces + [swap(piece, "core") for piece in rows_pieces]
    out_slots, row_slots, factor_gate, factor_up, active, gates = experts_forward(
        spread(rows_pieces, sizes),
        place,
        mask_low,
        scale_all,
        mine.astype(F32),
        w_router.T,
        (halves_o, halves_x, halves_y, half_da, half_db),
        slots,
    )
    out_slots, grad_next = tie(out_slots, grad_next)
    grad_last = line_step(grad_next, zs)
    out_terms = to_owners(
        place_of_token, [out_slots], ((0, 0), (0, 1), (0, 2), (0, 3)), slots, sizes
    )
    grad_last, out_terms[1] = tie(grad_last, out_terms[1])
    grad_pieces = [grad_low, grad_first, grad_next, grad_last]
    grad_pieces = grad_pieces + [swap(piece, "core") for piece in grad_pieces]
    out_terms[1], grad_pieces = tie(out_terms[1], grad_pieces)
    grad_pieces = spread(grad_pieces, sizes)
    saved = (row_slots, factor_gate, factor_up, active)
    out_run = line_step(out_terms[1], zs)
    rows_dx, gate_dx, gda0, gda1, gdb0, gdb1, gxa0, gxa1, gxb0, gxb1 = experts_backward(
        3, grad_pieces, place, gates, saved, (half_da, half_db, halves_x), slots
    )
    out_run = out_terms[2] + out_run
    out_run, gates, rows_dx = tie(out_run, gates, rows_dx)
    out_run = line_step(out_run, zs)
    gda0, gdb0 = swap(gda0, "yl"), swap(gdb0, "xl")
    rows_yo, gate_yo, gya0, gya1, gyb0, gyb1, goa0, goa1, gob0, gob1 = experts_backward(
        2, grad_pieces, place, gates, saved, (halves_y, halves_o), slots
    )
    out_run = out_terms[3] + out_run
    out_run, rows_yo, gda0, gdb0 = tie(out_run, rows_yo, gda0, gdb0)
    gda1, gdb1 = swap(gda1, "yl"), swap(gdb1, "xl")
    moe_terms = to_owners(
        place_of_token,
        [rows_dx, rows_yo],
        ((1, 1), (0, 1), (1, 0), (0, 0)),
        slots,
        sizes,
        (gate_dx, gate_yo),
        mine.astype(F32),
    )
    moe_terms[1], gda1, gdb1 = tie(moe_terms[1], gda1, gdb1)
    gxb0, gya0 = swap(gxb0, "xl"), swap(gya0, "yl")
    moe_run = moe_terms[2] + line_step(moe_terms[1], zs)
    moe_run, gxb0, gya0 = tie(moe_run, gxb0, gya0)
    gxb1, gya1 = swap(gxb1, "xl"), swap(gya1, "yl")
    moe_run = moe_terms[3] + line_step(moe_run, zs)
    moe_run, gxb1, gya1, gxa0, gyb0 = tie(moe_run, gxb1, gya1, gxa0 + gda0, gyb0 + gdb0)
    gxa0, gyb0 = swap(gxa0, "xl"), swap(gyb0, "yl")
    moe_sum = moe_terms[0].astype(F32) + line_step(moe_run, zs).astype(F32)
    moe_sum, gxa0, gyb0, gxa1, gyb1 = tie(moe_sum, gxa0, gyb0, gxa1 + gda1, gyb1 + gdb1)
    gxa1, gyb1 = swap(gxa1, "xl"), swap(gyb1, "yl")

    grad_normed_moe = moe_sum[:tok_rows]
    gate_grads = gates_of_extra(moe_sum[tok_rows:], expert_count, tok_rows)
    mask_own, scale_own = chosen_tables(meta[:pick_count], meta[pick_count:], expert_count)
    logits_own = dot(w_router, normed_two_low, ((0,), (1,)))
    prob_own = masked_softmax(logits_own, mask_own, 0)
    grad_scaled = gate_grads * scale_own
    grad_chosen = prob_own * (
        grad_scaled - jnp.sum(prob_own * grad_scaled, axis=0, keepdims=True)
    )
    grad_logits = grad_chosen.astype(BF16)
    grad_router_part = dot(grad_logits, normed_two_low, ((1,), (0,)))
    grad_normed_two = grad_normed_moe + dot(grad_logits, w_router, ((0,), (1,)))
    grad_middle = out_grad + norm_back(grad_normed_two, scaled_two, inverse_two, norm2_gain)
    grad_gain_two = jnp.sum(grad_normed_two * scaled_two, axis=0)
    grad_branch = (RESIDUAL_SCALE * grad_middle).astype(BF16)

    grad_attended = jnp.stack(
        [dot(grad_branch, w_out[i], ((1,), (0,))).astype(BF16) for i in range(zs)]
    )
    grad_attended = exchange(grad_attended, "z")
    gxa1, gyb1, out_run, grad_attended = tie(gxa1, gyb1, out_run, grad_attended)
    out_run = line_step(out_run, zs)
    grad_proj = attend_back(
        qkv, lse, grad_attended.reshape(length, query_width), cosine, sine, heads, groups
    )
    out_run, grad_proj = tie(out_run, grad_proj)
    grad_parts = behind(grad_proj.reshape(zs, tok_rows, -1), zs)
    grad_normed_one = line_sum([dot(g, w_in, ((1,), (1,))).astype(BF16) for g in grad_parts])
    grad_w_in, gain_rows = project_back(places, seq_pieces, grad_proj, w_in)
    shard_in = lax.psum_scatter(grad_w_in, ROWS, scatter_dimension=0, tiled=True).astype(F32)
    shard_query = shard_in[:, :query_width]
    shard_keyvalue = jnp.stack(
        [
            shard_in[:, query_width : query_width + kv_width],
            shard_in[:, query_width + kv_width :],
        ]
    )

    grad_w_gate_up, grad_w_down = unpack(
        (
            ((goa0, gxa0, gya0), (goa1, gxa1, gya1)),
            ((gob0, gxb0, gyb0), (gob1, gxb1, gyb1)),
        ),
        model_width,
    )

    attended_rows = attended_own.transpose(1, 0, 2).reshape(tok_rows, zs * query_width)
    grad_w_out = dot(grad_branch, attended_rows, ((0,), (0,))).astype(BF16)
    shard_out = lax.psum_scatter(grad_w_out, ROWS, scatter_dimension=0, tiled=True)
    shard_out = shard_out.reshape(-1, zs, query_width).transpose(1, 0, 2)
    shard_output = jnp.sum(exchange(shard_out, "z").astype(F32), axis=0).T

    normed_back = norm_back(grad_normed_one, scaled_one, inverse_one, norm1_gain)
    grad_hidden = grad_middle + normed_back
    output = middle + RESIDUAL_SCALE * (out_terms[0].astype(F32) + out_run.astype(F32))
    sums = jnp.concatenate([grad_router_part, grad_gain_two[None], gain_rows[:1]], axis=0)
    sums = sums.reshape(-1, 128)
    each = -(-sums.shape[0] // (dp_count * zs))
    sums = jnp.pad(sums, ((0, each * dp_count * zs - sums.shape[0]), (0, 0)))
    sums = jnp.sum(exchange(sums.reshape(dp_count * zs, each, 128), ALL), axis=0)
    sums = share(sums, ALL, dp_count * zs).reshape(-1, 128)
    sums = sums[: (expert_count + 2) * model_width // 128].reshape(expert_count + 2, model_width)
    return (
        output,
        grad_hidden,
        sums[expert_count + 1] / norm1_gain,
        shard_query,
        shard_keyvalue,
        shard_output,
        sums[expert_count],
        sums[:expert_count].T,
        grad_w_gate_up,
        grad_w_down,
    )


def solution(mesh):
    high = math.isqrt(mesh.shape["dp"] // 2) // 2
    zs = mesh.shape["tensor"]
    inner = Mesh(mesh.devices.reshape(high, 2, high, 2, 2, zs), ALL)
    sizes = dict(inner.shape)
    in_specs = (
        P(ALL, None),
        P(),
        P(ROWS, "z"),
        P(None, ROWS, "z"),
        P("z", ROWS),
        P(),
        P(),
        P(ALL, None, None, None),
        P(ALL, None, None),
        P(ALL, None),
        P(ALL, None),
        P(ALL, None),
    )
    out_specs = (
        P(ALL, None),
        P(ALL, None),
        P(),
        P(ROWS, "z"),
        P(None, ROWS, "z"),
        P("z", ROWS),
        P(),
        P(),
        P(ALL, None, None, None),
        P(ALL, None, None),
    )
    return jax.shard_map(
        functools.partial(local, sizes),
        mesh=inner,
        in_specs=in_specs,
        out_specs=out_specs,
        check_vma=False,
    )
```

```python
import functools
import math

import jax
import jax.numpy as jnp
from jax import lax
from jax.experimental import pallas as pl
from jax.experimental.pallas import tpu as pltpu
from jax.sharding import Mesh
from jax.sharding import PartitionSpec as P

HEAD = 64
EPSILON = 1e-06
ATTN_SCALE = 0.015625
RESIDUAL_SCALE = 0.22
THETA = 10000.0
QUERY_BLOCK = 256
F32 = jnp.float32
BF16 = jnp.bfloat16
SWAP = [(0, 1), (1, 0)]
VMEM_LIMIT = 56 * 1024 * 1024


def lasts(microseconds):
    return pl.CostEstimate(
        flops=int(microseconds * 1.15e9), bytes_accessed=1, transcendentals=0
    )


ROWS = ("yh", "yl", "xh", "xl", "core")
ALL = ROWS + ("z",)


def swap(value, axis):
    return lax.ppermute(value, axis, SWAP)


def dot(a, b, dims):
    return lax.dot_general(a, b, (dims, ((), ())), preferred_element_type=F32)


def rotary_tables(length):
    half_width = HEAD // 2
    frequency = THETA ** (-2.0 * jnp.arange(half_width, dtype=F32) / HEAD)
    angles = jnp.arange(length, dtype=F32)[:, None] * frequency[None, :]
    cosine, sine = jnp.cos(angles), jnp.sin(angles)
    return jnp.tile(cosine, (1, 4)), jnp.tile(jnp.concatenate([-sine, sine], axis=1), (1, 2))


def line_step(value, size):
    return lax.ppermute(value, "z", [(i, (i + 1) % size) for i in range(size)])


def line_pieces(value, size, count=None):
    pieces = [value]
    for _ in range((count or size) - 1):
        pieces.append(line_step(pieces[-1], size))
    return pieces


def line_order(pieces):
    size = len(pieces)
    z = lax.axis_index("z")
    whole = jnp.zeros((size,) + pieces[0].shape, pieces[0].dtype)
    for step, piece in enumerate(pieces):
        whole = lax.dynamic_update_index_in_dim(whole, piece, lax.rem(z + size - step, size), 0)
    return whole


def tie(*values):
    return lax.optimization_barrier(values)


def behind(value, size):
    z = lax.axis_index("z")
    return [
        lax.dynamic_index_in_dim(value, lax.rem(z + size - j, size), 0, False) for j in range(size)
    ]


def spread(pieces, sizes):
    if sizes["yh"] == 1:
        return [piece[None] for piece in pieces]
    return [lax.all_gather(piece, ("yh", "xh"), axis=0, tiled=False) for piece in pieces]


def exchange(value, axes):
    return lax.all_to_all(value, axes, split_axis=0, concat_axis=0, tiled=True)


def share(value, axes, count):
    return exchange(jnp.broadcast_to(value[None], (count,) + value.shape), axes)


def one_hot(place_row, slots):
    rank = lax.broadcasted_iota(jnp.int32, (slots, place_row.shape[1]), 0).astype(F32)
    return jnp.where(rank == place_row, 1.0, 0.0)


def load_weights(sources, gate_up, down, sem):
    step, inner = pl.program_id(0), pl.program_id(1)
    block, half = gate_up.shape[2] // 2, gate_up.shape[3] // 2

    def pairs(k):
        slot = k % 2
        if len(sources[k]) == 2:
            yield sources[k][0], gate_up.at[slot]
            yield sources[k][1], down.at[slot]
            return
        for n, ref in enumerate(sources[k]):
            which, piece = divmod(n, 3)
            if piece == 2:
                yield ref, down.at[slot, pl.ds(which * half, half)]
            else:
                yield ref, gate_up.at[slot, which, pl.ds(piece * block, block)]

    def copies(k):
        for n, (source, target) in enumerate(pairs(k)):
            yield pltpu.make_async_copy(source, target, sem.at[k % 2, n])

    @pl.when((step == 0) & (inner == 0))
    def _():
        for copy in copies(0):
            copy.start()

    for k in range(len(sources)):

        @pl.when((step == k) & (inner == 0))
        def _(k=k):
            for copy in copies(k):
                copy.wait()
            if k + 1 < len(sources):
                for copy in copies(k + 1):
                    copy.start()


def sources_of(refs):
    sources, refs = [], list(refs)
    while refs:
        count = 2 if len(refs[0].shape) == 3 else 6
        sources.append(refs[:count])
        refs = refs[count:]
    return sources


def weight_scratch(width, hidden):
    return [
        pltpu.VMEM((2, 2, width, hidden), BF16),
        pltpu.VMEM((2, hidden, width), BF16),
        pltpu.SemaphoreType.DMA((2, 6)),
    ]


def slot_gates_of(picks, gate_ref, group, number):
    return jnp.concatenate(
        [
            jnp.sum(pick * gate_ref[group, j, pl.ds(number, 1), :], axis=1, keepdims=True)
            for j, pick in enumerate(picks)
        ],
        axis=0,
    )


def forward_kernel(pieces, slots, first, given, *refs):
    x_refs, refs = refs[:pieces], refs[pieces:]
    place_ref, refs = refs[0], refs[1:]
    if first == 0:
        mask_ref, scale_ref, mine_ref, router_ref = refs[:4]
        gate_ref = refs[4 + given + 5]
        weights, outs = sources_of(refs[4 : 4 + given]), refs[4 + given : 4 + given + 5]
    else:
        gate_ref = refs[0]
        weights, outs = sources_of(refs[6 : 6 + given]), refs[6 + given : 6 + given + 5]
    y_ref, xs_ref, dg_ref, du_ref, act_ref = outs
    gate_up, down, sem = refs[-3:]
    step, group = pl.program_id(0), pl.program_id(1)
    number = first + step
    load_weights(weights, gate_up, down, sem)

    if first == 0:

        @pl.when(step == 0)
        def _():
            for j in range(pieces):
                mask = mask_ref[group, j]
                logits = dot(router_ref[...], x_refs[j][0], ((1,), (1,)))
                logits = jnp.where(mask > 0.0, logits, -1e30)
                top = jnp.max(logits, axis=0, keepdims=True)
                exponent = jnp.where(mask > 0.0, jnp.exp(logits - top), 0.0)
                gates = exponent / jnp.sum(exponent, axis=0, keepdims=True) * scale_ref[group, j]
                for e in range(gate_ref.shape[2]):
                    gate_ref[group, j, e : e + 1] = jnp.sum(
                        gates * mine_ref[:, e : e + 1], axis=0, keepdims=True
                    )

    picks = [one_hot(place_ref[group, j, pl.ds(number, 1), :], slots) for j in range(pieces)]
    for j, pick in enumerate(picks):
        rows = dot(pick.astype(BF16), x_refs[j][0], ((1,), (0,)))
        xs_ref[0, j * slots : (j + 1) * slots] = rows.astype(BF16)
    slot_gate = slot_gates_of(picks, gate_ref, group, number)
    now = lax.rem(step, 2)
    x = xs_ref[0]
    gate = dot(x, gate_up[now, 0], ((1,), (0,)))
    up = dot(x, gate_up[now, 1], ((1,), (0,)))
    sigmoid = 1.0 / (1.0 + jnp.exp(-gate))
    silu = gate * sigmoid
    active = (silu * up).astype(BF16)
    act_ref[0] = active
    dg_ref[0] = (up * sigmoid * (1.0 + gate * (1.0 - sigmoid))).astype(BF16)
    du_ref[0] = silu.astype(BF16)
    weighted = (active.astype(F32) * slot_gate).astype(BF16)
    y_ref[0] = dot(weighted, down[now], ((1,), (0,))).astype(BF16)


def backward_kernel(pieces, slots, first, given, *refs):
    g_refs, refs = refs[:pieces], refs[pieces:]
    place_ref, gate_ref, xs_ref, dg_ref, du_ref, act_ref = refs[:6]
    weights, refs = sources_of(refs[6 : 6 + given]), refs[6 + given :]
    experts = len(weights)
    rows_ref, through_ref = refs[:2]
    results = [refs[2 + 6 * k : 8 + 6 * k] for k in range(experts)]
    gate_up, down, sem, gs_ref, stage, stage_down, out_sem = refs[2 + 6 * experts : 9 + 6 * experts]
    sums = refs[9 + 6 * experts :]
    step, group = pl.program_id(0), pl.program_id(1)
    number = first - 2 * step
    load_weights(weights, gate_up, down, sem)
    width = g_refs[0].shape[-1]
    half = down.shape[1] // 2
    now = lax.rem(step, 2)
    last = pl.num_programs(1) - 1

    def stores(k):
        block = width // 2
        for n, ref in enumerate(results[k]):
            which, piece = divmod(n, 3)
            source = stage_down.at[pl.ds(which * half, half)]
            if piece < 2:
                source = stage.at[which, pl.ds(piece * block, block)]
            yield pltpu.make_async_copy(source, ref, out_sem.at[n])

    picks = [one_hot(place_ref[group, j, pl.ds(number, 1), :], slots) for j in range(pieces)]
    for j, pick in enumerate(picks):
        rows = dot(pick.astype(BF16), g_refs[j][0], ((1,), (0,)))
        gs_ref[j * slots : (j + 1) * slots] = rows.astype(BF16)
    slot_gate = slot_gates_of(picks, gate_ref, group, number) * RESIDUAL_SCALE
    grad_active = dot(gs_ref[...], down[now], ((1,), (1,)))
    active = act_ref[0].astype(F32)
    through = jnp.sum(grad_active * active, axis=1, keepdims=True) * RESIDUAL_SCALE
    for j, pick in enumerate(picks):
        through_ref[0, 0, j : j + 1] = jnp.sum(
            pick * through[j * slots : (j + 1) * slots], axis=0, keepdims=True
        )
    grad_active = grad_active * slot_gate
    grad_gate = (grad_active * dg_ref[0].astype(F32)).astype(BF16)
    grad_up = (grad_active * du_ref[0].astype(F32)).astype(BF16)
    rows = dot(grad_gate, gate_up[now, 0], ((1,), (1,)))
    rows = rows + dot(grad_up, gate_up[now, 1], ((1,), (1,)))
    rows_ref[0] = rows.astype(BF16)
    weighted = (active * slot_gate).astype(BF16)

    for k in range(1, experts):

        @pl.when((step == k) & (group == last))
        def _(k=k):
            for copy in stores(k - 1):
                copy.wait()

    def add(target, total, left, right):
        part = dot(left, right, ((0,), (0,)))
        if total is None:
            target[...] = part.astype(BF16)
            return

        @pl.when(group == 0)
        def _():
            total[...] = part

        @pl.when(group > 0)
        def _():
            total[...] += part

        @pl.when(group == last)
        def _():
            target[...] = total[...].astype(BF16)

    x = xs_ref[0]
    totals = [sums[0].at[0], sums[0].at[1], sums[1]] if sums else [None] * 3
    add(stage.at[0], totals[0], x, grad_gate)
    add(stage.at[1], totals[1], x, grad_up)
    add(stage_down, totals[2], weighted, gs_ref[...])
    for k in range(experts):

        @pl.when((step == k) & (group == last))
        def _(k=k):
            for copy in stores(k):
                copy.start()
            if k == experts - 1:
                for copy in stores(k):
                    copy.wait()


def resident(arrays):
    return [
        pl.BlockSpec(a.shape, lambda e, c, n=a.ndim: (0,) * n, pipeline_mode=pl.Buffered(1))
        for a in arrays
    ]


def piece_spec(piece):
    groups, tokens, width = piece.shape
    mode = pl.Buffered(1) if groups == 1 else None
    return pl.BlockSpec((1, tokens, width), lambda e, c: (c, 0, 0), pipeline_mode=mode)


def experts_forward(first, x_pieces, place, tables, weights, slots, before=None):
    pieces = len(x_pieces)
    groups, tokens, width = x_pieces[0].shape
    hidden = weights[0][0].shape[-1]
    rows = pieces * slots
    experts = place.shape[2]
    anywhere = pl.BlockSpec(memory_space=pl.ANY)
    flat = [array for pair in weights for array in pair]
    before = list(before or [])

    def by_slot(n):
        return pl.BlockSpec((1, rows, n), lambda e, c: (first + e, c, 0))

    gate_shape = (groups, pieces, experts, tokens)
    widths = (width, width, hidden, hidden, hidden)
    out_specs = [by_slot(n) for n in widths]
    out_shape = [jax.ShapeDtypeStruct((experts, groups * rows, n), BF16) for n in widths]
    if first == 0:
        out_specs.append(pl.BlockSpec(gate_shape, lambda e, c: (0, 0, 0, 0)))
        out_shape.append(jax.ShapeDtypeStruct(gate_shape, F32))
    operands = [*x_pieces, place, *tables]
    return pl.pallas_call(
        functools.partial(forward_kernel, pieces, slots, first, len(flat)),
        grid=(len(weights), groups),
        in_specs=[piece_spec(p) for p in x_pieces]
        + resident([place, *tables])
        + [anywhere] * (len(before) + len(flat)),
        out_specs=out_specs,
        out_shape=out_shape,
        input_output_aliases={len(operands) + n: n for n in range(len(before))},
        scratch_shapes=weight_scratch(width, hidden),
        compiler_params=pltpu.CompilerParams(vmem_limit_bytes=VMEM_LIMIT),
        cost_estimate=lasts(8.0 * len(weights)),
        name="experts_forward",
    )(*operands, *before, *flat)


def experts_backward(first, g_pieces, place, gates, saved, weights, slots):
    pieces = len(g_pieces)
    groups, tokens, width = g_pieces[0].shape
    experts = len(weights)
    hidden = weights[0][0].shape[-1]
    rows = pieces * slots
    flat = [array for pair in weights for array in pair]

    def by_slot(n):
        return pl.BlockSpec((1, rows, n), lambda e, c: (first - 2 * e, c, 0))

    anywhere = pl.BlockSpec(memory_space=pl.ANY)
    block = jax.ShapeDtypeStruct((width // 2, hidden), BF16)
    return pl.pallas_call(
        functools.partial(backward_kernel, pieces, slots, first, len(flat)),
        grid=(experts, groups),
        in_specs=[piece_spec(p) for p in g_pieces]
        + resident([place, gates])
        + [by_slot(width)]
        + [by_slot(hidden)] * 3
        + [anywhere] * len(flat),
        out_specs=[
            pl.BlockSpec((1, rows, width), lambda e, c: (e, c, 0)),
            pl.BlockSpec((1, 1, pieces, tokens), lambda e, c: (e, c, 0, 0)),
        ]
        + [anywhere] * (6 * experts),
        out_shape=[
            jax.ShapeDtypeStruct((experts, groups * rows, width), BF16),
            jax.ShapeDtypeStruct((experts, groups, pieces, tokens), F32),
        ]
        + [block, block, jax.ShapeDtypeStruct((hidden // 2, width), BF16)] * (2 * experts),
        scratch_shapes=weight_scratch(width, hidden)
        + [
            pltpu.VMEM((rows, width), BF16),
            pltpu.VMEM((2, width, hidden), BF16),
            pltpu.VMEM((hidden, width), BF16),
            pltpu.SemaphoreType.DMA((6,)),
        ]
        + (
            [pltpu.VMEM((2, width, hidden), F32), pltpu.VMEM((hidden, width), F32)]
            if groups > 1
            else []
        ),
        compiler_params=pltpu.CompilerParams(vmem_limit_bytes=VMEM_LIMIT),
        cost_estimate=lasts(14.5 * experts),
        name="experts_backward",
    )(*g_pieces, place, gates, *saved, *flat)


def extra_rows(expert_count, tokens, width):
    return 16 * -(-(-(-2 * expert_count // 16)) // (width // tokens))


def extra_places(expert_count, tokens, width):
    across = width // tokens
    for block in range(-(-2 * expert_count // 16)):
        yield block, 16 * (block // across), tokens * (block % across)


def combine_kernel(order, slots, extra, pieces, place_ref, *refs):
    parts = 1 + max(which for which, _ in order)
    experts = len(order)
    rows_refs, refs = refs[:parts], refs[parts:]
    if extra:
        through_refs, mine_ref, refs = refs[:parts], refs[parts], refs[parts + 1 :]
    step = pl.program_id(0)
    tokens = place_ref.shape[1]
    lane = lax.broadcasted_iota(jnp.int32, (tokens, experts * slots), 1).astype(F32)
    hit = lane == place_ref[0, :, 0:1]
    for e in range(1, experts):
        hit = hit | (lane == place_ref[0, :, e : e + 1])
    pick = jnp.where(hit, 1.0, 0.0).astype(BF16)
    rows = jnp.concatenate([rows_refs[which][k] for which, k in order], axis=0)
    out = dot(pick, rows, ((1,), (0,)))
    width = out.shape[1]
    more = None
    if extra:
        dense = 0.0
        for e, (which, k) in enumerate(order):
            dense = dense + mine_ref[:, e : e + 1] * through_refs[which][k, 0]
        high = dense.astype(BF16).astype(F32)
        both = jnp.concatenate([high, dense - high], axis=0)
        across = width // tokens
        lines = []
        for start in range(0, both.shape[0], 16 * across):
            line = [both[i : i + 16] for i in range(start, min(start + 16 * across, both.shape[0]), 16)]
            line += [jnp.zeros((16, tokens), F32)] * (across - len(line))
            lines.append(jnp.concatenate(line, axis=1))
        more = jnp.concatenate(lines, axis=0)

    def store(ref):
        if not pieces:
            ref[0, :tokens] = out.astype(BF16)
            if extra:
                ref[0, tokens:] = more.astype(BF16)
            return
        ref[0, :tokens] = (out + refs[0][0, :tokens].astype(F32)).astype(BF16)
        if extra:
            ref[0, tokens:] = (more + refs[0][0, tokens:].astype(F32)).astype(BF16)

    if not pieces:
        store(refs[0])
        return
    for j in range(pieces):

        @pl.when(lax.rem(step, pieces) == j)
        def _(j=j):
            store(refs[1 + j])


def combine(place, parts, order, slots, half, start, count, other=None, through=None, mine=None):
    groups, pieces, tokens, experts = place.shape
    column = pieces // 2
    width = parts[0].shape[-1]
    extra = 0 if through is None else extra_rows(mine.shape[0], tokens, width)

    def at(i):
        return (i // count) * pieces + half * column + (start + i % count) % column

    in_specs = [pl.BlockSpec((1, tokens, experts), lambda i: (at(i), 0, 0))]
    in_specs += [pl.BlockSpec((p.shape[0], slots, width), lambda i: (0, at(i), 0)) for p in parts]
    operands = [place.reshape(groups * pieces, tokens, experts), *parts]
    if extra:
        in_specs += [
            pl.BlockSpec((t.shape[0], 1, 1, tokens), lambda i: (0, at(i), 0, 0)) for t in through
        ]
        in_specs.append(pl.BlockSpec(mine.shape, lambda i: (0, 0)))
        operands += [t.reshape(t.shape[0], groups * pieces, 1, tokens) for t in through] + [mine]
    rows = tokens + extra
    by_step = pl.BlockSpec((1, rows, width), lambda i: (i, 0, 0))
    if other is None:
        out_specs, out_shape = by_step, jax.ShapeDtypeStruct((groups * count, rows, width), BF16)
    else:
        in_specs.append(by_step)
        operands.append(other)
        out_specs = [pl.BlockSpec((1, rows, width), lambda i: (i // count, 0, 0))] * count
        out_shape = [jax.ShapeDtypeStruct((groups, rows, width), BF16)] * count
    return pl.pallas_call(
        functools.partial(combine_kernel, order, slots, extra, 0 if other is None else count),
        grid=(groups * count,),
        in_specs=in_specs,
        out_specs=out_specs,
        out_shape=out_shape,
        compiler_params=pltpu.CompilerParams(vmem_limit_bytes=VMEM_LIMIT),
        cost_estimate=lasts(0.1),
        name="combine",
    )(*operands)


def only_own(terms, sizes):
    if sizes["yh"] == 1:
        return [term[0] for term in terms]
    return [
        lax.psum_scatter(term, ("yh", "xh"), scatter_dimension=0, tiled=True)[0] for term in terms
    ]


def packed_specs(width, hidden):
    block = width // 2
    return (
        pl.BlockSpec((1, 1, block, hidden), lambda h, i: (0, h, jnp.minimum(i, 1), 0)),
        pl.BlockSpec((1, hidden // 2, width), lambda h, i: (0, h, 0)),
    )


def take_kernel(gate_ref, down_a_ref, up_ref, down_b_ref, *out_refs):
    step = pl.program_id(0)
    for n in (0, 1):

        @pl.when(step == n)
        def _(n=n):
            out_refs[n][...] = gate_ref[0]
            out_refs[3 + n][...] = up_ref[0]

    @pl.when(step == 2)
    def _():
        out_refs[2][...] = down_a_ref[...]
        out_refs[5][...] = down_b_ref[...]


def take_pieces(gate_up_x, down_x, gate_up_y, down_y):
    _, width, hidden = gate_up_x.shape
    block, half = width // 2, hidden // 2

    def specs(which):
        return [
            pl.BlockSpec((1, block, hidden), lambda i: (which, jnp.minimum(i, 1), 0)),
            pl.BlockSpec((half, width), lambda i: (which, 0)),
        ]

    shapes = [(block, hidden), (block, hidden), (half, width)] * 2
    return pl.pallas_call(
        take_kernel,
        grid=(3,),
        in_specs=specs(0) + specs(1),
        out_specs=[pl.BlockSpec(shape, lambda i: (0, 0)) for shape in shapes],
        out_shape=[jax.ShapeDtypeStruct(shape, BF16) for shape in shapes],
        compiler_params=pltpu.CompilerParams(vmem_limit_bytes=VMEM_LIMIT),
        cost_estimate=lasts(4.0),
        name="take_pieces",
    )(gate_up_x, down_x, gate_up_y, down_y)


def collect_kernel(*refs):
    gate_up_ref, down_ref, wide, deep, sem = refs[-5:]
    step = pl.program_id(0) * 3 + pl.program_id(1)

    def slot(n):
        return deep.at[n // 3] if n % 3 == 2 else wide.at[n % 3]

    def copies(n):
        for k in range(3):
            yield pltpu.make_async_copy(refs[3 * n + k], slot(n).at[k], sem.at[n, k])

    @pl.when(step == 0)
    def _():
        for n in (0, 1, 2, 5):
            for copy in copies(n):
                copy.start()

    for n in range(6):

        @pl.when(step == n)
        def _(n=n):
            for copy in copies(n):
                copy.wait()
            here = slot(n)
            total = here[0].astype(F32) + here[1].astype(F32) + here[2].astype(F32)
            if n % 3 < 2:
                gate_up_ref[0, 0] = total
            else:
                down_ref[0] = total
            if n < 2:
                for copy in copies(n + 3):
                    copy.start()


def collect(pieces, width):
    hidden = pieces[0][0].shape[1]
    gate_up_spec, down_spec = packed_specs(width, hidden)
    return pl.pallas_call(
        collect_kernel,
        grid=(2, 3),
        in_specs=[pl.BlockSpec(memory_space=pl.ANY)] * 18,
        out_specs=[gate_up_spec, down_spec],
        out_shape=[
            jax.ShapeDtypeStruct((1, 2, width, hidden), F32),
            jax.ShapeDtypeStruct((1, hidden, width), F32),
        ],
        scratch_shapes=[
            pltpu.VMEM((2, 3, width // 2, hidden), BF16),
            pltpu.VMEM((2, 3, hidden // 2, width), BF16),
            pltpu.SemaphoreType.DMA((6, 3)),
        ],
        compiler_params=pltpu.CompilerParams(vmem_limit_bytes=VMEM_LIMIT),
        cost_estimate=lasts(9.5),
        name="collect",
    )(*[array for piece in pieces for array in piece])


def inverse_root(values):
    return lax.rsqrt(jnp.mean(values * values, axis=-1, keepdims=True) + EPSILON)


def branch_kernel(place_ref, att_ref, w_ref, hidden_ref, gain_ref, middle_ref, low_ref):
    step = pl.program_id(0)
    weights = w_ref[:, 0].reshape(hidden_ref.shape[1], w_ref.shape[-1])
    part = RESIDUAL_SCALE * dot(att_ref[0], weights, ((1,), (1,)))

    @pl.when(step == 0)
    def _():
        middle_ref[...] = hidden_ref[...] + part

    @pl.when(step > 0)
    def _():
        middle_ref[...] += part

    @pl.when(step == pl.num_programs(0) - 1)
    def _():
        middle = middle_ref[...]
        low_ref[...] = (middle * inverse_root(middle) * gain_ref[...]).astype(BF16)


def out_weights_spec(weights):
    rows, _, height, columns = weights.shape
    return pl.BlockSpec((rows, 1, height, columns), lambda i, p: (0, i, 0, 0))


def branch_norm(places, attended, weights, hidden, gain):
    count, tokens, columns = attended.shape
    width = hidden.shape[1]
    return pl.pallas_call(
        branch_kernel,
        grid_spec=pltpu.PrefetchScalarGridSpec(
            num_scalar_prefetch=1,
            grid=(count,),
            in_specs=[
                pl.BlockSpec((1, tokens, columns), lambda i, p: (p[i], 0, 0)),
                out_weights_spec(weights),
                pl.BlockSpec((tokens, width), lambda i, p: (0, 0)),
                pl.BlockSpec((1, width), lambda i, p: (0, 0)),
            ],
            out_specs=[pl.BlockSpec((tokens, width), lambda i, p: (0, 0))] * 2,
        ),
        out_shape=[
            jax.ShapeDtypeStruct((tokens, width), F32),
            jax.ShapeDtypeStruct((tokens, width), BF16),
        ],
        compiler_params=pltpu.CompilerParams(vmem_limit_bytes=VMEM_LIMIT),
        cost_estimate=lasts(7.0),
        name="branch_norm",
    )(places, attended, weights, hidden, gain.reshape(1, width))


def moe_back_kernel(
    extra, place_ref, own_ref, run_ref, prob_ref, scale_ref, router_ref, low_ref, middle_ref, gain_ref, grad_ref, w_ref,
    grad_middle_ref, branch_ref, attended_ref, sums_ref,
):
    tokens = middle_ref.shape[0]

    @pl.when(pl.program_id(0) == 0)
    def _():
        experts = prob_ref.shape[0]

        def total(rows, columns=slice(None)):
            return own_ref[rows, columns].astype(F32) + run_ref[rows, columns].astype(F32)

        both = jnp.concatenate(
            [
                total(slice(tokens + row, tokens + row + 16), slice(column, column + tokens))
                for _, row, column in extra
            ],
            axis=0,
        )
        scaled = (both[:experts] + both[experts : 2 * experts]) * scale_ref[...]
        prob = prob_ref[...]
        chosen = prob * (scaled - jnp.sum(prob * scaled, axis=0, keepdims=True))
        chosen = chosen.astype(BF16)
        sums_ref[:experts] = dot(chosen, low_ref[...], ((1,), (0,)))
        grad = total(slice(0, tokens)) + dot(chosen, router_ref[...], ((0,), (0,)))
        middle = middle_ref[...]
        inverse = inverse_root(middle)
        scaled = middle * inverse
        sums_ref[experts:] = jnp.zeros((sums_ref.shape[0] - experts, middle.shape[1]), F32)
        sums_ref[experts : experts + 1] = jnp.sum(grad * scaled, axis=0, keepdims=True)
        grad = grad * gain_ref[...]
        mean = jnp.mean(grad * scaled, axis=-1, keepdims=True)
        grad = grad_ref[...] + inverse * (grad - scaled * mean)
        grad_middle_ref[...] = grad
        branch_ref[...] = (RESIDUAL_SCALE * grad).astype(BF16)

    weights = w_ref[:, 0].reshape(middle_ref.shape[1], w_ref.shape[-1])
    attended_ref[0] = dot(branch_ref[...], weights, ((1,), (0,))).astype(BF16)


def moe_back(places, rows, own, run, prob, scale, router, low, middle, gain, grad, weights):
    tokens, width = middle.shape
    experts = prob.shape[0]
    _, count, _, columns = weights.shape
    extra = list(extra_places(experts, tokens, width))
    operands = [own, run, prob, scale, router, low, middle, gain.reshape(1, width), grad]
    return pl.pallas_call(
        functools.partial(moe_back_kernel, extra),
        grid_spec=pltpu.PrefetchScalarGridSpec(
            num_scalar_prefetch=1,
            grid=(count,),
            in_specs=[pl.BlockSpec(a.shape, lambda i, p: (0, 0)) for a in operands]
            + [out_weights_spec(weights)],
            out_specs=[
                pl.BlockSpec((tokens, width), lambda i, p: (0, 0)),
                pl.BlockSpec((tokens, width), lambda i, p: (0, 0)),
                pl.BlockSpec((1, tokens, columns), lambda i, p: (p[i], 0, 0)),
                pl.BlockSpec((rows, width), lambda i, p: (0, 0)),
            ],
        ),
        out_shape=[
            jax.ShapeDtypeStruct((tokens, width), F32),
            jax.ShapeDtypeStruct((tokens, width), BF16),
            jax.ShapeDtypeStruct((count, tokens, columns), BF16),
            jax.ShapeDtypeStruct((rows, width), F32),
        ],
        compiler_params=pltpu.CompilerParams(vmem_limit_bytes=VMEM_LIMIT),
        cost_estimate=lasts(20.0),
        name="moe_back",
    )(places, *operands, weights)


def finish_kernel(own_ref, run_ref, hidden_ref, gain_ref, grad_ref, out_ref):
    grad = own_ref[...].astype(F32) + run_ref[...].astype(F32)
    hidden = hidden_ref[...]
    inverse = inverse_root(hidden)
    scaled = hidden * inverse
    grad = grad * gain_ref[...]
    mean = jnp.mean(grad * scaled, axis=-1, keepdims=True)
    out_ref[...] = grad_ref[...] + inverse * (grad - scaled * mean)


def finish(own, run, hidden, gain, grad):
    tokens, width = hidden.shape
    rows = pl.BlockSpec((tokens // 2, width), lambda i: (i, 0))
    return pl.pallas_call(
        finish_kernel,
        grid=(2,),
        in_specs=[rows, rows, rows, pl.BlockSpec((1, width), lambda i: (0, 0)), rows],
        out_specs=rows,
        out_shape=jax.ShapeDtypeStruct((tokens, width), F32),
        compiler_params=pltpu.CompilerParams(vmem_limit_bytes=VMEM_LIMIT),
        cost_estimate=lasts(3.5),
        name="finish",
    )(own, run, hidden, gain.reshape(1, width), grad)


def causal_mask(scores, start):
    keys, columns = scores.shape
    block = keys - start
    key = lax.broadcasted_iota(jnp.int32, (block, columns), 0)
    query = lax.rem(lax.broadcasted_iota(jnp.int32, (block, columns), 1), block)
    low = jnp.where(key <= query, scores[start:], -1e30)
    return low if start == 0 else jnp.concatenate([scores[:start], low], axis=0)


def head_rows(pair, odd):
    lane = lax.broadcasted_iota(jnp.int32, pair.shape, 1)
    return jnp.where((lane >= HEAD) == odd, pair, jnp.zeros_like(pair))


def both_halves(rows):
    return jnp.concatenate([rows, rows], axis=1)


def attend_kernel(heads, groups, block, qkv_ref, out_ref, lse_ref):
    length = qkv_ref.shape[0]
    each = heads // groups
    at_key = heads * HEAD
    at_value = at_key + groups * HEAD
    for i in range(length // block):
        start, stop = i * block, (i + 1) * block
        parts = []
        for g in range(groups):
            key = both_halves(qkv_ref[:stop, at_key + g * HEAD : at_key + (g + 1) * HEAD])
            value = qkv_ref[:stop, at_value + g * HEAD : at_value + (g + 1) * HEAD]
            query = []
            for h in range(g * each, (g + 1) * each):
                pair = qkv_ref[start:stop, h // 2 * 2 * HEAD : (h // 2 + 1) * 2 * HEAD]
                query.append(head_rows(pair, h % 2 == 1) * ATTN_SCALE)
            query = jnp.concatenate(query, axis=0).astype(BF16)
            scores = causal_mask(dot(key, query, ((1,), (1,))), start)
            top = jnp.max(scores, axis=0, keepdims=True)
            exponent = jnp.exp(scores - top)
            norm = jnp.sum(exponent, axis=0, keepdims=True)
            total = top + jnp.log(norm)
            out = dot(value, exponent.astype(BF16), ((0,), (0,))) / norm
            for k in range(each):
                columns = slice(k * block, (k + 1) * block)
                lse_ref[g * each + k : g * each + k + 1, start:stop] = total[:, columns]
                parts.append(out[:, columns])
        for pair in range(heads // 2):
            rows = jnp.concatenate(parts[2 * pair : 2 * pair + 2], axis=0)
            out_ref[start:stop, pair * 2 * HEAD : (pair + 1) * 2 * HEAD] = rows.T.astype(BF16)


def attend(qkv, heads, groups):
    length = qkv.shape[0]
    return pl.pallas_call(
        functools.partial(attend_kernel, heads, groups, min(QUERY_BLOCK, length)),
        out_shape=[
            jax.ShapeDtypeStruct((length, heads * HEAD), BF16),
            jax.ShapeDtypeStruct((8 * -(-heads // 8), length), F32),
        ],
        compiler_params=pltpu.CompilerParams(vmem_limit_bytes=VMEM_LIMIT),
        cost_estimate=lasts(8.0),
        name="attend",
    )(qkv)


def turn(values, cosine, sine, direction):
    width = values.shape[1]
    lane = lax.broadcasted_iota(jnp.int32, values.shape, 1)
    first = lax.rem(lane, HEAD) < HEAD // 2
    behind_half = pltpu.roll(values, width - HEAD // 2, 1)
    other = jnp.where(first, behind_half, pltpu.roll(values, HEAD // 2, 1))
    repeats = width // cosine.shape[1]
    cosine = jnp.concatenate([cosine] * repeats, axis=1) if repeats > 1 else cosine
    sine = jnp.concatenate([sine] * repeats, axis=1) if repeats > 1 else sine
    return values * cosine + direction * (other * sine)


def attend_back_kernel(
    heads, groups, block, qkv_ref, lse_ref, grad_ref, cos_ref, sin_ref, out_ref, key_sum, value_sum
):
    length = qkv_ref.shape[0]
    each = heads // groups
    at_key = heads * HEAD
    at_value = at_key + groups * HEAD
    for i in reversed(range(length // block)):
        start, stop = i * block, (i + 1) * block
        parts = []
        for g in range(groups):
            key = qkv_ref[:stop, at_key + g * HEAD : at_key + (g + 1) * HEAD]
            value = both_halves(qkv_ref[:stop, at_value + g * HEAD : at_value + (g + 1) * HEAD])
            query, grad, lse = [], [], []
            for h in range(g * each, (g + 1) * each):
                columns = slice(h // 2 * 2 * HEAD, (h // 2 + 1) * 2 * HEAD)
                query.append(head_rows(qkv_ref[start:stop, columns], h % 2 == 1) * ATTN_SCALE)
                grad.append(head_rows(grad_ref[start:stop, columns], h % 2 == 1))
                lse.append(lse_ref[h : h + 1, start:stop])
            query = jnp.concatenate(query, axis=0).astype(BF16)
            grad = jnp.concatenate(grad, axis=0)
            lse = jnp.concatenate(lse, axis=1)
            scores = causal_mask(dot(both_halves(key), query, ((1,), (1,))), start)
            probs = jnp.exp(scores - lse)
            grad_probs = dot(value, grad, ((1,), (1,)))
            weighted = probs * grad_probs
            delta = jnp.sum(weighted, axis=0, keepdims=True)
            grad_scores = (weighted - probs * delta).astype(BF16)
            grad_value = dot(probs.astype(BF16), grad, ((1,), (0,)))
            grad_key = dot(grad_scores, query, ((1,), (0,)))
            if stop == length:
                value_sum[g] = grad_value
                key_sum[g] = grad_key
            else:
                value_sum[g, :stop] += grad_value
                key_sum[g, :stop] += grad_key
            grad_query = dot(key, grad_scores, ((0,), (0,))) * ATTN_SCALE
            for k in range(each):
                parts.append(grad_query[:, k * block : (k + 1) * block])
        cosine, sine = cos_ref[start:stop], sin_ref[start:stop]
        for pair in range(heads // 2):
            rows = jnp.concatenate(parts[2 * pair : 2 * pair + 2], axis=0).T
            rows = turn(rows, cosine, sine, -1.0).astype(BF16)
            out_ref[start:stop, pair * 2 * HEAD : (pair + 1) * 2 * HEAD] = rows
    rows = [key_sum[g][:, :HEAD] + key_sum[g][:, HEAD:] for g in range(groups)]
    rows = turn(jnp.concatenate(rows, axis=1), cos_ref[...], sin_ref[...], -1.0)
    out_ref[:, at_key:at_value] = rows.astype(BF16)
    rows = [value_sum[g][:, :HEAD] + value_sum[g][:, HEAD:] for g in range(groups)]
    out_ref[:, at_value:] = jnp.concatenate(rows, axis=1).astype(BF16)


def attend_back(qkv, lse, grad, cosine, sine, heads, groups):
    length = qkv.shape[0]
    return pl.pallas_call(
        functools.partial(attend_back_kernel, heads, groups, min(QUERY_BLOCK, length)),
        out_shape=jax.ShapeDtypeStruct(qkv.shape, BF16),
        scratch_shapes=[pltpu.VMEM((groups, length, 2 * HEAD), F32)] * 2,
        compiler_params=pltpu.CompilerParams(vmem_limit_bytes=VMEM_LIMIT),
        cost_estimate=lasts(14.0),
        name="attend_back",
    )(qkv, lse, grad, cosine, sine)


def project_kernel(turned, place_ref, x_ref, w_ref, cos_ref, sin_ref, *refs):
    out_ref = refs[-1]
    values = dot(x_ref[...], w_ref[...], ((1,), (0,)))
    out_ref[:, :turned] = turn(values[:, :turned], cos_ref[...], sin_ref[...], 1.0).astype(BF16)
    out_ref[:, turned:] = values[:, turned:].astype(BF16)


def project(place, rows, weights, cosine, sine, turned, before=None):
    tokens, width = rows.shape
    columns = weights.shape[1]
    in_specs = [
        pl.BlockSpec((tokens, width), lambda i, p: (0, 0)),
        pl.BlockSpec((width, columns), lambda i, p: (0, 0)),
        pl.BlockSpec((tokens, cosine.shape[1]), lambda i, p: (p[0], 0)),
        pl.BlockSpec((tokens, sine.shape[1]), lambda i, p: (p[0], 0)),
    ]
    operands = [place.reshape(1), rows, weights, cosine, sine]
    if before is not None:
        in_specs.append(pl.BlockSpec(memory_space=pl.ANY))
        operands.append(before)
    return pl.pallas_call(
        functools.partial(project_kernel, turned),
        grid_spec=pltpu.PrefetchScalarGridSpec(
            num_scalar_prefetch=1,
            grid=(1,),
            in_specs=in_specs,
            out_specs=pl.BlockSpec((tokens, columns), lambda i, p: (p[0], 0)),
        ),
        out_shape=jax.ShapeDtypeStruct((cosine.shape[0], columns), BF16),
        input_output_aliases={} if before is None else {5: 0},
        compiler_params=pltpu.CompilerParams(vmem_limit_bytes=VMEM_LIMIT),
        cost_estimate=lasts(4.0),
        name="project",
    )(*operands)


def project_back_kernel(pieces, place_ref, *refs):
    x_refs = refs[:pieces]
    grad_ref, w_ref, out_ref, gain_ref = refs[pieces:]
    tokens = x_refs[0].shape[0]
    grad = 0.0
    for j in range(pieces):
        start = pl.multiple_of(place_ref[j] * tokens, tokens)
        grad = grad + dot(x_refs[j][...], grad_ref[pl.ds(start, tokens), :], ((0,), (0,)))
    out_ref[...] = grad.astype(BF16)
    ones = jnp.ones((8, w_ref.shape[1]), BF16)
    products = w_ref[...].astype(F32) * grad
    high = products.astype(BF16)
    low = (products - high.astype(F32)).astype(BF16)
    gain_ref[...] = dot(ones, high, ((1,), (1,))) + dot(ones, low, ((1,), (1,)))


def project_back(places, pieces, grad, weights):
    tokens, width = pieces[0].shape
    columns = weights.shape[1]
    cut = width // 3
    return pl.pallas_call(
        functools.partial(project_back_kernel, len(pieces)),
        grid_spec=pltpu.PrefetchScalarGridSpec(
            num_scalar_prefetch=1,
            grid=(3,),
            in_specs=[pl.BlockSpec((tokens, cut), lambda i, p: (0, i))] * len(pieces)
            + [
                pl.BlockSpec(grad.shape, lambda i, p: (0, 0)),
                pl.BlockSpec((cut, columns), lambda i, p: (i, 0)),
            ],
            out_specs=[
                pl.BlockSpec((cut, columns), lambda i, p: (i, 0)),
                pl.BlockSpec((8, cut), lambda i, p: (0, i)),
            ],
        ),
        out_shape=[
            jax.ShapeDtypeStruct((width, columns), BF16),
            jax.ShapeDtypeStruct((8, width), F32),
        ],
        compiler_params=pltpu.CompilerParams(vmem_limit_bytes=VMEM_LIMIT),
        cost_estimate=lasts(9.0),
        name="project_back",
    )(places, *pieces, grad, weights)


def chosen_tables(ids, scale, expert_count):
    lead = (1,) * (ids.ndim - 2)
    numbers = jnp.arange(expert_count, dtype=F32).reshape(lead + (1, expert_count, 1))
    hits = ids[..., :, None, :] == numbers
    mask = jnp.any(hits, axis=-3)
    return mask, jnp.sum(jnp.where(hits, scale[..., :, None, :], 0.0), axis=-3)


def masked_softmax(logits, mask, axis):
    top = jnp.max(jnp.where(mask, logits, -jnp.inf), axis=axis, keepdims=True)
    exponent = jnp.where(mask, jnp.exp(jnp.where(mask, logits - top, 0.0)), 0.0)
    return exponent / jnp.sum(exponent, axis=axis, keepdims=True)


def local(
    sizes,
    hidden_in,
    norm1_gain,
    w_query,
    w_keyvalue,
    w_output,
    norm2_gain,
    w_router,
    w_gate_up,
    w_down,
    expert_ids,
    choice_scale,
    out_grad,
):
    tok_rows, model_width = hidden_in.shape
    pick_count = expert_ids.shape[1]
    expert_count = w_router.shape[1]
    capacity = max(2, (tok_rows * pick_count * 11 + 8 * expert_count - 1) // (8 * expert_count))
    slots = -(-capacity // 16) * 16
    zs, high = sizes["z"], sizes["yh"]
    yl, xl, core, z = (lax.axis_index(a) for a in ("yl", "xl", "core", "z"))
    yh, xh = lax.axis_index("yh"), lax.axis_index("xh")

    packed = jnp.concatenate([w_query, w_keyvalue[0], w_keyvalue[1]], axis=1)
    dp_count = 8 * high * high
    w_in = lax.all_gather(packed, ROWS, axis=0, tiled=True)
    query_width = w_query.shape[1]
    kv_width = w_keyvalue.shape[2]
    normed_low = (hidden_in * inverse_root(hidden_in) * norm1_gain).astype(BF16)
    weights_o = (w_gate_up[0], w_down[0])
    weights_x = tuple(swap(w, "xl") for w in weights_o)
    weights_y = tuple(swap(w, "yl") for w in weights_o)
    w_out = share(w_output.T, "z", zs)
    seq_pieces = [normed_low, line_step(normed_low, zs)]
    w_out = lax.all_gather(w_out, ROWS, axis=0)
    seq_pieces.append(line_step(seq_pieces[1], zs))
    seq_pieces[2], w_in = tie(seq_pieces[2], w_in)
    seq_pieces.append(line_step(seq_pieces[2], zs))
    meta = jnp.concatenate([expert_ids.astype(F32).T, choice_scale.T], axis=0)
    grad_low, meta, seq_pieces[-1] = tie(out_grad.astype(BF16), meta, seq_pieces[-1])
    grad_first = line_step(grad_low, zs)
    meta_all = share(meta, ("yh", "xh", "core", "z"), high * high * 2 * zs)
    meta_all = meta_all.reshape((high * high, 2, zs) + meta.shape)
    meta_all = jnp.where(core == 1, meta_all[:, ::-1], meta_all)
    meta_all = jnp.stack(behind(jnp.moveaxis(meta_all, 2, 0), zs), axis=2)
    meta_all = meta_all.reshape((high * high, 2 * zs) + meta.shape)

    length = zs * tok_rows
    heads = query_width // HEAD
    groups = kv_width // HEAD
    places = lax.rem(z + zs - jnp.arange(zs, dtype=jnp.int32), zs)
    cosine, sine = rotary_tables(length)
    qkv = None
    for j, piece in enumerate(seq_pieces):
        qkv = project(places[j], piece, w_in, cosine, sine, query_width + kv_width, qkv)
    attended, lse = attend(qkv, heads, groups)
    attended = attended.reshape(zs, tok_rows, query_width)
    attended, grad_first = tie(attended, grad_first)
    attended_own = exchange(attended, "z")
    mask_all, scale_all = chosen_tables(
        meta_all[:, :, :pick_count], meta_all[:, :, pick_count:], expert_count
    )
    side = 2 * high
    numbers = []
    for dy, dx in ((0, 0), (0, 1), (1, 0), (1, 1)):
        chip = (yh * 2 + (yl ^ dy)) * side + xh * 2 + (xl ^ dx)
        numbers.append((chip * 2 + core) * zs + z)
    mine = jnp.stack(numbers)[None, :] == jnp.arange(expert_count)[:, None]
    mask_mine = jnp.any(mine[:, :, None] & mask_all[:, :, :, None], axis=2)
    earlier = (jnp.arange(tok_rows)[:, None] < jnp.arange(tok_rows)[None, :]).astype(BF16)
    rank = jnp.einsum(
        "gpes,st->gpet", mask_mine.astype(BF16), earlier, preferred_element_type=F32
    )
    place = jnp.where(mask_mine, rank, -1.0)
    place_of_token = jnp.where(
        mask_mine, rank + (jnp.arange(4, dtype=F32) * slots)[:, None], -1.0
    ).swapaxes(2, 3)

    tables = (place, place_of_token, mask_all.astype(F32), scale_all)
    attended_own, tables = tie(attended_own, tables)
    place, place_of_token, mask_low, scale_all = tables
    middle, normed_two_low = branch_norm(jnp.arange(zs), attended_own, w_out, hidden_in, norm2_gain)

    rows_pieces = [normed_two_low, line_step(normed_two_low, zs)]
    rows_pieces[1], *weights_d = tie(rows_pieces[1], *take_pieces(*weights_x, *weights_y))
    for step in range(3):
        weights_d[step] = swap(weights_d[step], "yl")
        weights_d[3 + step] = swap(weights_d[3 + step], "xl")
        if step < 2:
            rows_pieces.append(line_step(rows_pieces[-1], zs))
            rows_pieces[-1], weights_d[step], weights_d[3 + step] = tie(
                rows_pieces[-1], weights_d[step], weights_d[3 + step]
            )
    grad_first, rows_pieces[-1] = tie(grad_first, rows_pieces[-1])
    grad_next = line_step(grad_first, zs)
    rows_pieces = rows_pieces + [swap(piece, "core") for piece in rows_pieces]
    rows_pieces = spread(rows_pieces, sizes)
    *by_slot, gates = experts_forward(
        0,
        rows_pieces,
        place,
        (mask_low, scale_all, mine.astype(F32), w_router.T),
        (weights_o, weights_x, weights_y),
        slots,
    )
    by_slot[0], grad_next = tie(by_slot[0], grad_next)
    grad_last = line_step(grad_next, zs)
    out_slots, *saved = experts_forward(
        3, rows_pieces, place, (gates,), (weights_d,), slots, by_slot
    )
    out_order = ((0, 0), (0, 1), (0, 2), (0, 3))
    out_parts = [out_slots]

    def out_other(start, count):
        return combine(place_of_token, out_parts, out_order, slots, 1, start, count)

    def out_own(start, count, other):
        return only_own(
            combine(place_of_token, out_parts, out_order, slots, 0, start, count, other), sizes
        )

    out_near, out_far = out_other(1, 1), out_other(2, zs - 1)
    out_near, out_far, grad_last = swap(out_near, "core"), *tie(out_far, grad_last)
    out_far = swap(out_far, "core")
    (term,) = out_own(1, 1, out_near)
    grad_pieces = [grad_low, grad_first, grad_next, grad_last]
    grad_pieces = grad_pieces + [swap(piece, "core") for piece in grad_pieces]
    term, grad_pieces = tie(term, grad_pieces)
    grad_pieces = spread(grad_pieces, sizes)
    out_run = line_step(term, zs)
    rows_dx, gate_dx, *grads = experts_backward(
        3, grad_pieces, place, gates, saved, (weights_d, weights_x), slots
    )
    gd, gx = grads[:6], grads[6:]
    gd[0], gd[3] = swap(gd[0], "yl"), swap(gd[3], "xl")
    gd[1], gd[4] = swap(gd[1], "yl"), swap(gd[4], "xl")
    out_far, out_run, rows_dx = tie(out_far, out_run, rows_dx)
    out_terms = out_own(2, zs - 1, out_far)
    out_run, gates = tie(out_terms[0] + out_run, gates)
    out_run = line_step(out_run, zs)
    rows_yo, gate_yo, *grads = experts_backward(
        2, grad_pieces, place, gates, saved, (weights_y, weights_o), slots
    )
    gy, go = grads[:6], grads[6:]
    out_run, rows_yo, gd[0], gd[3], gd[1], gd[4] = tie(
        out_terms[1] + out_run, rows_yo, gd[0], gd[3], gd[1], gd[4]
    )
    gd[2], gd[5] = swap(gd[2], "yl"), swap(gd[5], "xl")
    moe_parts, moe_order = [rows_dx, rows_yo], ((1, 1), (0, 1), (1, 0), (0, 0))
    more = ((gate_dx, gate_yo), mine.astype(F32))

    def moe_sums(start, count):
        other = combine(place_of_token, moe_parts, moe_order, slots, 1, start, count, None, *more)
        other = swap(other, "core")
        return only_own(
            combine(place_of_token, moe_parts, moe_order, slots, 0, start, count, other, *more),
            sizes,
        )

    (term,) = moe_sums(1, 1)
    term, *moe_parts = tie(term, *moe_parts)
    moe_run = line_step(term, zs)
    moe_terms = moe_sums(2, zs - 1)
    moe_run, gd[2], gd[5] = tie(moe_terms[0] + moe_run, gd[2], gd[5])
    gx[3], gy[0] = swap(gx[3], "xl"), swap(gy[0], "yl")
    moe_run = line_step(moe_run, zs)
    moe_run, gx[3], gy[0] = tie(moe_terms[1] + moe_run, gx[3], gy[0])
    gx[4], gy[1] = swap(gx[4], "xl"), swap(gy[1], "yl")
    moe_run = line_step(moe_run, zs)

    mask_own, scale_own = chosen_tables(meta[:pick_count], meta[pick_count:], expert_count)
    logits_own = dot(w_router, normed_two_low, ((0,), (1,)))
    prob_own = masked_softmax(logits_own, mask_own, 0)
    unit = max(8, dp_count * zs * 128 // math.gcd(model_width, dp_count * zs * 128))
    sum_rows = -(-(expert_count + 2) // unit) * unit
    prob_own, scale_own, moe_terms[1] = tie(prob_own, scale_own, moe_terms[1])
    for i in range(3):
        gx[i], gy[3 + i] = gx[i] + gd[i], gy[3 + i] + gd[3 + i]
    moe_run, gx[4], gy[1], *both = tie(moe_run, gx[4], gy[1], *gx[:3], *gy[3:])
    gx[:3], gy[3:] = both[:3], both[3:]
    gx[5], gy[2] = swap(gx[5], "xl"), swap(gy[2], "yl")
    gx[0], gy[3] = swap(gx[0], "xl"), swap(gy[3], "yl")
    grad_middle, grad_branch, grad_attended, early_sums = moe_back(
        jnp.arange(zs),
        sum_rows,
        moe_terms[2],
        moe_run,
        prob_own,
        scale_own,
        w_router.T,
        normed_two_low,
        middle,
        norm2_gain,
        out_grad,
        w_out,
    )

    attended_rows = attended_own.transpose(1, 0, 2).reshape(tok_rows, zs * query_width)
    grad_w_out = dot(grad_branch, attended_rows, ((0,), (0,))).astype(BF16)
    shard_out = lax.psum_scatter(grad_w_out, ROWS, scatter_dimension=0, tiled=True)
    grad_attended = exchange(grad_attended, "z")
    out_run, grad_attended, _, gx[5], gy[2] = tie(
        out_run, grad_attended, grad_w_out, gx[5], gy[2]
    )
    gx[1], gy[4] = swap(gx[1], "xl"), swap(gy[4], "yl")
    out_run = line_step(out_run, zs)
    grad_proj = attend_back(
        qkv, lse, grad_attended.reshape(length, query_width), cosine, sine, heads, groups
    )
    out_run, grad_proj = tie(out_run, grad_proj)
    terms = [
        dot(g, w_in, ((1,), (1,))).astype(BF16)
        for g in behind(grad_proj.reshape(zs, tok_rows, -1), zs)
    ]
    terms[1], grad_proj = tie(terms[1], grad_proj)
    run = line_step(terms[1], zs)
    grad_w_in, gain_rows = project_back(places, seq_pieces, grad_proj, w_in)
    run, grad_w_in, gain_rows, gx[0], gy[3], gx[1], gy[4], *terms = tie(
        run, grad_w_in, gain_rows, gx[0], gy[3], gx[1], gy[4], *terms
    )
    gx[2], gy[5] = swap(gx[2], "xl"), swap(gy[5], "yl")
    run = line_step(terms[2] + run, zs)
    shard_out, grad_w_in = tie(shard_out, grad_w_in)
    shard_in = lax.psum_scatter(grad_w_in, ROWS, scatter_dimension=0, tiled=True).astype(F32)

    sums = lax.dynamic_update_slice(early_sums, gain_rows[:1], (expert_count + 1, 0))
    sums = sums.reshape(dp_count * zs, -1, 128)
    sums = jnp.sum(exchange(sums, ALL), axis=0)
    output = middle + RESIDUAL_SCALE * (out_terms[2].astype(F32) + out_run.astype(F32))
    run, gx[2], gy[5], output = tie(terms[3] + run, gx[2], gy[5], output)
    run = line_step(run, zs)
    sums = share(sums, ALL, dp_count * zs).reshape(sum_rows, model_width)
    grad_w_gate_up, grad_w_down = collect(
        [(go[i], gx[i], gy[i]) for i in range(6)], model_width
    )

    shard_out = shard_out.reshape(-1, zs, query_width).transpose(1, 0, 2)
    chunks = behind(shard_out, zs)
    for step in range(1, zs):
        chunks[step] = lax.ppermute(
            chunks[step], "z", [(i, (i + zs - step) % zs) for i in range(zs)]
        )

    run, grad_w_gate_up, grad_w_down, *chunks = tie(run, grad_w_gate_up, grad_w_down, *chunks)
    grad_hidden = finish(terms[0], run, hidden_in, norm1_gain, grad_middle)
    shard_output = sum(chunk.astype(F32) for chunk in chunks).T
    shard_query = shard_in[:, :query_width]
    shard_keyvalue = jnp.stack(
        [
            shard_in[:, query_width : query_width + kv_width],
            shard_in[:, query_width + kv_width :],
        ]
    )
    return (
        output,
        grad_hidden,
        sums[expert_count + 1] / norm1_gain,
        shard_query,
        shard_keyvalue,
        shard_output,
        sums[expert_count],
        sums[:expert_count].T,
        grad_w_gate_up,
        grad_w_down,
    )


def solution(mesh):
    high = math.isqrt(mesh.shape["dp"] // 2) // 2
    zs = mesh.shape["tensor"]
    inner = Mesh(mesh.devices.reshape(high, 2, high, 2, 2, zs), ALL)
    sizes = dict(inner.shape)
    in_specs = (
        P(ALL, None),
        P(),
        P(ROWS, "z"),
        P(None, ROWS, "z"),
        P("z", ROWS),
        P(),
        P(),
        P(ALL, None, None, None),
        P(ALL, None, None),
        P(ALL, None),
        P(ALL, None),
        P(ALL, None),
    )
    out_specs = (
        P(ALL, None),
        P(ALL, None),
        P(),
        P(ROWS, "z"),
        P(None, ROWS, "z"),
        P("z", ROWS),
        P(),
        P(),
        P(ALL, None, None, None),
        P(ALL, None, None),
    )
    return jax.shard_map(
        functools.partial(local, sizes),
        mesh=inner,
        in_specs=in_specs,
        out_specs=out_specs,
        check_vma=False,
    )
```

```python
import functools
import math

import jax
import jax.numpy as jnp
from jax import lax
from jax.experimental import pallas as pl
from jax.experimental.pallas import tpu as pltpu
from jax.sharding import Mesh
from jax.sharding import PartitionSpec as P

HEAD = 64
EPSILON = 1e-06
ATTN_SCALE = 0.015625
RESIDUAL_SCALE = 0.22
THETA = 10000.0
QUERY_BLOCK = 256
F32 = jnp.float32
BF16 = jnp.bfloat16
SWAP = [(0, 1), (1, 0)]
VMEM_LIMIT = 56 * 1024 * 1024


def lasts(microseconds):
    return pl.CostEstimate(
        flops=int(microseconds * 1.15e9), bytes_accessed=1, transcendentals=0
    )


ROWS = ("yh", "yl", "xh", "xl", "core")
ALL = ROWS + ("z",)


def swap(value, axis):
    return lax.ppermute(value, axis, SWAP)


def dot(a, b, dims):
    return lax.dot_general(a, b, (dims, ((), ())), preferred_element_type=F32)


def rotary_tables(length):
    half_width = HEAD // 2
    frequency = THETA ** (-2.0 * jnp.arange(half_width, dtype=F32) / HEAD)
    angles = jnp.arange(length, dtype=F32)[:, None] * frequency[None, :]
    cosine, sine = jnp.cos(angles), jnp.sin(angles)
    return jnp.tile(cosine, (1, 4)), jnp.tile(jnp.concatenate([-sine, sine], axis=1), (1, 2))


def line_step(value, size):
    return lax.ppermute(value, "z", [(i, (i + 1) % size) for i in range(size)])


def line_pieces(value, size, count=None):
    pieces = [value]
    for _ in range((count or size) - 1):
        pieces.append(line_step(pieces[-1], size))
    return pieces


def line_order(pieces):
    size = len(pieces)
    z = lax.axis_index("z")
    whole = jnp.zeros((size,) + pieces[0].shape, pieces[0].dtype)
    for step, piece in enumerate(pieces):
        whole = lax.dynamic_update_index_in_dim(whole, piece, lax.rem(z + size - step, size), 0)
    return whole


def tie(*values):
    return lax.optimization_barrier(values)


def behind(value, size):
    z = lax.axis_index("z")
    return [
        lax.dynamic_index_in_dim(value, lax.rem(z + size - j, size), 0, False) for j in range(size)
    ]


def spread(pieces, sizes):
    if sizes["yh"] == 1:
        return [piece[None] for piece in pieces]
    return [lax.all_gather(piece, ("yh", "xh"), axis=0, tiled=False) for piece in pieces]


def exchange(value, axes):
    return lax.all_to_all(value, axes, split_axis=0, concat_axis=0, tiled=True)


def share(value, axes, count):
    return exchange(jnp.broadcast_to(value[None], (count,) + value.shape), axes)


def one_hot(place_row, slots):
    rank = lax.broadcasted_iota(jnp.int32, (slots, place_row.shape[1]), 0).astype(F32)
    return jnp.where(rank == place_row, 1.0, 0.0)


def load_weights(sources, gate_up, down, sem):
    step, inner = pl.program_id(0), pl.program_id(1)
    block, half = gate_up.shape[2] // 2, gate_up.shape[3] // 2

    def pairs(k):
        slot = k % 2
        if len(sources[k]) == 2:
            yield sources[k][0], gate_up.at[slot]
            yield sources[k][1], down.at[slot]
            return
        for n, ref in enumerate(sources[k]):
            which, piece = divmod(n, 3)
            if piece == 2:
                yield ref, down.at[slot, pl.ds(which * half, half)]
            else:
                yield ref, gate_up.at[slot, which, pl.ds(piece * block, block)]

    def copies(k):
        for n, (source, target) in enumerate(pairs(k)):
            yield pltpu.make_async_copy(source, target, sem.at[k % 2, n])

    @pl.when((step == 0) & (inner == 0))
    def _():
        for copy in copies(0):
            copy.start()

    for k in range(len(sources)):

        @pl.when((step == k) & (inner == 0))
        def _(k=k):
            for copy in copies(k):
                copy.wait()
            if k + 1 < len(sources):
                for copy in copies(k + 1):
                    copy.start()


def sources_of(refs):
    sources, refs = [], list(refs)
    while refs:
        count = 2 if len(refs[0].shape) == 3 else 6
        sources.append(refs[:count])
        refs = refs[count:]
    return sources


def weight_scratch(width, hidden):
    return [
        pltpu.VMEM((2, 2, width, hidden), BF16),
        pltpu.VMEM((2, hidden, width), BF16),
        pltpu.SemaphoreType.DMA((2, 6)),
    ]


def slot_gates_of(picks, gate_ref, group, number):
    return jnp.concatenate(
        [
            jnp.sum(pick * gate_ref[group, j, pl.ds(number, 1), :], axis=1, keepdims=True)
            for j, pick in enumerate(picks)
        ],
        axis=0,
    )


def forward_kernel(pieces, slots, first, given, *refs):
    x_refs, refs = refs[:pieces], refs[pieces:]
    place_ref, refs = refs[0], refs[1:]
    if first == 0:
        mask_ref, scale_ref, mine_ref, router_ref = refs[:4]
        gate_ref = refs[4 + given + 5]
        weights, outs = sources_of(refs[4 : 4 + given]), refs[4 + given : 4 + given + 5]
    else:
        gate_ref = refs[0]
        weights, outs = sources_of(refs[6 : 6 + given]), refs[6 + given : 6 + given + 5]
    y_ref, xs_ref, dg_ref, du_ref, act_ref = outs
    gate_up, down, sem = refs[-3:]
    step, group = pl.program_id(0), pl.program_id(1)
    number = first + step
    load_weights(weights, gate_up, down, sem)

    if first == 0:

        @pl.when(step == 0)
        def _():
            for j in range(pieces):
                mask = mask_ref[group, j]
                logits = dot(router_ref[...], x_refs[j][0], ((1,), (1,)))
                logits = jnp.where(mask > 0.0, logits, -1e30)
                top = jnp.max(logits, axis=0, keepdims=True)
                exponent = jnp.where(mask > 0.0, jnp.exp(logits - top), 0.0)
                gates = exponent / jnp.sum(exponent, axis=0, keepdims=True) * scale_ref[group, j]
                for e in range(gate_ref.shape[2]):
                    gate_ref[group, j, e : e + 1] = jnp.sum(
                        gates * mine_ref[:, e : e + 1], axis=0, keepdims=True
                    )

    picks = [one_hot(place_ref[group, j, pl.ds(number, 1), :], slots) for j in range(pieces)]
    for j, pick in enumerate(picks):
        rows = dot(pick.astype(BF16), x_refs[j][0], ((1,), (0,)))
        xs_ref[0, j * slots : (j + 1) * slots] = rows.astype(BF16)
    slot_gate = slot_gates_of(picks, gate_ref, group, number)
    now = lax.rem(step, 2)
    x = xs_ref[0]
    gate = dot(x, gate_up[now, 0], ((1,), (0,)))
    up = dot(x, gate_up[now, 1], ((1,), (0,)))
    sigmoid = 1.0 / (1.0 + jnp.exp(-gate))
    silu = gate * sigmoid
    active = (silu * up).astype(BF16)
    act_ref[0] = active
    dg_ref[0] = (up * sigmoid * (1.0 + gate * (1.0 - sigmoid))).astype(BF16)
    du_ref[0] = silu.astype(BF16)
    weighted = (active.astype(F32) * slot_gate).astype(BF16)
    y_ref[0] = dot(weighted, down[now], ((1,), (0,))).astype(BF16)


def backward_kernel(pieces, slots, first, given, *refs):
    g_refs, refs = refs[:pieces], refs[pieces:]
    place_ref, gate_ref, xs_ref, dg_ref, du_ref, act_ref = refs[:6]
    weights, refs = sources_of(refs[6 : 6 + given]), refs[6 + given :]
    experts = len(weights)
    rows_ref, through_ref = refs[:2]
    results = [refs[2 + 6 * k : 8 + 6 * k] for k in range(experts)]
    gate_up, down, sem, gs_ref, stage, stage_down, out_sem = refs[2 + 6 * experts : 9 + 6 * experts]
    sums = refs[9 + 6 * experts :]
    step, group = pl.program_id(0), pl.program_id(1)
    number = first - 2 * step
    load_weights(weights, gate_up, down, sem)
    width = g_refs[0].shape[-1]
    half = down.shape[1] // 2
    now = lax.rem(step, 2)
    last = pl.num_programs(1) - 1

    def stores(k):
        block = width // 2
        for n, ref in enumerate(results[k]):
            which, piece = divmod(n, 3)
            source = stage_down.at[pl.ds(which * half, half)]
            if piece < 2:
                source = stage.at[which, pl.ds(piece * block, block)]
            yield pltpu.make_async_copy(source, ref, out_sem.at[n])

    picks = [one_hot(place_ref[group, j, pl.ds(number, 1), :], slots) for j in range(pieces)]
    for j, pick in enumerate(picks):
        rows = dot(pick.astype(BF16), g_refs[j][0], ((1,), (0,)))
        gs_ref[j * slots : (j + 1) * slots] = rows.astype(BF16)
    slot_gate = slot_gates_of(picks, gate_ref, group, number) * RESIDUAL_SCALE
    grad_active = dot(gs_ref[...], down[now], ((1,), (1,)))
    active = act_ref[0].astype(F32)
    through = jnp.sum(grad_active * active, axis=1, keepdims=True) * RESIDUAL_SCALE
    for j, pick in enumerate(picks):
        through_ref[0, 0, j : j + 1] = jnp.sum(
            pick * through[j * slots : (j + 1) * slots], axis=0, keepdims=True
        )
    grad_active = grad_active * slot_gate
    grad_gate = (grad_active * dg_ref[0].astype(F32)).astype(BF16)
    grad_up = (grad_active * du_ref[0].astype(F32)).astype(BF16)
    rows = dot(grad_gate, gate_up[now, 0], ((1,), (1,)))
    rows = rows + dot(grad_up, gate_up[now, 1], ((1,), (1,)))
    rows_ref[0] = rows.astype(BF16)
    weighted = (active * slot_gate).astype(BF16)

    for k in range(1, experts):

        @pl.when((step == k) & (group == last))
        def _(k=k):
            for copy in stores(k - 1):
                copy.wait()

    def add(target, total, left, right):
        part = dot(left, right, ((0,), (0,)))
        if total is None:
            target[...] = part.astype(BF16)
            return

        @pl.when(group == 0)
        def _():
            total[...] = part

        @pl.when(group > 0)
        def _():
            total[...] += part

        @pl.when(group == last)
        def _():
            target[...] = total[...].astype(BF16)

    x = xs_ref[0]
    totals = [sums[0].at[0], sums[0].at[1], sums[1]] if sums else [None] * 3
    add(stage.at[0], totals[0], x, grad_gate)
    add(stage.at[1], totals[1], x, grad_up)
    add(stage_down, totals[2], weighted, gs_ref[...])
    for k in range(experts):

        @pl.when((step == k) & (group == last))
        def _(k=k):
            for copy in stores(k):
                copy.start()
            if k == experts - 1:
                for copy in stores(k):
                    copy.wait()


def resident(arrays):
    return [
        pl.BlockSpec(a.shape, lambda e, c, n=a.ndim: (0,) * n, pipeline_mode=pl.Buffered(1))
        for a in arrays
    ]


def piece_spec(piece):
    groups, tokens, width = piece.shape
    mode = pl.Buffered(1) if groups == 1 else None
    return pl.BlockSpec((1, tokens, width), lambda e, c: (c, 0, 0), pipeline_mode=mode)


def experts_forward(first, x_pieces, place, tables, weights, slots, before=None):
    pieces = len(x_pieces)
    groups, tokens, width = x_pieces[0].shape
    hidden = weights[0][0].shape[-1]
    rows = pieces * slots
    experts = place.shape[2]
    anywhere = pl.BlockSpec(memory_space=pl.ANY)
    flat = [array for pair in weights for array in pair]
    before = list(before or [])

    def by_slot(n):
        return pl.BlockSpec((1, rows, n), lambda e, c: (first + e, c, 0))

    gate_shape = (groups, pieces, experts, tokens)
    widths = (width, width, hidden, hidden, hidden)
    out_specs = [by_slot(n) for n in widths]
    out_shape = [jax.ShapeDtypeStruct((experts, groups * rows, n), BF16) for n in widths]
    if first == 0:
        out_specs.append(pl.BlockSpec(gate_shape, lambda e, c: (0, 0, 0, 0)))
        out_shape.append(jax.ShapeDtypeStruct(gate_shape, F32))
    operands = [*x_pieces, place, *tables]
    return pl.pallas_call(
        functools.partial(forward_kernel, pieces, slots, first, len(flat)),
        grid=(len(weights), groups),
        in_specs=[piece_spec(p) for p in x_pieces]
        + resident([place, *tables])
        + [anywhere] * (len(before) + len(flat)),
        out_specs=out_specs,
        out_shape=out_shape,
        input_output_aliases={len(operands) + n: n for n in range(len(before))},
        scratch_shapes=weight_scratch(width, hidden),
        compiler_params=pltpu.CompilerParams(vmem_limit_bytes=VMEM_LIMIT),
        cost_estimate=lasts(8.0 * len(weights)),
        name="experts_forward",
    )(*operands, *before, *flat)


def experts_backward(first, g_pieces, place, gates, saved, weights, slots):
    pieces = len(g_pieces)
    groups, tokens, width = g_pieces[0].shape
    experts = len(weights)
    hidden = weights[0][0].shape[-1]
    rows = pieces * slots
    flat = [array for pair in weights for array in pair]

    def by_slot(n):
        return pl.BlockSpec((1, rows, n), lambda e, c: (first - 2 * e, c, 0))

    anywhere = pl.BlockSpec(memory_space=pl.ANY)
    block = jax.ShapeDtypeStruct((width // 2, hidden), BF16)
    return pl.pallas_call(
        functools.partial(backward_kernel, pieces, slots, first, len(flat)),
        grid=(experts, groups),
        in_specs=[piece_spec(p) for p in g_pieces]
        + resident([place, gates])
        + [by_slot(width)]
        + [by_slot(hidden)] * 3
        + [anywhere] * len(flat),
        out_specs=[
            pl.BlockSpec((1, rows, width), lambda e, c: (e, c, 0)),
            pl.BlockSpec((1, 1, pieces, tokens), lambda e, c: (e, c, 0, 0)),
        ]
        + [anywhere] * (6 * experts),
        out_shape=[
            jax.ShapeDtypeStruct((experts, groups * rows, width), BF16),
            jax.ShapeDtypeStruct((experts, groups, pieces, tokens), F32),
        ]
        + [block, block, jax.ShapeDtypeStruct((hidden // 2, width), BF16)] * (2 * experts),
        scratch_shapes=weight_scratch(width, hidden)
        + [
            pltpu.VMEM((rows, width), BF16),
            pltpu.VMEM((2, width, hidden), BF16),
            pltpu.VMEM((hidden, width), BF16),
            pltpu.SemaphoreType.DMA((6,)),
        ]
        + (
            [pltpu.VMEM((2, width, hidden), F32), pltpu.VMEM((hidden, width), F32)]
            if groups > 1
            else []
        ),
        compiler_params=pltpu.CompilerParams(vmem_limit_bytes=VMEM_LIMIT),
        cost_estimate=lasts(14.5 * experts),
        name="experts_backward",
    )(*g_pieces, place, gates, *saved, *flat)


def extra_rows(expert_count, tokens, width):
    return 16 * -(-(-(-2 * expert_count // 16)) // (width // tokens))


def extra_places(expert_count, tokens, width):
    across = width // tokens
    for block in range(-(-2 * expert_count // 16)):
        yield block, 16 * (block // across), tokens * (block % across)


def combine_kernel(order, slots, extra, pieces, place_ref, *refs):
    parts = 1 + max(which for which, _ in order)
    experts = len(order)
    rows_refs, refs = refs[:parts], refs[parts:]
    if extra:
        through_refs, mine_ref, refs = refs[:parts], refs[parts], refs[parts + 1 :]
    step = pl.program_id(0)
    tokens = place_ref.shape[1]
    lane = lax.broadcasted_iota(jnp.int32, (tokens, experts * slots), 1).astype(F32)
    hit = lane == place_ref[0, :, 0:1]
    for e in range(1, experts):
        hit = hit | (lane == place_ref[0, :, e : e + 1])
    pick = jnp.where(hit, 1.0, 0.0).astype(BF16)
    rows = jnp.concatenate([rows_refs[which][k] for which, k in order], axis=0)
    out = dot(pick, rows, ((1,), (0,)))
    width = out.shape[1]
    more = None
    if extra:
        dense = 0.0
        for e, (which, k) in enumerate(order):
            dense = dense + mine_ref[:, e : e + 1] * through_refs[which][k, 0]
        high = dense.astype(BF16).astype(F32)
        both = jnp.concatenate([high, dense - high], axis=0)
        across = width // tokens
        lines = []
        for start in range(0, both.shape[0], 16 * across):
            line = [both[i : i + 16] for i in range(start, min(start + 16 * across, both.shape[0]), 16)]
            line += [jnp.zeros((16, tokens), F32)] * (across - len(line))
            lines.append(jnp.concatenate(line, axis=1))
        more = jnp.concatenate(lines, axis=0)

    def store(ref):
        if not pieces:
            ref[0, :tokens] = out.astype(BF16)
            if extra:
                ref[0, tokens:] = more.astype(BF16)
            return
        ref[0, :tokens] = (out + refs[0][0, :tokens].astype(F32)).astype(BF16)
        if extra:
            ref[0, tokens:] = (more + refs[0][0, tokens:].astype(F32)).astype(BF16)

    if not pieces:
        store(refs[0])
        return
    for j in range(pieces):

        @pl.when(lax.rem(step, pieces) == j)
        def _(j=j):
            store(refs[1 + j])


def combine(place, parts, order, slots, half, start, count, other=None, through=None, mine=None):
    groups, pieces, tokens, experts = place.shape
    column = pieces // 2
    width = parts[0].shape[-1]
    extra = 0 if through is None else extra_rows(mine.shape[0], tokens, width)

    def at(i):
        return (i // count) * pieces + half * column + (start + i % count) % column

    in_specs = [pl.BlockSpec((1, tokens, experts), lambda i: (at(i), 0, 0))]
    in_specs += [pl.BlockSpec((p.shape[0], slots, width), lambda i: (0, at(i), 0)) for p in parts]
    operands = [place.reshape(groups * pieces, tokens, experts), *parts]
    if extra:
        in_specs += [
            pl.BlockSpec((t.shape[0], 1, 1, tokens), lambda i: (0, at(i), 0, 0)) for t in through
        ]
        in_specs.append(pl.BlockSpec(mine.shape, lambda i: (0, 0)))
        operands += [t.reshape(t.shape[0], groups * pieces, 1, tokens) for t in through] + [mine]
    rows = tokens + extra
    by_step = pl.BlockSpec((1, rows, width), lambda i: (i, 0, 0))
    if other is None:
        out_specs, out_shape = by_step, jax.ShapeDtypeStruct((groups * count, rows, width), BF16)
    else:
        in_specs.append(by_step)
        operands.append(other)
        out_specs = [pl.BlockSpec((1, rows, width), lambda i: (i // count, 0, 0))] * count
        out_shape = [jax.ShapeDtypeStruct((groups, rows, width), BF16)] * count
    return pl.pallas_call(
        functools.partial(combine_kernel, order, slots, extra, 0 if other is None else count),
        grid=(groups * count,),
        in_specs=in_specs,
        out_specs=out_specs,
        out_shape=out_shape,
        compiler_params=pltpu.CompilerParams(vmem_limit_bytes=VMEM_LIMIT),
        cost_estimate=lasts(0.1),
        name="combine",
    )(*operands)


def only_own(terms, sizes):
    if sizes["yh"] == 1:
        return [term[0] for term in terms]
    return [
        lax.psum_scatter(term, ("yh", "xh"), scatter_dimension=0, tiled=True)[0] for term in terms
    ]


def packed_specs(width, hidden):
    block = width // 2
    return (
        pl.BlockSpec((1, 1, block, hidden), lambda h, i: (0, h, jnp.minimum(i, 1), 0)),
        pl.BlockSpec((1, hidden // 2, width), lambda h, i: (0, h, 0)),
    )


def take_kernel(gate_ref, down_a_ref, up_ref, down_b_ref, *out_refs):
    step = pl.program_id(0)
    for n in (0, 1):

        @pl.when(step == n)
        def _(n=n):
            out_refs[n][...] = gate_ref[0]
            out_refs[3 + n][...] = up_ref[0]

    @pl.when(step == 2)
    def _():
        out_refs[2][...] = down_a_ref[...]
        out_refs[5][...] = down_b_ref[...]


def take_pieces(gate_up_x, down_x, gate_up_y, down_y):
    _, width, hidden = gate_up_x.shape
    block, half = width // 2, hidden // 2

    def specs(which):
        return [
            pl.BlockSpec((1, block, hidden), lambda i: (which, jnp.minimum(i, 1), 0)),
            pl.BlockSpec((half, width), lambda i: (which, 0)),
        ]

    shapes = [(block, hidden), (block, hidden), (half, width)] * 2
    return pl.pallas_call(
        take_kernel,
        grid=(3,),
        in_specs=specs(0) + specs(1),
        out_specs=[pl.BlockSpec(shape, lambda i: (0, 0)) for shape in shapes],
        out_shape=[jax.ShapeDtypeStruct(shape, BF16) for shape in shapes],
        compiler_params=pltpu.CompilerParams(vmem_limit_bytes=VMEM_LIMIT),
        cost_estimate=lasts(4.0),
        name="take_pieces",
    )(gate_up_x, down_x, gate_up_y, down_y)


def collect_kernel(*refs):
    gate_up_ref, down_ref, wide, deep, sem = refs[-5:]
    step = pl.program_id(0) * 3 + pl.program_id(1)

    def slot(n):
        return deep.at[n // 3] if n % 3 == 2 else wide.at[n % 3]

    def copies(n):
        for k in range(3):
            yield pltpu.make_async_copy(refs[3 * n + k], slot(n).at[k], sem.at[n, k])

    @pl.when(step == 0)
    def _():
        for n in (0, 1, 2, 5):
            for copy in copies(n):
                copy.start()

    for n in range(6):

        @pl.when(step == n)
        def _(n=n):
            for copy in copies(n):
                copy.wait()
            here = slot(n)
            total = here[0].astype(F32) + here[1].astype(F32) + here[2].astype(F32)
            if n % 3 < 2:
                gate_up_ref[0, 0] = total
            else:
                down_ref[0] = total
            if n < 2:
                for copy in copies(n + 3):
                    copy.start()


def collect(pieces, width):
    hidden = pieces[0][0].shape[1]
    gate_up_spec, down_spec = packed_specs(width, hidden)
    return pl.pallas_call(
        collect_kernel,
        grid=(2, 3),
        in_specs=[pl.BlockSpec(memory_space=pl.ANY)] * 18,
        out_specs=[gate_up_spec, down_spec],
        out_shape=[
            jax.ShapeDtypeStruct((1, 2, width, hidden), F32),
            jax.ShapeDtypeStruct((1, hidden, width), F32),
        ],
        scratch_shapes=[
            pltpu.VMEM((2, 3, width // 2, hidden), BF16),
            pltpu.VMEM((2, 3, hidden // 2, width), BF16),
            pltpu.SemaphoreType.DMA((6, 3)),
        ],
        compiler_params=pltpu.CompilerParams(vmem_limit_bytes=VMEM_LIMIT),
        cost_estimate=lasts(9.5),
        name="collect",
    )(*[array for piece in pieces for array in piece])


def inverse_root(values):
    return lax.rsqrt(jnp.mean(values * values, axis=-1, keepdims=True) + EPSILON)


def branch_kernel(place_ref, att_ref, w_ref, hidden_ref, gain_ref, middle_ref, low_ref):
    step = pl.program_id(0)
    weights = w_ref[:, 0].reshape(hidden_ref.shape[1], w_ref.shape[-1])
    part = RESIDUAL_SCALE * dot(att_ref[0], weights, ((1,), (1,)))

    @pl.when(step == 0)
    def _():
        middle_ref[...] = hidden_ref[...] + part

    @pl.when(step > 0)
    def _():
        middle_ref[...] += part

    @pl.when(step == pl.num_programs(0) - 1)
    def _():
        middle = middle_ref[...]
        low_ref[...] = (middle * inverse_root(middle) * gain_ref[...]).astype(BF16)


def out_weights_spec(weights):
    rows, _, height, columns = weights.shape
    return pl.BlockSpec((rows, 1, height, columns), lambda i, p: (0, i, 0, 0))


def branch_norm(places, attended, weights, hidden, gain):
    count, tokens, columns = attended.shape
    width = hidden.shape[1]
    return pl.pallas_call(
        branch_kernel,
        grid_spec=pltpu.PrefetchScalarGridSpec(
            num_scalar_prefetch=1,
            grid=(count,),
            in_specs=[
                pl.BlockSpec((1, tokens, columns), lambda i, p: (p[i], 0, 0)),
                out_weights_spec(weights),
                pl.BlockSpec((tokens, width), lambda i, p: (0, 0)),
                pl.BlockSpec((1, width), lambda i, p: (0, 0)),
            ],
            out_specs=[pl.BlockSpec((tokens, width), lambda i, p: (0, 0))] * 2,
        ),
        out_shape=[
            jax.ShapeDtypeStruct((tokens, width), F32),
            jax.ShapeDtypeStruct((tokens, width), BF16),
        ],
        compiler_params=pltpu.CompilerParams(vmem_limit_bytes=VMEM_LIMIT),
        cost_estimate=lasts(7.0),
        name="branch_norm",
    )(places, attended, weights, hidden, gain.reshape(1, width))


def moe_back_kernel(
    extra, place_ref, own_ref, run_ref, prob_ref, scale_ref, router_ref, low_ref, middle_ref, gain_ref, grad_ref, w_ref,
    grad_middle_ref, branch_ref, attended_ref, sums_ref,
):
    tokens = middle_ref.shape[0]

    @pl.when(pl.program_id(0) == 0)
    def _():
        experts = prob_ref.shape[0]

        def total(rows, columns=slice(None)):
            return own_ref[rows, columns].astype(F32) + run_ref[rows, columns].astype(F32)

        both = jnp.concatenate(
            [
                total(slice(tokens + row, tokens + row + 16), slice(column, column + tokens))
                for _, row, column in extra
            ],
            axis=0,
        )
        scaled = (both[:experts] + both[experts : 2 * experts]) * scale_ref[...]
        prob = prob_ref[...]
        chosen = prob * (scaled - jnp.sum(prob * scaled, axis=0, keepdims=True))
        chosen = chosen.astype(BF16)
        sums_ref[:experts] = dot(chosen, low_ref[...], ((1,), (0,)))
        grad = total(slice(0, tokens)) + dot(chosen, router_ref[...], ((0,), (0,)))
        middle = middle_ref[...]
        inverse = inverse_root(middle)
        scaled = middle * inverse
        sums_ref[experts:] = jnp.zeros((sums_ref.shape[0] - experts, middle.shape[1]), F32)
        sums_ref[experts : experts + 1] = jnp.sum(grad * scaled, axis=0, keepdims=True)
        grad = grad * gain_ref[...]
        mean = jnp.mean(grad * scaled, axis=-1, keepdims=True)
        grad = grad_ref[...] + inverse * (grad - scaled * mean)
        grad_middle_ref[...] = grad
        branch_ref[...] = (RESIDUAL_SCALE * grad).astype(BF16)

    weights = w_ref[:, 0].reshape(middle_ref.shape[1], w_ref.shape[-1])
    attended_ref[0] = dot(branch_ref[...], weights, ((1,), (0,))).astype(BF16)


def moe_back(places, rows, own, run, prob, scale, router, low, middle, gain, grad, weights):
    tokens, width = middle.shape
    experts = prob.shape[0]
    _, count, _, columns = weights.shape
    extra = list(extra_places(experts, tokens, width))
    operands = [own, run, prob, scale, router, low, middle, gain.reshape(1, width), grad]
    return pl.pallas_call(
        functools.partial(moe_back_kernel, extra),
        grid_spec=pltpu.PrefetchScalarGridSpec(
            num_scalar_prefetch=1,
            grid=(count,),
            in_specs=[pl.BlockSpec(a.shape, lambda i, p: (0, 0)) for a in operands]
            + [out_weights_spec(weights)],
            out_specs=[
                pl.BlockSpec((tokens, width), lambda i, p: (0, 0)),
                pl.BlockSpec((tokens, width), lambda i, p: (0, 0)),
                pl.BlockSpec((1, tokens, columns), lambda i, p: (p[i], 0, 0)),
                pl.BlockSpec((rows, width), lambda i, p: (0, 0)),
            ],
        ),
        out_shape=[
            jax.ShapeDtypeStruct((tokens, width), F32),
            jax.ShapeDtypeStruct((tokens, width), BF16),
            jax.ShapeDtypeStruct((count, tokens, columns), BF16),
            jax.ShapeDtypeStruct((rows, width), F32),
        ],
        compiler_params=pltpu.CompilerParams(vmem_limit_bytes=VMEM_LIMIT),
        cost_estimate=lasts(20.0),
        name="moe_back",
    )(places, *operands, weights)


def split_kernel(value_ref, first_ref, rest_ref):
    value = value_ref[...].astype(F32)
    cut, each = first_ref.shape[1], rest_ref.shape[2]
    first_ref[...] = value[:, :cut]
    for k in (0, 1):
        rest_ref[k] = value[:, cut + k * each : cut + (k + 1) * each]


def split_columns(value, cut):
    rows, columns = value.shape
    return pl.pallas_call(
        split_kernel,
        out_shape=[
            jax.ShapeDtypeStruct((rows, cut), F32),
            jax.ShapeDtypeStruct((2, rows, (columns - cut) // 2), F32),
        ],
        cost_estimate=lasts(1.0),
        name="split_columns",
    )(value)


def finish_kernel(own_ref, run_ref, hidden_ref, gain_ref, grad_ref, out_ref):
    grad = own_ref[...].astype(F32) + run_ref[...].astype(F32)
    hidden = hidden_ref[...]
    inverse = inverse_root(hidden)
    scaled = hidden * inverse
    grad = grad * gain_ref[...]
    mean = jnp.mean(grad * scaled, axis=-1, keepdims=True)
    out_ref[...] = grad_ref[...] + inverse * (grad - scaled * mean)


def finish(own, run, hidden, gain, grad):
    tokens, width = hidden.shape
    rows = pl.BlockSpec((tokens // 2, width), lambda i: (i, 0))
    return pl.pallas_call(
        finish_kernel,
        grid=(2,),
        in_specs=[rows, rows, rows, pl.BlockSpec((1, width), lambda i: (0, 0)), rows],
        out_specs=rows,
        out_shape=jax.ShapeDtypeStruct((tokens, width), F32),
        compiler_params=pltpu.CompilerParams(vmem_limit_bytes=VMEM_LIMIT),
        cost_estimate=lasts(3.5),
        name="finish",
    )(own, run, hidden, gain.reshape(1, width), grad)


def causal_mask(scores, start):
    keys, columns = scores.shape
    block = keys - start
    key = lax.broadcasted_iota(jnp.int32, (block, columns), 0)
    query = lax.rem(lax.broadcasted_iota(jnp.int32, (block, columns), 1), block)
    low = jnp.where(key <= query, scores[start:], -1e30)
    return low if start == 0 else jnp.concatenate([scores[:start], low], axis=0)


def head_rows(pair, odd):
    lane = lax.broadcasted_iota(jnp.int32, pair.shape, 1)
    return jnp.where((lane >= HEAD) == odd, pair, jnp.zeros_like(pair))


def both_halves(rows):
    return jnp.concatenate([rows, rows], axis=1)


def attend_kernel(heads, groups, block, qkv_ref, out_ref, lse_ref):
    length = qkv_ref.shape[0]
    each = heads // groups
    at_key = heads * HEAD
    at_value = at_key + groups * HEAD
    for i in range(length // block):
        start, stop = i * block, (i + 1) * block
        parts = []
        for g in range(groups):
            key = both_halves(qkv_ref[:stop, at_key + g * HEAD : at_key + (g + 1) * HEAD])
            value = qkv_ref[:stop, at_value + g * HEAD : at_value + (g + 1) * HEAD]
            query = []
            for h in range(g * each, (g + 1) * each):
                pair = qkv_ref[start:stop, h // 2 * 2 * HEAD : (h // 2 + 1) * 2 * HEAD]
                query.append(head_rows(pair, h % 2 == 1) * ATTN_SCALE)
            query = jnp.concatenate(query, axis=0).astype(BF16)
            scores = causal_mask(dot(key, query, ((1,), (1,))), start)
            top = jnp.max(scores, axis=0, keepdims=True)
            exponent = jnp.exp(scores - top)
            norm = jnp.sum(exponent, axis=0, keepdims=True)
            total = top + jnp.log(norm)
            out = dot(value, exponent.astype(BF16), ((0,), (0,))) / norm
            for k in range(each):
                columns = slice(k * block, (k + 1) * block)
                lse_ref[g * each + k : g * each + k + 1, start:stop] = total[:, columns]
                parts.append(out[:, columns])
        for pair in range(heads // 2):
            rows = jnp.concatenate(parts[2 * pair : 2 * pair + 2], axis=0)
            out_ref[start:stop, pair * 2 * HEAD : (pair + 1) * 2 * HEAD] = rows.T.astype(BF16)


def attend(qkv, heads, groups):
    length = qkv.shape[0]
    return pl.pallas_call(
        functools.partial(attend_kernel, heads, groups, min(QUERY_BLOCK, length)),
        out_shape=[
            jax.ShapeDtypeStruct((length, heads * HEAD), BF16),
            jax.ShapeDtypeStruct((8 * -(-heads // 8), length), F32),
        ],
        compiler_params=pltpu.CompilerParams(vmem_limit_bytes=VMEM_LIMIT),
        cost_estimate=lasts(8.0),
        name="attend",
    )(qkv)


def turn(values, cosine, sine, direction):
    width = values.shape[1]
    lane = lax.broadcasted_iota(jnp.int32, values.shape, 1)
    first = lax.rem(lane, HEAD) < HEAD // 2
    behind_half = pltpu.roll(values, width - HEAD // 2, 1)
    other = jnp.where(first, behind_half, pltpu.roll(values, HEAD // 2, 1))
    repeats = width // cosine.shape[1]
    cosine = jnp.concatenate([cosine] * repeats, axis=1) if repeats > 1 else cosine
    sine = jnp.concatenate([sine] * repeats, axis=1) if repeats > 1 else sine
    return values * cosine + direction * (other * sine)


def attend_back_kernel(
    heads, groups, block, qkv_ref, lse_ref, grad_ref, cos_ref, sin_ref, out_ref, key_sum, value_sum
):
    length = qkv_ref.shape[0]
    each = heads // groups
    at_key = heads * HEAD
    at_value = at_key + groups * HEAD
    for i in reversed(range(length // block)):
        start, stop = i * block, (i + 1) * block
        parts = []
        for g in range(groups):
            key = qkv_ref[:stop, at_key + g * HEAD : at_key + (g + 1) * HEAD]
            value = both_halves(qkv_ref[:stop, at_value + g * HEAD : at_value + (g + 1) * HEAD])
            query, grad, lse = [], [], []
            for h in range(g * each, (g + 1) * each):
                columns = slice(h // 2 * 2 * HEAD, (h // 2 + 1) * 2 * HEAD)
                query.append(head_rows(qkv_ref[start:stop, columns], h % 2 == 1) * ATTN_SCALE)
                grad.append(head_rows(grad_ref[start:stop, columns], h % 2 == 1))
                lse.append(lse_ref[h : h + 1, start:stop])
            query = jnp.concatenate(query, axis=0).astype(BF16)
            grad = jnp.concatenate(grad, axis=0)
            lse = jnp.concatenate(lse, axis=1)
            scores = causal_mask(dot(both_halves(key), query, ((1,), (1,))), start)
            probs = jnp.exp(scores - lse)
            grad_probs = dot(value, grad, ((1,), (1,)))
            weighted = probs * grad_probs
            delta = jnp.sum(weighted, axis=0, keepdims=True)
            grad_scores = (weighted - probs * delta).astype(BF16)
            grad_value = dot(probs.astype(BF16), grad, ((1,), (0,)))
            grad_key = dot(grad_scores, query, ((1,), (0,)))
            if stop == length:
                value_sum[g] = grad_value
                key_sum[g] = grad_key
            else:
                value_sum[g, :stop] += grad_value
                key_sum[g, :stop] += grad_key
            grad_query = dot(key, grad_scores, ((0,), (0,))) * ATTN_SCALE
            for k in range(each):
                parts.append(grad_query[:, k * block : (k + 1) * block])
        cosine, sine = cos_ref[start:stop], sin_ref[start:stop]
        for pair in range(heads // 2):
            rows = jnp.concatenate(parts[2 * pair : 2 * pair + 2], axis=0).T
            rows = turn(rows, cosine, sine, -1.0).astype(BF16)
            out_ref[start:stop, pair * 2 * HEAD : (pair + 1) * 2 * HEAD] = rows
    rows = [key_sum[g][:, :HEAD] + key_sum[g][:, HEAD:] for g in range(groups)]
    rows = turn(jnp.concatenate(rows, axis=1), cos_ref[...], sin_ref[...], -1.0)
    out_ref[:, at_key:at_value] = rows.astype(BF16)
    rows = [value_sum[g][:, :HEAD] + value_sum[g][:, HEAD:] for g in range(groups)]
    out_ref[:, at_value:] = jnp.concatenate(rows, axis=1).astype(BF16)


def attend_back(qkv, lse, grad, cosine, sine, heads, groups):
    length = qkv.shape[0]
    return pl.pallas_call(
        functools.partial(attend_back_kernel, heads, groups, min(QUERY_BLOCK, length)),
        out_shape=jax.ShapeDtypeStruct(qkv.shape, BF16),
        scratch_shapes=[pltpu.VMEM((groups, length, 2 * HEAD), F32)] * 2,
        compiler_params=pltpu.CompilerParams(vmem_limit_bytes=VMEM_LIMIT),
        cost_estimate=lasts(14.0),
        name="attend_back",
    )(qkv, lse, grad, cosine, sine)


def project_kernel(turned, place_ref, x_ref, w_ref, cos_ref, sin_ref, *refs):
    out_ref = refs[-1]
    values = dot(x_ref[...], w_ref[...], ((1,), (0,)))
    out_ref[:, :turned] = turn(values[:, :turned], cos_ref[...], sin_ref[...], 1.0).astype(BF16)
    out_ref[:, turned:] = values[:, turned:].astype(BF16)


def project(place, rows, weights, cosine, sine, turned, before=None):
    tokens, width = rows.shape
    columns = weights.shape[1]
    in_specs = [
        pl.BlockSpec((tokens, width), lambda i, p: (0, 0)),
        pl.BlockSpec((width, columns), lambda i, p: (0, 0)),
        pl.BlockSpec((tokens, cosine.shape[1]), lambda i, p: (p[0], 0)),
        pl.BlockSpec((tokens, sine.shape[1]), lambda i, p: (p[0], 0)),
    ]
    operands = [place.reshape(1), rows, weights, cosine, sine]
    if before is not None:
        in_specs.append(pl.BlockSpec(memory_space=pl.ANY))
        operands.append(before)
    return pl.pallas_call(
        functools.partial(project_kernel, turned),
        grid_spec=pltpu.PrefetchScalarGridSpec(
            num_scalar_prefetch=1,
            grid=(1,),
            in_specs=in_specs,
            out_specs=pl.BlockSpec((tokens, columns), lambda i, p: (p[0], 0)),
        ),
        out_shape=jax.ShapeDtypeStruct((cosine.shape[0], columns), BF16),
        input_output_aliases={} if before is None else {5: 0},
        compiler_params=pltpu.CompilerParams(vmem_limit_bytes=VMEM_LIMIT),
        cost_estimate=lasts(4.0),
        name="project",
    )(*operands)


def project_back_kernel(pieces, place_ref, *refs):
    x_refs = refs[:pieces]
    grad_ref, w_ref, out_ref, gain_ref = refs[pieces:]
    tokens = x_refs[0].shape[0]
    grad = 0.0
    for j in range(pieces):
        start = pl.multiple_of(place_ref[j] * tokens, tokens)
        grad = grad + dot(x_refs[j][...], grad_ref[pl.ds(start, tokens), :], ((0,), (0,)))
    out_ref[...] = grad.astype(BF16)
    ones = jnp.ones((8, w_ref.shape[1]), BF16)
    products = w_ref[...].astype(F32) * grad
    high = products.astype(BF16)
    low = (products - high.astype(F32)).astype(BF16)
    gain_ref[...] = dot(ones, high, ((1,), (1,))) + dot(ones, low, ((1,), (1,)))


def project_back(places, pieces, grad, weights):
    tokens, width = pieces[0].shape
    columns = weights.shape[1]
    cut = width // 3
    return pl.pallas_call(
        functools.partial(project_back_kernel, len(pieces)),
        grid_spec=pltpu.PrefetchScalarGridSpec(
            num_scalar_prefetch=1,
            grid=(3,),
            in_specs=[pl.BlockSpec((tokens, cut), lambda i, p: (0, i))] * len(pieces)
            + [
                pl.BlockSpec(grad.shape, lambda i, p: (0, 0)),
                pl.BlockSpec((cut, columns), lambda i, p: (i, 0)),
            ],
            out_specs=[
                pl.BlockSpec((cut, columns), lambda i, p: (i, 0)),
                pl.BlockSpec((8, cut), lambda i, p: (0, i)),
            ],
        ),
        out_shape=[
            jax.ShapeDtypeStruct((width, columns), BF16),
            jax.ShapeDtypeStruct((8, width), F32),
        ],
        compiler_params=pltpu.CompilerParams(vmem_limit_bytes=VMEM_LIMIT),
        cost_estimate=lasts(9.0),
        name="project_back",
    )(places, *pieces, grad, weights)


def chosen_tables(ids, scale, expert_count):
    lead = (1,) * (ids.ndim - 2)
    numbers = jnp.arange(expert_count, dtype=F32).reshape(lead + (1, expert_count, 1))
    hits = ids[..., :, None, :] == numbers
    mask = jnp.any(hits, axis=-3)
    return mask, jnp.sum(jnp.where(hits, scale[..., :, None, :], 0.0), axis=-3)


def masked_softmax(logits, mask, axis):
    top = jnp.max(jnp.where(mask, logits, -jnp.inf), axis=axis, keepdims=True)
    exponent = jnp.where(mask, jnp.exp(jnp.where(mask, logits - top, 0.0)), 0.0)
    return exponent / jnp.sum(exponent, axis=axis, keepdims=True)


def local(
    sizes,
    hidden_in,
    norm1_gain,
    w_query,
    w_keyvalue,
    w_output,
    norm2_gain,
    w_router,
    w_gate_up,
    w_down,
    expert_ids,
    choice_scale,
    out_grad,
):
    tok_rows, model_width = hidden_in.shape
    pick_count = expert_ids.shape[1]
    expert_count = w_router.shape[1]
    capacity = max(2, (tok_rows * pick_count * 11 + 8 * expert_count - 1) // (8 * expert_count))
    slots = -(-capacity // 16) * 16
    zs, high = sizes["z"], sizes["yh"]
    yl, xl, core, z = (lax.axis_index(a) for a in ("yl", "xl", "core", "z"))
    yh, xh = lax.axis_index("yh"), lax.axis_index("xh")

    packed = jnp.concatenate([w_query, w_keyvalue[0], w_keyvalue[1]], axis=1)
    dp_count = 8 * high * high
    w_in = lax.all_gather(packed, ROWS, axis=0, tiled=True)
    query_width = w_query.shape[1]
    kv_width = w_keyvalue.shape[2]
    normed_low = (hidden_in * inverse_root(hidden_in) * norm1_gain).astype(BF16)
    weights_o = (w_gate_up[0], w_down[0])
    weights_x = tuple(swap(w, "xl") for w in weights_o)
    weights_y = tuple(swap(w, "yl") for w in weights_o)
    w_out = share(w_output.T, "z", zs)
    seq_pieces = [normed_low, line_step(normed_low, zs)]
    w_out = lax.all_gather(w_out, ROWS, axis=0)
    seq_pieces.append(line_step(seq_pieces[1], zs))
    seq_pieces[2], w_in = tie(seq_pieces[2], w_in)
    seq_pieces.append(line_step(seq_pieces[2], zs))
    meta = jnp.concatenate([expert_ids.astype(F32).T, choice_scale.T], axis=0)
    grad_low, meta, seq_pieces[-1] = tie(out_grad.astype(BF16), meta, seq_pieces[-1])
    grad_first = line_step(grad_low, zs)
    meta_all = share(meta, ("yh", "xh", "core", "z"), high * high * 2 * zs)
    meta_all = meta_all.reshape((high * high, 2, zs) + meta.shape)
    meta_all = jnp.where(core == 1, meta_all[:, ::-1], meta_all)
    meta_all = jnp.stack(behind(jnp.moveaxis(meta_all, 2, 0), zs), axis=2)
    meta_all = meta_all.reshape((high * high, 2 * zs) + meta.shape)

    length = zs * tok_rows
    heads = query_width // HEAD
    groups = kv_width // HEAD
    places = lax.rem(z + zs - jnp.arange(zs, dtype=jnp.int32), zs)
    cosine, sine = rotary_tables(length)
    qkv = None
    for j, piece in enumerate(seq_pieces):
        qkv = project(places[j], piece, w_in, cosine, sine, query_width + kv_width, qkv)
    attended, lse = attend(qkv, heads, groups)
    attended = attended.reshape(zs, tok_rows, query_width)
    attended, grad_first = tie(attended, grad_first)
    attended_own = exchange(attended, "z")
    mask_all, scale_all = chosen_tables(
        meta_all[:, :, :pick_count], meta_all[:, :, pick_count:], expert_count
    )
    side = 2 * high
    numbers = []
    for dy, dx in ((0, 0), (0, 1), (1, 0), (1, 1)):
        chip = (yh * 2 + (yl ^ dy)) * side + xh * 2 + (xl ^ dx)
        numbers.append((chip * 2 + core) * zs + z)
    mine = jnp.stack(numbers)[None, :] == jnp.arange(expert_count)[:, None]
    mask_mine = jnp.any(mine[:, :, None] & mask_all[:, :, :, None], axis=2)
    earlier = (jnp.arange(tok_rows)[:, None] < jnp.arange(tok_rows)[None, :]).astype(BF16)
    rank = jnp.einsum(
        "gpes,st->gpet", mask_mine.astype(BF16), earlier, preferred_element_type=F32
    )
    place = jnp.where(mask_mine, rank, -1.0)
    place_of_token = jnp.where(
        mask_mine, rank + (jnp.arange(4, dtype=F32) * slots)[:, None], -1.0
    ).swapaxes(2, 3)

    tables = (place, place_of_token, mask_all.astype(F32), scale_all)
    attended_own, tables = tie(attended_own, tables)
    place, place_of_token, mask_low, scale_all = tables
    middle, normed_two_low = branch_norm(jnp.arange(zs), attended_own, w_out, hidden_in, norm2_gain)

    rows_pieces = [normed_two_low, line_step(normed_two_low, zs)]
    rows_pieces[1], *weights_d = tie(rows_pieces[1], *take_pieces(*weights_x, *weights_y))
    for step in range(3):
        weights_d[step] = swap(weights_d[step], "yl")
        weights_d[3 + step] = swap(weights_d[3 + step], "xl")
        if step < 2:
            rows_pieces.append(line_step(rows_pieces[-1], zs))
            rows_pieces[-1], weights_d[step], weights_d[3 + step] = tie(
                rows_pieces[-1], weights_d[step], weights_d[3 + step]
            )
    grad_first, rows_pieces[-1] = tie(grad_first, rows_pieces[-1])
    grad_next = line_step(grad_first, zs)
    rows_pieces = rows_pieces + [swap(piece, "core") for piece in rows_pieces]
    rows_pieces = spread(rows_pieces, sizes)
    *by_slot, gates = experts_forward(
        0,
        rows_pieces,
        place,
        (mask_low, scale_all, mine.astype(F32), w_router.T),
        (weights_o, weights_x, weights_y),
        slots,
    )
    by_slot[0], grad_next = tie(by_slot[0], grad_next)
    grad_last = line_step(grad_next, zs)
    out_slots, *saved = experts_forward(
        3, rows_pieces, place, (gates,), (weights_d,), slots, by_slot
    )
    out_order = ((0, 0), (0, 1), (0, 2), (0, 3))
    out_parts = [out_slots]

    def out_other(start, count):
        return combine(place_of_token, out_parts, out_order, slots, 1, start, count)

    def out_own(start, count, other):
        return only_own(
            combine(place_of_token, out_parts, out_order, slots, 0, start, count, other), sizes
        )

    out_near, out_far = out_other(1, 1), out_other(2, zs - 1)
    out_near, out_far, grad_last = swap(out_near, "core"), *tie(out_far, grad_last)
    out_far = swap(out_far, "core")
    (term,) = out_own(1, 1, out_near)
    grad_pieces = [grad_low, grad_first, grad_next, grad_last]
    grad_pieces = grad_pieces + [swap(piece, "core") for piece in grad_pieces]
    term, grad_pieces = tie(term, grad_pieces)
    grad_pieces = spread(grad_pieces, sizes)
    out_run = line_step(term, zs)
    rows_dx, gate_dx, *grads = experts_backward(
        3, grad_pieces, place, gates, saved, (weights_d, weights_x), slots
    )
    gd, gx = grads[:6], grads[6:]
    gd[0], gd[3] = swap(gd[0], "yl"), swap(gd[3], "xl")
    gd[1], gd[4] = swap(gd[1], "yl"), swap(gd[4], "xl")
    out_far, out_run, rows_dx = tie(out_far, out_run, rows_dx)
    out_terms = out_own(2, zs - 1, out_far)
    out_run, gates = tie(out_terms[0] + out_run, gates)
    out_run = line_step(out_run, zs)
    rows_yo, gate_yo, *grads = experts_backward(
        2, grad_pieces, place, gates, saved, (weights_y, weights_o), slots
    )
    gy, go = grads[:6], grads[6:]
    out_run, rows_yo, gd[0], gd[3], gd[1], gd[4] = tie(
        out_terms[1] + out_run, rows_yo, gd[0], gd[3], gd[1], gd[4]
    )
    gd[2], gd[5] = swap(gd[2], "yl"), swap(gd[5], "xl")
    moe_parts, moe_order = [rows_dx, rows_yo], ((1, 1), (0, 1), (1, 0), (0, 0))
    more = ((gate_dx, gate_yo), mine.astype(F32))

    def moe_sums(start, count):
        other = combine(place_of_token, moe_parts, moe_order, slots, 1, start, count, None, *more)
        other = swap(other, "core")
        return only_own(
            combine(place_of_token, moe_parts, moe_order, slots, 0, start, count, other, *more),
            sizes,
        )

    (term,) = moe_sums(1, 1)
    term, *moe_parts = tie(term, *moe_parts)
    moe_run = line_step(term, zs)
    moe_terms = moe_sums(2, zs - 1)
    moe_run, gd[2], gd[5] = tie(moe_terms[0] + moe_run, gd[2], gd[5])
    gx[3], gy[0] = swap(gx[3], "xl"), swap(gy[0], "yl")
    moe_run = line_step(moe_run, zs)
    moe_run, gx[3], gy[0] = tie(moe_terms[1] + moe_run, gx[3], gy[0])
    gx[4], gy[1] = swap(gx[4], "xl"), swap(gy[1], "yl")
    moe_run = line_step(moe_run, zs)

    mask_own, scale_own = chosen_tables(meta[:pick_count], meta[pick_count:], expert_count)
    logits_own = dot(w_router, normed_two_low, ((0,), (1,)))
    prob_own = masked_softmax(logits_own, mask_own, 0)
    unit = max(8, dp_count * zs * 128 // math.gcd(model_width, dp_count * zs * 128))
    sum_rows = -(-(expert_count + 2) // unit) * unit
    prob_own, scale_own, moe_terms[1] = tie(prob_own, scale_own, moe_terms[1])
    for i in range(3):
        gx[i], gy[3 + i] = gx[i] + gd[i], gy[3 + i] + gd[3 + i]
    moe_run, gx[4], gy[1], *both = tie(moe_run, gx[4], gy[1], *gx[:3], *gy[3:])
    gx[:3], gy[3:] = both[:3], both[3:]
    gx[5], gy[2] = swap(gx[5], "xl"), swap(gy[2], "yl")
    gx[0], gy[3] = swap(gx[0], "xl"), swap(gy[3], "yl")
    grad_middle, grad_branch, grad_attended, early_sums = moe_back(
        jnp.arange(zs),
        sum_rows,
        moe_terms[2],
        moe_run,
        prob_own,
        scale_own,
        w_router.T,
        normed_two_low,
        middle,
        norm2_gain,
        out_grad,
        w_out,
    )

    attended_rows = attended_own.transpose(1, 0, 2).reshape(tok_rows, zs * query_width)
    grad_w_out = dot(grad_branch, attended_rows, ((0,), (0,))).astype(BF16)
    shard_out = lax.psum_scatter(grad_w_out, ROWS, scatter_dimension=0, tiled=True)
    grad_attended = exchange(grad_attended, "z")
    out_run, grad_attended, _, gx[5], gy[2] = tie(
        out_run, grad_attended, grad_w_out, gx[5], gy[2]
    )
    gx[1], gy[4] = swap(gx[1], "xl"), swap(gy[4], "yl")
    out_run = line_step(out_run, zs)
    grad_proj = attend_back(
        qkv, lse, grad_attended.reshape(length, query_width), cosine, sine, heads, groups
    )
    out_run, grad_proj = tie(out_run, grad_proj)
    terms = [
        dot(g, w_in, ((1,), (1,))).astype(BF16)
        for g in behind(grad_proj.reshape(zs, tok_rows, -1), zs)
    ]
    terms[1], grad_proj = tie(terms[1], grad_proj)
    run = line_step(terms[1], zs)
    grad_w_in, gain_rows = project_back(places, seq_pieces, grad_proj, w_in)
    run, grad_w_in, gain_rows, gx[0], gy[3], *terms = tie(
        run, grad_w_in, gain_rows, gx[0], gy[3], *terms
    )
    gx[2], gy[5] = swap(gx[2], "xl"), swap(gy[5], "yl")
    run = line_step(terms[2] + run, zs)

    sums = lax.dynamic_update_slice(early_sums, gain_rows[:1], (expert_count + 1, 0))
    sums, shard_out, grad_w_in = tie(sums.reshape(dp_count * zs, -1, 128), shard_out, grad_w_in)
    shard_in = lax.psum_scatter(grad_w_in, ROWS, scatter_dimension=0, tiled=True)
    shard_out = shard_out.reshape(-1, zs, query_width).transpose(1, 0, 2)
    chunks = behind(shard_out, zs)
    for step in range(1, zs):
        chunks[step] = lax.ppermute(
            chunks[step], "z", [(i, (i + zs - step) % zs) for i in range(zs)]
        )
    sums = jnp.sum(exchange(sums, ALL), axis=0)
    output = middle + RESIDUAL_SCALE * (out_terms[2].astype(F32) + out_run.astype(F32))
    run, sums, gx[1], gy[4], gx[2], gy[5], output, *chunks = tie(
        terms[3] + run, sums, gx[1], gy[4], gx[2], gy[5], output, *chunks
    )
    run = line_step(run, zs)
    sums = share(sums, ALL, dp_count * zs)
    grad_w_gate_up, grad_w_down = collect(
        [(go[i], gx[i], gy[i]) for i in range(6)], model_width
    )

    run, grad_w_gate_up, grad_w_down = tie(run, grad_w_gate_up, grad_w_down)
    grad_hidden = finish(terms[0], run, hidden_in, norm1_gain, grad_middle)
    grad_hidden, sums = tie(grad_hidden, sums)
    sums = sums.reshape(sum_rows, model_width)
    shard_output = sum(chunk.astype(F32) for chunk in chunks).T
    shard_query, shard_keyvalue = split_columns(shard_in, query_width)
    return (
        output,
        grad_hidden,
        sums[expert_count + 1] / norm1_gain,
        shard_query,
        shard_keyvalue,
        shard_output,
        sums[expert_count],
        sums[:expert_count].T,
        grad_w_gate_up,
        grad_w_down,
    )


def solution(mesh):
    high = math.isqrt(mesh.shape["dp"] // 2) // 2
    zs = mesh.shape["tensor"]
    inner = Mesh(mesh.devices.reshape(high, 2, high, 2, 2, zs), ALL)
    sizes = dict(inner.shape)
    in_specs = (
        P(ALL, None),
        P(),
        P(ROWS, "z"),
        P(None, ROWS, "z"),
        P("z", ROWS),
        P(),
        P(),
        P(ALL, None, None, None),
        P(ALL, None, None),
        P(ALL, None),
        P(ALL, None),
        P(ALL, None),
    )
    out_specs = (
        P(ALL, None),
        P(ALL, None),
        P(),
        P(ROWS, "z"),
        P(None, ROWS, "z"),
        P("z", ROWS),
        P(),
        P(),
        P(ALL, None, None, None),
        P(ALL, None, None),
    )
    return jax.shard_map(
        functools.partial(local, sizes),
        mesh=inner,
        in_specs=in_specs,
        out_specs=out_specs,
        check_vma=False,
    )
```

```python
import functools
import math

import jax
import jax.numpy as jnp
from jax import lax
from jax.experimental import pallas as pl
from jax.experimental.pallas import tpu as pltpu
from jax.sharding import Mesh
from jax.sharding import PartitionSpec as P

HEAD = 64
EPSILON = 1e-06
ATTN_SCALE = 0.015625
RESIDUAL_SCALE = 0.22
THETA = 10000.0
QUERY_BLOCK = 256
F32 = jnp.float32
BF16 = jnp.bfloat16
SWAP = [(0, 1), (1, 0)]
VMEM_LIMIT = 56 * 1024 * 1024


def lasts(microseconds):
    return pl.CostEstimate(
        flops=int(microseconds * 1.15e9), bytes_accessed=1, transcendentals=0
    )


ROWS = ("yh", "yl", "xh", "xl", "core")
ALL = ROWS + ("z",)


def swap(value, axis):
    return lax.ppermute(value, axis, SWAP)


def dot(a, b, dims):
    return lax.dot_general(a, b, (dims, ((), ())), preferred_element_type=F32)


def rotary_tables(length):
    half_width = HEAD // 2
    frequency = THETA ** (-2.0 * jnp.arange(half_width, dtype=F32) / HEAD)
    angles = jnp.arange(length, dtype=F32)[:, None] * frequency[None, :]
    cosine, sine = jnp.cos(angles), jnp.sin(angles)
    return jnp.tile(cosine, (1, 4)), jnp.tile(jnp.concatenate([-sine, sine], axis=1), (1, 2))


def line_step(value, size):
    return lax.ppermute(value, "z", [(i, (i + 1) % size) for i in range(size)])


def line_pieces(value, size, count=None):
    pieces = [value]
    for _ in range((count or size) - 1):
        pieces.append(line_step(pieces[-1], size))
    return pieces


def line_order(pieces):
    size = len(pieces)
    z = lax.axis_index("z")
    whole = jnp.zeros((size,) + pieces[0].shape, pieces[0].dtype)
    for step, piece in enumerate(pieces):
        whole = lax.dynamic_update_index_in_dim(whole, piece, lax.rem(z + size - step, size), 0)
    return whole


def tie(*values):
    return lax.optimization_barrier(values)


def behind(value, size):
    z = lax.axis_index("z")
    return [
        lax.dynamic_index_in_dim(value, lax.rem(z + size - j, size), 0, False) for j in range(size)
    ]


def spread(pieces, sizes):
    if sizes["yh"] == 1:
        return [piece[None] for piece in pieces]
    return [lax.all_gather(piece, ("yh", "xh"), axis=0, tiled=False) for piece in pieces]


def exchange(value, axes):
    return lax.all_to_all(value, axes, split_axis=0, concat_axis=0, tiled=True)


def share(value, axes, count):
    return exchange(jnp.broadcast_to(value[None], (count,) + value.shape), axes)


def one_hot(place_row, slots):
    rank = lax.broadcasted_iota(jnp.int32, (slots, place_row.shape[1]), 0).astype(F32)
    return jnp.where(rank == place_row, 1.0, 0.0)


def load_weights(sources, gate_up, down, sem):
    step, inner = pl.program_id(0), pl.program_id(1)
    block, half = gate_up.shape[2] // 2, gate_up.shape[3] // 2

    def pairs(k):
        slot = k % 2
        if len(sources[k]) == 2:
            yield sources[k][0], gate_up.at[slot]
            yield sources[k][1], down.at[slot]
            return
        for n, ref in enumerate(sources[k]):
            which, piece = divmod(n, 3)
            if piece == 2:
                yield ref, down.at[slot, pl.ds(which * half, half)]
            else:
                yield ref, gate_up.at[slot, which, pl.ds(piece * block, block)]

    def copies(k):
        for n, (source, target) in enumerate(pairs(k)):
            yield pltpu.make_async_copy(source, target, sem.at[k % 2, n])

    @pl.when((step == 0) & (inner == 0))
    def _():
        for copy in copies(0):
            copy.start()

    for k in range(len(sources)):

        @pl.when((step == k) & (inner == 0))
        def _(k=k):
            for copy in copies(k):
                copy.wait()
            if k + 1 < len(sources):
                for copy in copies(k + 1):
                    copy.start()


def sources_of(refs):
    sources, refs = [], list(refs)
    while refs:
        count = 2 if len(refs[0].shape) == 3 else 6
        sources.append(refs[:count])
        refs = refs[count:]
    return sources


def weight_scratch(width, hidden):
    return [
        pltpu.VMEM((2, 2, width, hidden), BF16),
        pltpu.VMEM((2, hidden, width), BF16),
        pltpu.SemaphoreType.DMA((2, 6)),
    ]


def slot_gates_of(picks, gate_ref, group, number):
    return jnp.concatenate(
        [
            jnp.sum(pick * gate_ref[group, j, pl.ds(number, 1), :], axis=1, keepdims=True)
            for j, pick in enumerate(picks)
        ],
        axis=0,
    )


def forward_kernel(pieces, slots, first, given, *refs):
    x_refs, refs = refs[:pieces], refs[pieces:]
    place_ref, refs = refs[0], refs[1:]
    if first == 0:
        mask_ref, scale_ref, mine_ref, router_ref = refs[:4]
        gate_ref = refs[4 + given + 5]
        weights, outs = sources_of(refs[4 : 4 + given]), refs[4 + given : 4 + given + 5]
    else:
        gate_ref = refs[0]
        weights, outs = sources_of(refs[6 : 6 + given]), refs[6 + given : 6 + given + 5]
    y_ref, xs_ref, dg_ref, du_ref, act_ref = outs
    gate_up, down, sem = refs[-3:]
    step, group = pl.program_id(0), pl.program_id(1)
    number = first + step
    load_weights(weights, gate_up, down, sem)

    if first == 0:

        @pl.when(step == 0)
        def _():
            for j in range(pieces):
                mask = mask_ref[group, j]
                logits = dot(router_ref[...], x_refs[j][0], ((1,), (1,)))
                logits = jnp.where(mask > 0.0, logits, -1e30)
                top = jnp.max(logits, axis=0, keepdims=True)
                exponent = jnp.where(mask > 0.0, jnp.exp(logits - top), 0.0)
                gates = exponent / jnp.sum(exponent, axis=0, keepdims=True) * scale_ref[group, j]
                for e in range(gate_ref.shape[2]):
                    gate_ref[group, j, e : e + 1] = jnp.sum(
                        gates * mine_ref[:, e : e + 1], axis=0, keepdims=True
                    )

    picks = [one_hot(place_ref[group, j, pl.ds(number, 1), :], slots) for j in range(pieces)]
    for j, pick in enumerate(picks):
        rows = dot(pick.astype(BF16), x_refs[j][0], ((1,), (0,)))
        xs_ref[0, j * slots : (j + 1) * slots] = rows.astype(BF16)
    slot_gate = slot_gates_of(picks, gate_ref, group, number)
    now = lax.rem(step, 2)
    x = xs_ref[0]
    gate = dot(x, gate_up[now, 0], ((1,), (0,)))
    up = dot(x, gate_up[now, 1], ((1,), (0,)))
    sigmoid = 1.0 / (1.0 + jnp.exp(-gate))
    silu = gate * sigmoid
    active = (silu * up).astype(BF16)
    act_ref[0] = active
    dg_ref[0] = (up * sigmoid * (1.0 + gate * (1.0 - sigmoid))).astype(BF16)
    du_ref[0] = silu.astype(BF16)
    weighted = (active.astype(F32) * slot_gate).astype(BF16)
    y_ref[0] = dot(weighted, down[now], ((1,), (0,))).astype(BF16)


def backward_kernel(pieces, slots, first, given, *refs):
    g_refs, refs = refs[:pieces], refs[pieces:]
    place_ref, gate_ref, xs_ref, dg_ref, du_ref, act_ref = refs[:6]
    weights, refs = sources_of(refs[6 : 6 + given]), refs[6 + given :]
    experts = len(weights)
    rows_ref, through_ref = refs[:2]
    results = [refs[2 + 6 * k : 8 + 6 * k] for k in range(experts)]
    gate_up, down, sem, gs_ref, stage, stage_down, out_sem = refs[2 + 6 * experts : 9 + 6 * experts]
    sums = refs[9 + 6 * experts :]
    step, group = pl.program_id(0), pl.program_id(1)
    number = first - 2 * step
    load_weights(weights, gate_up, down, sem)
    width = g_refs[0].shape[-1]
    half = down.shape[1] // 2
    now = lax.rem(step, 2)
    last = pl.num_programs(1) - 1

    def stores(k):
        block = width // 2
        for n, ref in enumerate(results[k]):
            which, piece = divmod(n, 3)
            source = stage_down.at[pl.ds(which * half, half)]
            if piece < 2:
                source = stage.at[which, pl.ds(piece * block, block)]
            yield pltpu.make_async_copy(source, ref, out_sem.at[n])

    picks = [one_hot(place_ref[group, j, pl.ds(number, 1), :], slots) for j in range(pieces)]
    for j, pick in enumerate(picks):
        rows = dot(pick.astype(BF16), g_refs[j][0], ((1,), (0,)))
        gs_ref[j * slots : (j + 1) * slots] = rows.astype(BF16)
    slot_gate = slot_gates_of(picks, gate_ref, group, number) * RESIDUAL_SCALE
    grad_active = dot(gs_ref[...], down[now], ((1,), (1,)))
    active = act_ref[0].astype(F32)
    through = jnp.sum(grad_active * active, axis=1, keepdims=True) * RESIDUAL_SCALE
    for j, pick in enumerate(picks):
        through_ref[0, j] = jnp.sum(
            pick * through[j * slots : (j + 1) * slots], axis=0, keepdims=True
        )
    grad_active = grad_active * slot_gate
    grad_gate = (grad_active * dg_ref[0].astype(F32)).astype(BF16)
    grad_up = (grad_active * du_ref[0].astype(F32)).astype(BF16)
    rows = dot(grad_gate, gate_up[now, 0], ((1,), (1,)))
    rows = rows + dot(grad_up, gate_up[now, 1], ((1,), (1,)))
    rows_ref[0] = rows.astype(BF16)
    weighted = (active * slot_gate).astype(BF16)

    for k in range(1, experts):

        @pl.when((step == k) & (group == last))
        def _(k=k):
            for copy in stores(k - 1):
                copy.wait()

    def add(target, total, left, right):
        part = dot(left, right, ((0,), (0,)))
        if total is None:
            target[...] = part.astype(BF16)
            return

        @pl.when(group == 0)
        def _():
            total[...] = part

        @pl.when(group > 0)
        def _():
            total[...] += part

        @pl.when(group == last)
        def _():
            target[...] = total[...].astype(BF16)

    x = xs_ref[0]
    totals = [sums[0].at[0], sums[0].at[1], sums[1]] if sums else [None] * 3
    add(stage.at[0], totals[0], x, grad_gate)
    add(stage.at[1], totals[1], x, grad_up)
    add(stage_down, totals[2], weighted, gs_ref[...])
    for k in range(experts):

        @pl.when((step == k) & (group == last))
        def _(k=k):
            for copy in stores(k):
                copy.start()
            if k == experts - 1:
                for copy in stores(k):
                    copy.wait()


def resident(arrays):
    return [
        pl.BlockSpec(a.shape, lambda e, c, n=a.ndim: (0,) * n, pipeline_mode=pl.Buffered(1))
        for a in arrays
    ]


def piece_spec(piece):
    groups, tokens, width = piece.shape
    mode = pl.Buffered(1) if groups == 1 else None
    return pl.BlockSpec((1, tokens, width), lambda e, c: (c, 0, 0), pipeline_mode=mode)


def experts_forward(first, x_pieces, place, tables, weights, slots, before=None):
    pieces = len(x_pieces)
    groups, tokens, width = x_pieces[0].shape
    hidden = weights[0][0].shape[-1]
    rows = pieces * slots
    experts = place.shape[2]
    anywhere = pl.BlockSpec(memory_space=pl.ANY)
    flat = [array for pair in weights for array in pair]
    before = list(before or [])

    def by_slot(n):
        return pl.BlockSpec((1, rows, n), lambda e, c: (first + e, c, 0))

    gate_shape = (groups, pieces, experts, tokens)
    widths = (width, width, hidden, hidden, hidden)
    out_specs = [by_slot(n) for n in widths]
    out_shape = [jax.ShapeDtypeStruct((experts, groups * rows, n), BF16) for n in widths]
    if first == 0:
        out_specs.append(pl.BlockSpec(gate_shape, lambda e, c: (0, 0, 0, 0)))
        out_shape.append(jax.ShapeDtypeStruct(gate_shape, F32))
    operands = [*x_pieces, place, *tables]
    return pl.pallas_call(
        functools.partial(forward_kernel, pieces, slots, first, len(flat)),
        grid=(len(weights), groups),
        in_specs=[piece_spec(p) for p in x_pieces]
        + resident([place, *tables])
        + [anywhere] * (len(before) + len(flat)),
        out_specs=out_specs,
        out_shape=out_shape,
        input_output_aliases={len(operands) + n: n for n in range(len(before))},
        scratch_shapes=weight_scratch(width, hidden),
        compiler_params=pltpu.CompilerParams(vmem_limit_bytes=VMEM_LIMIT),
        cost_estimate=lasts(8.0 * len(weights)),
        name="experts_forward",
    )(*operands, *before, *flat)


def experts_backward(first, g_pieces, place, gates, saved, weights, slots):
    pieces = len(g_pieces)
    groups, tokens, width = g_pieces[0].shape
    experts = len(weights)
    hidden = weights[0][0].shape[-1]
    rows = pieces * slots
    flat = [array for pair in weights for array in pair]

    def by_slot(n):
        return pl.BlockSpec((1, rows, n), lambda e, c: (first - 2 * e, c, 0))

    anywhere = pl.BlockSpec(memory_space=pl.ANY)
    block = jax.ShapeDtypeStruct((width // 2, hidden), BF16)
    return pl.pallas_call(
        functools.partial(backward_kernel, pieces, slots, first, len(flat)),
        grid=(experts, groups),
        in_specs=[piece_spec(p) for p in g_pieces]
        + resident([place, gates])
        + [by_slot(width)]
        + [by_slot(hidden)] * 3
        + [anywhere] * len(flat),
        out_specs=[
            pl.BlockSpec((1, rows, width), lambda e, c: (e, c, 0)),
            pl.BlockSpec((1, pieces, 1, tokens), lambda e, c: (e, c, 0, 0)),
        ]
        + [anywhere] * (6 * experts),
        out_shape=[
            jax.ShapeDtypeStruct((experts, groups * rows, width), BF16),
            jax.ShapeDtypeStruct((experts, groups * pieces, 1, tokens), F32),
        ]
        + [block, block, jax.ShapeDtypeStruct((hidden // 2, width), BF16)] * (2 * experts),
        scratch_shapes=weight_scratch(width, hidden)
        + [
            pltpu.VMEM((rows, width), BF16),
            pltpu.VMEM((2, width, hidden), BF16),
            pltpu.VMEM((hidden, width), BF16),
            pltpu.SemaphoreType.DMA((6,)),
        ]
        + (
            [pltpu.VMEM((2, width, hidden), F32), pltpu.VMEM((hidden, width), F32)]
            if groups > 1
            else []
        ),
        compiler_params=pltpu.CompilerParams(vmem_limit_bytes=VMEM_LIMIT),
        cost_estimate=lasts(14.5 * experts),
        name="experts_backward",
    )(*g_pieces, place, gates, *saved, *flat)


def extra_rows(expert_count, tokens, width):
    return 16 * -(-(-(-2 * expert_count // 16)) // (width // tokens))


def extra_places(expert_count, tokens, width):
    across = width // tokens
    for block in range(-(-2 * expert_count // 16)):
        yield block, 16 * (block // across), tokens * (block % across)


def combine_kernel(order, slots, extra, pieces, place_ref, *refs):
    parts = 1 + max(which for which, _ in order)
    experts = len(order)
    rows_refs, refs = refs[:parts], refs[parts:]
    if extra:
        through_refs, mine_ref, refs = refs[:parts], refs[parts], refs[parts + 1 :]
    step = pl.program_id(0)
    tokens = place_ref.shape[1]
    lane = lax.broadcasted_iota(jnp.int32, (tokens, experts * slots), 1).astype(F32)
    hit = lane == place_ref[0, :, 0:1]
    for e in range(1, experts):
        hit = hit | (lane == place_ref[0, :, e : e + 1])
    pick = jnp.where(hit, 1.0, 0.0).astype(BF16)
    rows = jnp.concatenate([rows_refs[which][k] for which, k in order], axis=0)
    out = dot(pick, rows, ((1,), (0,)))
    width = out.shape[1]
    more = None
    if extra:
        dense = 0.0
        for e, (which, k) in enumerate(order):
            dense = dense + mine_ref[:, e : e + 1] * through_refs[which][k, 0]
        high = dense.astype(BF16).astype(F32)
        both = jnp.concatenate([high, dense - high], axis=0)
        across = width // tokens
        lines = []
        for start in range(0, both.shape[0], 16 * across):
            line = [both[i : i + 16] for i in range(start, min(start + 16 * across, both.shape[0]), 16)]
            line += [jnp.zeros((16, tokens), F32)] * (across - len(line))
            lines.append(jnp.concatenate(line, axis=1))
        more = jnp.concatenate(lines, axis=0)

    def store(ref):
        if not pieces:
            ref[0, :tokens] = out.astype(BF16)
            if extra:
                ref[0, tokens:] = more.astype(BF16)
            return
        ref[0, :tokens] = (out + refs[0][0, :tokens].astype(F32)).astype(BF16)
        if extra:
            ref[0, tokens:] = (more + refs[0][0, tokens:].astype(F32)).astype(BF16)

    if not pieces:
        store(refs[0])
        return
    for j in range(pieces):

        @pl.when(lax.rem(step, pieces) == j)
        def _(j=j):
            store(refs[1 + j])


def combine(place, parts, order, slots, half, start, count, other=None, through=None, mine=None):
    groups, pieces, tokens, experts = place.shape
    column = pieces // 2
    width = parts[0].shape[-1]
    extra = 0 if through is None else extra_rows(mine.shape[0], tokens, width)

    def at(i):
        return (i // count) * pieces + half * column + (start + i % count) % column

    in_specs = [pl.BlockSpec((1, tokens, experts), lambda i: (at(i), 0, 0))]
    in_specs += [pl.BlockSpec((p.shape[0], slots, width), lambda i: (0, at(i), 0)) for p in parts]
    operands = [place.reshape(groups * pieces, tokens, experts), *parts]
    if extra:
        in_specs += [
            pl.BlockSpec((t.shape[0], 1, 1, tokens), lambda i: (0, at(i), 0, 0)) for t in through
        ]
        in_specs.append(pl.BlockSpec(mine.shape, lambda i: (0, 0)))
        operands += [*through, mine]
    rows = tokens + extra
    by_step = pl.BlockSpec((1, rows, width), lambda i: (i, 0, 0))
    if other is None:
        out_specs, out_shape = by_step, jax.ShapeDtypeStruct((groups * count, rows, width), BF16)
    else:
        in_specs.append(by_step)
        operands.append(other)
        out_specs = [pl.BlockSpec((1, rows, width), lambda i: (i // count, 0, 0))] * count
        out_shape = [jax.ShapeDtypeStruct((groups, rows, width), BF16)] * count
    return pl.pallas_call(
        functools.partial(combine_kernel, order, slots, extra, 0 if other is None else count),
        grid=(groups * count,),
        in_specs=in_specs,
        out_specs=out_specs,
        out_shape=out_shape,
        compiler_params=pltpu.CompilerParams(vmem_limit_bytes=VMEM_LIMIT),
        cost_estimate=lasts(0.1),
        name="combine",
    )(*operands)


def only_own(terms, sizes):
    if sizes["yh"] == 1:
        return [term[0] for term in terms]
    return [
        lax.psum_scatter(term, ("yh", "xh"), scatter_dimension=0, tiled=True)[0] for term in terms
    ]


def packed_specs(width, hidden):
    block = width // 2
    return (
        pl.BlockSpec((1, 1, block, hidden), lambda h, i: (0, h, jnp.minimum(i, 1), 0)),
        pl.BlockSpec((1, hidden // 2, width), lambda h, i: (0, h, 0)),
    )


def take_kernel(gate_ref, down_a_ref, up_ref, down_b_ref, *out_refs):
    step = pl.program_id(0)
    for n in (0, 1):

        @pl.when(step == n)
        def _(n=n):
            out_refs[n][...] = gate_ref[0]
            out_refs[3 + n][...] = up_ref[0]

    @pl.when(step == 2)
    def _():
        out_refs[2][...] = down_a_ref[...]
        out_refs[5][...] = down_b_ref[...]


def take_pieces(gate_up_x, down_x, gate_up_y, down_y):
    _, width, hidden = gate_up_x.shape
    block, half = width // 2, hidden // 2

    def specs(which):
        return [
            pl.BlockSpec((1, block, hidden), lambda i: (which, jnp.minimum(i, 1), 0)),
            pl.BlockSpec((half, width), lambda i: (which, 0)),
        ]

    shapes = [(block, hidden), (block, hidden), (half, width)] * 2
    return pl.pallas_call(
        take_kernel,
        grid=(3,),
        in_specs=specs(0) + specs(1),
        out_specs=[pl.BlockSpec(shape, lambda i: (0, 0)) for shape in shapes],
        out_shape=[jax.ShapeDtypeStruct(shape, BF16) for shape in shapes],
        compiler_params=pltpu.CompilerParams(vmem_limit_bytes=VMEM_LIMIT),
        cost_estimate=lasts(4.0),
        name="take_pieces",
    )(gate_up_x, down_x, gate_up_y, down_y)


def collect_kernel(*refs):
    gate_up_ref, down_ref, wide, deep, sem = refs[-5:]
    step = pl.program_id(0) * 3 + pl.program_id(1)

    def slot(n):
        return deep.at[n // 3] if n % 3 == 2 else wide.at[n % 3]

    def copies(n):
        for k in range(3):
            yield pltpu.make_async_copy(refs[3 * n + k], slot(n).at[k], sem.at[n, k])

    @pl.when(step == 0)
    def _():
        for n in (0, 1, 2, 5):
            for copy in copies(n):
                copy.start()

    for n in range(6):

        @pl.when(step == n)
        def _(n=n):
            for copy in copies(n):
                copy.wait()
            here = slot(n)
            total = here[0].astype(F32) + here[1].astype(F32) + here[2].astype(F32)
            if n % 3 < 2:
                gate_up_ref[0, 0] = total
            else:
                down_ref[0] = total
            if n < 2:
                for copy in copies(n + 3):
                    copy.start()


def collect(pieces, width):
    hidden = pieces[0][0].shape[1]
    gate_up_spec, down_spec = packed_specs(width, hidden)
    return pl.pallas_call(
        collect_kernel,
        grid=(2, 3),
        in_specs=[pl.BlockSpec(memory_space=pl.ANY)] * 18,
        out_specs=[gate_up_spec, down_spec],
        out_shape=[
            jax.ShapeDtypeStruct((1, 2, width, hidden), F32),
            jax.ShapeDtypeStruct((1, hidden, width), F32),
        ],
        scratch_shapes=[
            pltpu.VMEM((2, 3, width // 2, hidden), BF16),
            pltpu.VMEM((2, 3, hidden // 2, width), BF16),
            pltpu.SemaphoreType.DMA((6, 3)),
        ],
        compiler_params=pltpu.CompilerParams(vmem_limit_bytes=VMEM_LIMIT),
        cost_estimate=lasts(9.5),
        name="collect",
    )(*[array for piece in pieces for array in piece])


def inverse_root(values):
    return lax.rsqrt(jnp.mean(values * values, axis=-1, keepdims=True) + EPSILON)


def branch_kernel(place_ref, att_ref, w_ref, hidden_ref, gain_ref, middle_ref, low_ref):
    step = pl.program_id(0)
    weights = w_ref[:, 0].reshape(hidden_ref.shape[1], w_ref.shape[-1])
    part = RESIDUAL_SCALE * dot(att_ref[0], weights, ((1,), (1,)))

    @pl.when(step == 0)
    def _():
        middle_ref[...] = hidden_ref[...] + part

    @pl.when(step > 0)
    def _():
        middle_ref[...] += part

    @pl.when(step == pl.num_programs(0) - 1)
    def _():
        middle = middle_ref[...]
        low_ref[...] = (middle * inverse_root(middle) * gain_ref[...]).astype(BF16)


def out_weights_spec(weights):
    rows, _, height, columns = weights.shape
    return pl.BlockSpec((rows, 1, height, columns), lambda i, p: (0, i, 0, 0))


def branch_norm(places, attended, weights, hidden, gain):
    count, tokens, columns = attended.shape
    width = hidden.shape[1]
    return pl.pallas_call(
        branch_kernel,
        grid_spec=pltpu.PrefetchScalarGridSpec(
            num_scalar_prefetch=1,
            grid=(count,),
            in_specs=[
                pl.BlockSpec((1, tokens, columns), lambda i, p: (p[i], 0, 0)),
                out_weights_spec(weights),
                pl.BlockSpec((tokens, width), lambda i, p: (0, 0)),
                pl.BlockSpec((1, width), lambda i, p: (0, 0)),
            ],
            out_specs=[pl.BlockSpec((tokens, width), lambda i, p: (0, 0))] * 2,
        ),
        out_shape=[
            jax.ShapeDtypeStruct((tokens, width), F32),
            jax.ShapeDtypeStruct((tokens, width), BF16),
        ],
        compiler_params=pltpu.CompilerParams(vmem_limit_bytes=VMEM_LIMIT),
        cost_estimate=lasts(7.0),
        name="branch_norm",
    )(places, attended, weights, hidden, gain.reshape(1, width))


def moe_back_kernel(
    extra, place_ref, own_ref, run_ref, prob_ref, scale_ref, router_ref, low_ref, middle_ref, gain_ref, grad_ref, w_ref,
    grad_middle_ref, branch_ref, attended_ref, sums_ref,
):
    tokens = middle_ref.shape[0]

    @pl.when(pl.program_id(0) == 0)
    def _():
        experts = prob_ref.shape[0]

        def total(rows, columns=slice(None)):
            return own_ref[rows, columns].astype(F32) + run_ref[rows, columns].astype(F32)

        both = jnp.concatenate(
            [
                total(slice(tokens + row, tokens + row + 16), slice(column, column + tokens))
                for _, row, column in extra
            ],
            axis=0,
        )
        scaled = (both[:experts] + both[experts : 2 * experts]) * scale_ref[...]
        prob = prob_ref[...]
        chosen = prob * (scaled - jnp.sum(prob * scaled, axis=0, keepdims=True))
        chosen = chosen.astype(BF16)
        sums_ref[:experts] = dot(chosen, low_ref[...], ((1,), (0,)))
        grad = total(slice(0, tokens)) + dot(chosen, router_ref[...], ((0,), (0,)))
        middle = middle_ref[...]
        inverse = inverse_root(middle)
        scaled = middle * inverse
        sums_ref[experts:] = jnp.zeros((sums_ref.shape[0] - experts, middle.shape[1]), F32)
        sums_ref[experts : experts + 1] = jnp.sum(grad * scaled, axis=0, keepdims=True)
        grad = grad * gain_ref[...]
        mean = jnp.mean(grad * scaled, axis=-1, keepdims=True)
        grad = grad_ref[...] + inverse * (grad - scaled * mean)
        grad_middle_ref[...] = grad
        branch_ref[...] = (RESIDUAL_SCALE * grad).astype(BF16)

    weights = w_ref[:, 0].reshape(middle_ref.shape[1], w_ref.shape[-1])
    attended_ref[0] = dot(branch_ref[...], weights, ((1,), (0,))).astype(BF16)


def moe_back(places, rows, own, run, prob, scale, router, low, middle, gain, grad, weights):
    tokens, width = middle.shape
    experts = prob.shape[0]
    _, count, _, columns = weights.shape
    extra = list(extra_places(experts, tokens, width))
    operands = [own, run, prob, scale, router, low, middle, gain.reshape(1, width), grad]
    return pl.pallas_call(
        functools.partial(moe_back_kernel, extra),
        grid_spec=pltpu.PrefetchScalarGridSpec(
            num_scalar_prefetch=1,
            grid=(count,),
            in_specs=[pl.BlockSpec(a.shape, lambda i, p: (0, 0)) for a in operands]
            + [out_weights_spec(weights)],
            out_specs=[
                pl.BlockSpec((tokens, width), lambda i, p: (0, 0)),
                pl.BlockSpec((tokens, width), lambda i, p: (0, 0)),
                pl.BlockSpec((1, tokens, columns), lambda i, p: (p[i], 0, 0)),
                pl.BlockSpec((rows, width), lambda i, p: (0, 0)),
            ],
        ),
        out_shape=[
            jax.ShapeDtypeStruct((tokens, width), F32),
            jax.ShapeDtypeStruct((tokens, width), BF16),
            jax.ShapeDtypeStruct((count, tokens, columns), BF16),
            jax.ShapeDtypeStruct((rows, width), F32),
        ],
        compiler_params=pltpu.CompilerParams(vmem_limit_bytes=VMEM_LIMIT),
        cost_estimate=lasts(20.0),
        name="moe_back",
    )(places, *operands, weights)


def split_kernel(value_ref, first_ref, rest_ref):
    value = value_ref[...].astype(F32)
    cut, each = first_ref.shape[1], rest_ref.shape[2]
    first_ref[...] = value[:, :cut]
    for k in (0, 1):
        rest_ref[k] = value[:, cut + k * each : cut + (k + 1) * each]


def split_columns(value, cut):
    rows, columns = value.shape
    return pl.pallas_call(
        split_kernel,
        out_shape=[
            jax.ShapeDtypeStruct((rows, cut), F32),
            jax.ShapeDtypeStruct((2, rows, (columns - cut) // 2), F32),
        ],
        cost_estimate=lasts(1.0),
        name="split_columns",
    )(value)


def finish_kernel(own_ref, run_ref, hidden_ref, gain_ref, grad_ref, out_ref):
    grad = own_ref[...].astype(F32) + run_ref[...].astype(F32)
    hidden = hidden_ref[...]
    inverse = inverse_root(hidden)
    scaled = hidden * inverse
    grad = grad * gain_ref[...]
    mean = jnp.mean(grad * scaled, axis=-1, keepdims=True)
    out_ref[...] = grad_ref[...] + inverse * (grad - scaled * mean)


def finish(own, run, hidden, gain, grad):
    tokens, width = hidden.shape
    rows = pl.BlockSpec((tokens // 2, width), lambda i: (i, 0))
    return pl.pallas_call(
        finish_kernel,
        grid=(2,),
        in_specs=[rows, rows, rows, pl.BlockSpec((1, width), lambda i: (0, 0)), rows],
        out_specs=rows,
        out_shape=jax.ShapeDtypeStruct((tokens, width), F32),
        compiler_params=pltpu.CompilerParams(vmem_limit_bytes=VMEM_LIMIT),
        cost_estimate=lasts(3.5),
        name="finish",
    )(own, run, hidden, gain.reshape(1, width), grad)


def causal_mask(scores, start):
    keys, columns = scores.shape
    block = keys - start
    key = lax.broadcasted_iota(jnp.int32, (block, columns), 0)
    query = lax.rem(lax.broadcasted_iota(jnp.int32, (block, columns), 1), block)
    low = jnp.where(key <= query, scores[start:], -1e30)
    return low if start == 0 else jnp.concatenate([scores[:start], low], axis=0)


def head_rows(pair, odd):
    lane = lax.broadcasted_iota(jnp.int32, pair.shape, 1)
    return jnp.where((lane >= HEAD) == odd, pair, jnp.zeros_like(pair))


def both_halves(rows):
    return jnp.concatenate([rows, rows], axis=1)


def attend_kernel(heads, groups, block, qkv_ref, out_ref, lse_ref):
    length = qkv_ref.shape[0]
    each = heads // groups
    at_key = heads * HEAD
    at_value = at_key + groups * HEAD
    for i in range(length // block):
        start, stop = i * block, (i + 1) * block
        parts = []
        for g in range(groups):
            key = both_halves(qkv_ref[:stop, at_key + g * HEAD : at_key + (g + 1) * HEAD])
            value = qkv_ref[:stop, at_value + g * HEAD : at_value + (g + 1) * HEAD]
            query = []
            for h in range(g * each, (g + 1) * each):
                pair = qkv_ref[start:stop, h // 2 * 2 * HEAD : (h // 2 + 1) * 2 * HEAD]
                query.append(head_rows(pair, h % 2 == 1) * ATTN_SCALE)
            query = jnp.concatenate(query, axis=0).astype(BF16)
            scores = causal_mask(dot(key, query, ((1,), (1,))), start)
            top = jnp.max(scores, axis=0, keepdims=True)
            exponent = jnp.exp(scores - top)
            norm = jnp.sum(exponent, axis=0, keepdims=True)
            total = top + jnp.log(norm)
            out = dot(value, exponent.astype(BF16), ((0,), (0,))) / norm
            for k in range(each):
                columns = slice(k * block, (k + 1) * block)
                lse_ref[g * each + k : g * each + k + 1, start:stop] = total[:, columns]
                parts.append(out[:, columns])
        for pair in range(heads // 2):
            rows = jnp.concatenate(parts[2 * pair : 2 * pair + 2], axis=0)
            out_ref[start:stop, pair * 2 * HEAD : (pair + 1) * 2 * HEAD] = rows.T.astype(BF16)


def attend(qkv, heads, groups):
    length = qkv.shape[0]
    return pl.pallas_call(
        functools.partial(attend_kernel, heads, groups, min(QUERY_BLOCK, length)),
        out_shape=[
            jax.ShapeDtypeStruct((length, heads * HEAD), BF16),
            jax.ShapeDtypeStruct((8 * -(-heads // 8), length), F32),
        ],
        compiler_params=pltpu.CompilerParams(vmem_limit_bytes=VMEM_LIMIT),
        cost_estimate=lasts(8.0),
        name="attend",
    )(qkv)


def turn(values, cosine, sine, direction):
    width = values.shape[1]
    lane = lax.broadcasted_iota(jnp.int32, values.shape, 1)
    first = lax.rem(lane, HEAD) < HEAD // 2
    behind_half = pltpu.roll(values, width - HEAD // 2, 1)
    other = jnp.where(first, behind_half, pltpu.roll(values, HEAD // 2, 1))
    repeats = width // cosine.shape[1]
    cosine = jnp.concatenate([cosine] * repeats, axis=1) if repeats > 1 else cosine
    sine = jnp.concatenate([sine] * repeats, axis=1) if repeats > 1 else sine
    return values * cosine + direction * (other * sine)


def attend_back_kernel(
    heads, groups, block, qkv_ref, lse_ref, grad_ref, cos_ref, sin_ref, out_ref, key_sum, value_sum
):
    length = qkv_ref.shape[0]
    each = heads // groups
    at_key = heads * HEAD
    at_value = at_key + groups * HEAD
    for i in reversed(range(length // block)):
        start, stop = i * block, (i + 1) * block
        parts = []
        for g in range(groups):
            key = qkv_ref[:stop, at_key + g * HEAD : at_key + (g + 1) * HEAD]
            value = both_halves(qkv_ref[:stop, at_value + g * HEAD : at_value + (g + 1) * HEAD])
            query, grad, lse = [], [], []
            for h in range(g * each, (g + 1) * each):
                columns = slice(h // 2 * 2 * HEAD, (h // 2 + 1) * 2 * HEAD)
                query.append(head_rows(qkv_ref[start:stop, columns], h % 2 == 1) * ATTN_SCALE)
                grad.append(head_rows(grad_ref[start:stop, columns], h % 2 == 1))
                lse.append(lse_ref[h : h + 1, start:stop])
            query = jnp.concatenate(query, axis=0).astype(BF16)
            grad = jnp.concatenate(grad, axis=0)
            lse = jnp.concatenate(lse, axis=1)
            scores = causal_mask(dot(both_halves(key), query, ((1,), (1,))), start)
            probs = jnp.exp(scores - lse)
            grad_probs = dot(value, grad, ((1,), (1,)))
            weighted = probs * grad_probs
            delta = jnp.sum(weighted, axis=0, keepdims=True)
            grad_scores = (weighted - probs * delta).astype(BF16)
            grad_value = dot(probs.astype(BF16), grad, ((1,), (0,)))
            grad_key = dot(grad_scores, query, ((1,), (0,)))
            if stop == length:
                value_sum[g] = grad_value
                key_sum[g] = grad_key
            else:
                value_sum[g, :stop] += grad_value
                key_sum[g, :stop] += grad_key
            grad_query = dot(key, grad_scores, ((0,), (0,))) * ATTN_SCALE
            for k in range(each):
                parts.append(grad_query[:, k * block : (k + 1) * block])
        cosine, sine = cos_ref[start:stop], sin_ref[start:stop]
        for pair in range(heads // 2):
            rows = jnp.concatenate(parts[2 * pair : 2 * pair + 2], axis=0).T
            rows = turn(rows, cosine, sine, -1.0).astype(BF16)
            out_ref[start:stop, pair * 2 * HEAD : (pair + 1) * 2 * HEAD] = rows
    rows = [key_sum[g][:, :HEAD] + key_sum[g][:, HEAD:] for g in range(groups)]
    rows = turn(jnp.concatenate(rows, axis=1), cos_ref[...], sin_ref[...], -1.0)
    out_ref[:, at_key:at_value] = rows.astype(BF16)
    rows = [value_sum[g][:, :HEAD] + value_sum[g][:, HEAD:] for g in range(groups)]
    out_ref[:, at_value:] = jnp.concatenate(rows, axis=1).astype(BF16)


def attend_back(qkv, lse, grad, cosine, sine, heads, groups):
    length = qkv.shape[0]
    return pl.pallas_call(
        functools.partial(attend_back_kernel, heads, groups, min(QUERY_BLOCK, length)),
        out_shape=jax.ShapeDtypeStruct(qkv.shape, BF16),
        scratch_shapes=[pltpu.VMEM((groups, length, 2 * HEAD), F32)] * 2,
        compiler_params=pltpu.CompilerParams(vmem_limit_bytes=VMEM_LIMIT),
        cost_estimate=lasts(14.0),
        name="attend_back",
    )(qkv, lse, grad, cosine, sine)


def project_kernel(turned, place_ref, x_ref, w_ref, cos_ref, sin_ref, *refs):
    out_ref = refs[-1]
    values = dot(x_ref[...], w_ref[...], ((1,), (0,)))
    out_ref[:, :turned] = turn(values[:, :turned], cos_ref[...], sin_ref[...], 1.0).astype(BF16)
    out_ref[:, turned:] = values[:, turned:].astype(BF16)


def project(place, rows, weights, cosine, sine, turned, before=None):
    tokens, width = rows.shape
    columns = weights.shape[1]
    in_specs = [
        pl.BlockSpec((tokens, width), lambda i, p: (0, 0)),
        pl.BlockSpec((width, columns), lambda i, p: (0, 0)),
        pl.BlockSpec((tokens, cosine.shape[1]), lambda i, p: (p[0], 0)),
        pl.BlockSpec((tokens, sine.shape[1]), lambda i, p: (p[0], 0)),
    ]
    operands = [place.reshape(1), rows, weights, cosine, sine]
    if before is not None:
        in_specs.append(pl.BlockSpec(memory_space=pl.ANY))
        operands.append(before)
    return pl.pallas_call(
        functools.partial(project_kernel, turned),
        grid_spec=pltpu.PrefetchScalarGridSpec(
            num_scalar_prefetch=1,
            grid=(1,),
            in_specs=in_specs,
            out_specs=pl.BlockSpec((tokens, columns), lambda i, p: (p[0], 0)),
        ),
        out_shape=jax.ShapeDtypeStruct((cosine.shape[0], columns), BF16),
        input_output_aliases={} if before is None else {5: 0},
        compiler_params=pltpu.CompilerParams(vmem_limit_bytes=VMEM_LIMIT),
        cost_estimate=lasts(4.0),
        name="project",
    )(*operands)


def project_back_kernel(pieces, place_ref, *refs):
    x_refs = refs[:pieces]
    grad_ref, w_ref, out_ref, gain_ref = refs[pieces:]
    tokens = x_refs[0].shape[0]
    grad = 0.0
    for j in range(pieces):
        start = pl.multiple_of(place_ref[j] * tokens, tokens)
        grad = grad + dot(x_refs[j][...], grad_ref[pl.ds(start, tokens), :], ((0,), (0,)))
    out_ref[...] = grad.astype(BF16)
    ones = jnp.ones((8, w_ref.shape[1]), BF16)
    products = w_ref[...].astype(F32) * grad
    high = products.astype(BF16)
    low = (products - high.astype(F32)).astype(BF16)
    gain_ref[...] = dot(ones, high, ((1,), (1,))) + dot(ones, low, ((1,), (1,)))


def project_back(places, pieces, grad, weights):
    tokens, width = pieces[0].shape
    columns = weights.shape[1]
    cut = width // 3
    return pl.pallas_call(
        functools.partial(project_back_kernel, len(pieces)),
        grid_spec=pltpu.PrefetchScalarGridSpec(
            num_scalar_prefetch=1,
            grid=(3,),
            in_specs=[pl.BlockSpec((tokens, cut), lambda i, p: (0, i))] * len(pieces)
            + [
                pl.BlockSpec(grad.shape, lambda i, p: (0, 0)),
                pl.BlockSpec((cut, columns), lambda i, p: (i, 0)),
            ],
            out_specs=[
                pl.BlockSpec((cut, columns), lambda i, p: (i, 0)),
                pl.BlockSpec((8, cut), lambda i, p: (0, i)),
            ],
        ),
        out_shape=[
            jax.ShapeDtypeStruct((width, columns), BF16),
            jax.ShapeDtypeStruct((8, width), F32),
        ],
        compiler_params=pltpu.CompilerParams(vmem_limit_bytes=VMEM_LIMIT),
        cost_estimate=lasts(9.0),
        name="project_back",
    )(places, *pieces, grad, weights)


def chosen_tables(ids, scale, expert_count):
    lead = (1,) * (ids.ndim - 2)
    numbers = jnp.arange(expert_count, dtype=F32).reshape(lead + (1, expert_count, 1))
    hits = ids[..., :, None, :] == numbers
    mask = jnp.any(hits, axis=-3)
    return mask, jnp.sum(jnp.where(hits, scale[..., :, None, :], 0.0), axis=-3)


def masked_softmax(logits, mask, axis):
    top = jnp.max(jnp.where(mask, logits, -jnp.inf), axis=axis, keepdims=True)
    exponent = jnp.where(mask, jnp.exp(jnp.where(mask, logits - top, 0.0)), 0.0)
    return exponent / jnp.sum(exponent, axis=axis, keepdims=True)


def local(
    sizes,
    hidden_in,
    norm1_gain,
    w_query,
    w_keyvalue,
    w_output,
    norm2_gain,
    w_router,
    w_gate_up,
    w_down,
    expert_ids,
    choice_scale,
    out_grad,
):
    tok_rows, model_width = hidden_in.shape
    pick_count = expert_ids.shape[1]
    expert_count = w_router.shape[1]
    capacity = max(2, (tok_rows * pick_count * 11 + 8 * expert_count - 1) // (8 * expert_count))
    slots = -(-capacity // 16) * 16
    zs, high = sizes["z"], sizes["yh"]
    yl, xl, core, z = (lax.axis_index(a) for a in ("yl", "xl", "core", "z"))
    yh, xh = lax.axis_index("yh"), lax.axis_index("xh")

    packed = jnp.concatenate([w_query, w_keyvalue[0], w_keyvalue[1]], axis=1)
    dp_count = 8 * high * high
    w_in = lax.all_gather(packed, ROWS, axis=0, tiled=True)
    query_width = w_query.shape[1]
    kv_width = w_keyvalue.shape[2]
    normed_low = (hidden_in * inverse_root(hidden_in) * norm1_gain).astype(BF16)
    weights_o = (w_gate_up[0], w_down[0])
    weights_x = tuple(swap(w, "xl") for w in weights_o)
    weights_y = tuple(swap(w, "yl") for w in weights_o)
    w_out = share(w_output.T, "z", zs)
    seq_pieces = [normed_low, line_step(normed_low, zs)]
    w_out = lax.all_gather(w_out, ROWS, axis=0)
    seq_pieces.append(line_step(seq_pieces[1], zs))
    seq_pieces[2], w_in = tie(seq_pieces[2], w_in)
    seq_pieces.append(line_step(seq_pieces[2], zs))
    meta = jnp.concatenate([expert_ids.astype(F32).T, choice_scale.T], axis=0)
    grad_low, meta, seq_pieces[-1] = tie(out_grad.astype(BF16), meta, seq_pieces[-1])
    grad_first = line_step(grad_low, zs)
    meta_all = share(meta, ("yh", "xh", "core", "z"), high * high * 2 * zs)
    meta_all = meta_all.reshape((high * high, 2, zs) + meta.shape)
    meta_all = jnp.where(core == 1, meta_all[:, ::-1], meta_all)
    meta_all = jnp.stack(behind(jnp.moveaxis(meta_all, 2, 0), zs), axis=2)
    meta_all = meta_all.reshape((high * high, 2 * zs) + meta.shape)

    length = zs * tok_rows
    heads = query_width // HEAD
    groups = kv_width // HEAD
    places = lax.rem(z + zs - jnp.arange(zs, dtype=jnp.int32), zs)
    cosine, sine = rotary_tables(length)
    qkv = None
    for j, piece in enumerate(seq_pieces):
        qkv = project(places[j], piece, w_in, cosine, sine, query_width + kv_width, qkv)
    attended, lse = attend(qkv, heads, groups)
    attended = attended.reshape(zs, tok_rows, query_width)
    attended, grad_first = tie(attended, grad_first)
    attended_own = exchange(attended, "z")
    mask_all, scale_all = chosen_tables(
        meta_all[:, :, :pick_count], meta_all[:, :, pick_count:], expert_count
    )
    side = 2 * high
    numbers = []
    for dy, dx in ((0, 0), (0, 1), (1, 0), (1, 1)):
        chip = (yh * 2 + (yl ^ dy)) * side + xh * 2 + (xl ^ dx)
        numbers.append((chip * 2 + core) * zs + z)
    mine = jnp.stack(numbers)[None, :] == jnp.arange(expert_count)[:, None]
    mask_mine = jnp.any(mine[:, :, None] & mask_all[:, :, :, None], axis=2)
    earlier = (jnp.arange(tok_rows)[:, None] < jnp.arange(tok_rows)[None, :]).astype(BF16)
    rank = jnp.einsum(
        "gpes,st->gpet", mask_mine.astype(BF16), earlier, preferred_element_type=F32
    )
    place = jnp.where(mask_mine, rank, -1.0)
    place_of_token = jnp.where(
        mask_mine, rank + (jnp.arange(4, dtype=F32) * slots)[:, None], -1.0
    ).swapaxes(2, 3)

    tables = (place, place_of_token, mask_all.astype(F32), scale_all)
    attended_own, tables = tie(attended_own, tables)
    place, place_of_token, mask_low, scale_all = tables
    middle, normed_two_low = branch_norm(jnp.arange(zs), attended_own, w_out, hidden_in, norm2_gain)

    rows_pieces = [normed_two_low, line_step(normed_two_low, zs)]
    rows_pieces[1], *weights_d = tie(rows_pieces[1], *take_pieces(*weights_x, *weights_y))
    for step in range(3):
        weights_d[step] = swap(weights_d[step], "yl")
        weights_d[3 + step] = swap(weights_d[3 + step], "xl")
        if step < 2:
            rows_pieces.append(line_step(rows_pieces[-1], zs))
            rows_pieces[-1], weights_d[step], weights_d[3 + step] = tie(
                rows_pieces[-1], weights_d[step], weights_d[3 + step]
            )
    grad_first, rows_pieces[-1] = tie(grad_first, rows_pieces[-1])
    grad_next = line_step(grad_first, zs)
    rows_pieces = rows_pieces + [swap(piece, "core") for piece in rows_pieces]
    rows_pieces = spread(rows_pieces, sizes)
    *by_slot, gates = experts_forward(
        0,
        rows_pieces,
        place,
        (mask_low, scale_all, mine.astype(F32), w_router.T),
        (weights_o, weights_x, weights_y),
        slots,
    )
    by_slot[0], grad_next = tie(by_slot[0], grad_next)
    grad_last = line_step(grad_next, zs)
    out_slots, *saved = experts_forward(
        3, rows_pieces, place, (gates,), (weights_d,), slots, by_slot
    )
    out_order = ((0, 0), (0, 1), (0, 2), (0, 3))
    out_parts = [out_slots]

    def out_other(start, count):
        return combine(place_of_token, out_parts, out_order, slots, 1, start, count)

    def out_own(start, count, other):
        return only_own(
            combine(place_of_token, out_parts, out_order, slots, 0, start, count, other), sizes
        )

    out_near, out_far = out_other(1, 1), out_other(2, zs - 1)
    out_near, out_far, grad_last = swap(out_near, "core"), *tie(out_far, grad_last)
    out_far = swap(out_far, "core")
    (term,) = out_own(1, 1, out_near)
    grad_pieces = [grad_low, grad_first, grad_next, grad_last]
    grad_pieces = grad_pieces + [swap(piece, "core") for piece in grad_pieces]
    term, grad_pieces = tie(term, grad_pieces)
    grad_pieces = spread(grad_pieces, sizes)
    out_run = line_step(term, zs)
    rows_dx, gate_dx, *grads = experts_backward(
        3, grad_pieces, place, gates, saved, (weights_d, weights_x), slots
    )
    gd, gx = grads[:6], grads[6:]
    gd[0], gd[3] = swap(gd[0], "yl"), swap(gd[3], "xl")
    gd[1], gd[4] = swap(gd[1], "yl"), swap(gd[4], "xl")
    out_far, out_run, rows_dx = tie(out_far, out_run, rows_dx)
    out_terms = out_own(2, zs - 1, out_far)
    out_run, gates = tie(out_terms[0] + out_run, gates)
    out_run = line_step(out_run, zs)
    rows_yo, gate_yo, *grads = experts_backward(
        2, grad_pieces, place, gates, saved, (weights_y, weights_o), slots
    )
    gy, go = grads[:6], grads[6:]
    out_run, rows_yo, gd[0], gd[3], gd[1], gd[4] = tie(
        out_terms[1] + out_run, rows_yo, gd[0], gd[3], gd[1], gd[4]
    )
    gd[2], gd[5] = swap(gd[2], "yl"), swap(gd[5], "xl")
    moe_parts, moe_order = [rows_dx, rows_yo], ((1, 1), (0, 1), (1, 0), (0, 0))
    more = ((gate_dx, gate_yo), mine.astype(F32))

    def moe_other(start, count):
        return combine(place_of_token, moe_parts, moe_order, slots, 1, start, count, None, *more)

    def moe_own(start, count, other):
        return only_own(
            combine(place_of_token, moe_parts, moe_order, slots, 0, start, count, other, *more),
            sizes,
        )

    moe_near, moe_far = moe_other(1, 1), moe_other(2, zs - 1)
    moe_near, moe_far = swap(moe_near, "core"), swap(moe_far, "core")
    (term,) = moe_own(1, 1, moe_near)
    term, *moe_parts = tie(term, *moe_parts)
    moe_run = line_step(term, zs)
    moe_terms = moe_own(2, zs - 1, moe_far)
    moe_run, gd[2], gd[5] = tie(moe_terms[0] + moe_run, gd[2], gd[5])
    gx[3], gy[0] = swap(gx[3], "xl"), swap(gy[0], "yl")
    moe_run = line_step(moe_run, zs)
    moe_run, gx[3], gy[0] = tie(moe_terms[1] + moe_run, gx[3], gy[0])
    gx[4], gy[1] = swap(gx[4], "xl"), swap(gy[1], "yl")
    moe_run = line_step(moe_run, zs)

    mask_own, scale_own = chosen_tables(meta[:pick_count], meta[pick_count:], expert_count)
    logits_own = dot(w_router, normed_two_low, ((0,), (1,)))
    prob_own = masked_softmax(logits_own, mask_own, 0)
    unit = max(8, dp_count * zs * 128 // math.gcd(model_width, dp_count * zs * 128))
    sum_rows = -(-(expert_count + 2) // unit) * unit
    prob_own, scale_own, moe_terms[1] = tie(prob_own, scale_own, moe_terms[1])
    for i in range(3):
        gx[i], gy[3 + i] = gx[i] + gd[i], gy[3 + i] + gd[3 + i]
    moe_run, gx[4], gy[1], *both = tie(moe_run, gx[4], gy[1], *gx[:3], *gy[3:])
    gx[:3], gy[3:] = both[:3], both[3:]
    gx[5], gy[2] = swap(gx[5], "xl"), swap(gy[2], "yl")
    gx[0], gy[3] = swap(gx[0], "xl"), swap(gy[3], "yl")
    grad_middle, grad_branch, grad_attended, early_sums = moe_back(
        jnp.arange(zs),
        sum_rows,
        moe_terms[2],
        moe_run,
        prob_own,
        scale_own,
        w_router.T,
        normed_two_low,
        middle,
        norm2_gain,
        out_grad,
        w_out,
    )

    attended_rows = attended_own.transpose(1, 0, 2).reshape(tok_rows, zs * query_width)
    grad_w_out = dot(grad_branch, attended_rows, ((0,), (0,))).astype(BF16)
    shard_out = lax.psum_scatter(grad_w_out, ROWS, scatter_dimension=0, tiled=True)
    grad_attended = exchange(grad_attended, "z")
    out_run, grad_attended, _, gx[5], gy[2] = tie(
        out_run, grad_attended, grad_w_out, gx[5], gy[2]
    )
    gx[1], gy[4] = swap(gx[1], "xl"), swap(gy[4], "yl")
    out_run = line_step(out_run, zs)
    grad_proj = attend_back(
        qkv, lse, grad_attended.reshape(length, query_width), cosine, sine, heads, groups
    )
    out_run, grad_proj = tie(out_run, grad_proj)
    terms = [
        dot(g, w_in, ((1,), (1,))).astype(BF16)
        for g in behind(grad_proj.reshape(zs, tok_rows, -1), zs)
    ]
    terms[1], grad_proj = tie(terms[1], grad_proj)
    run = line_step(terms[1], zs)
    grad_w_in, gain_rows = project_back(places, seq_pieces, grad_proj, w_in)
    run, grad_w_in, gain_rows, gx[0], gy[3], *terms = tie(
        run, grad_w_in, gain_rows, gx[0], gy[3], *terms
    )
    gx[2], gy[5] = swap(gx[2], "xl"), swap(gy[5], "yl")
    run = line_step(terms[2] + run, zs)

    sums = lax.dynamic_update_slice(early_sums, gain_rows[:1], (expert_count + 1, 0))
    sums = sums.reshape(dp_count * zs, -1, 128)
    shard_out, grad_w_in = tie(shard_out, grad_w_in)
    shard_in = lax.psum_scatter(grad_w_in, ROWS, scatter_dimension=0, tiled=True)
    shard_out = shard_out.reshape(-1, zs, query_width).transpose(1, 0, 2)
    chunks = behind(shard_out, zs)
    for step in range(1, zs):
        chunks[step] = lax.ppermute(
            chunks[step], "z", [(i, (i + zs - step) % zs) for i in range(zs)]
        )
    sums = jnp.sum(exchange(sums, ALL), axis=0)
    output = middle + RESIDUAL_SCALE * (out_terms[2].astype(F32) + out_run.astype(F32))
    run, gx[1], gy[4], gx[2], gy[5], output, *chunks = tie(
        terms[3] + run, gx[1], gy[4], gx[2], gy[5], output, *chunks
    )
    run = line_step(run, zs)
    grad_w_gate_up, grad_w_down = collect(
        [(go[i], gx[i], gy[i]) for i in range(6)], model_width
    )

    sums, grad_w_gate_up, grad_w_down = tie(sums, grad_w_gate_up, grad_w_down)
    sums = share(sums, ALL, dp_count * zs)
    run, grad_w_gate_up, grad_w_down = tie(run, grad_w_gate_up, grad_w_down)
    grad_hidden = finish(terms[0], run, hidden_in, norm1_gain, grad_middle)
    grad_hidden, sums = tie(grad_hidden, sums)
    sums = sums.reshape(sum_rows, model_width)
    shard_output = sum(chunk.astype(F32) for chunk in chunks).T
    shard_query, shard_keyvalue = split_columns(shard_in, query_width)
    return (
        output,
        grad_hidden,
        sums[expert_count + 1] / norm1_gain,
        shard_query,
        shard_keyvalue,
        shard_output,
        sums[expert_count],
        sums[:expert_count].T,
        grad_w_gate_up,
        grad_w_down,
    )


def solution(mesh):
    high = math.isqrt(mesh.shape["dp"] // 2) // 2
    zs = mesh.shape["tensor"]
    inner = Mesh(mesh.devices.reshape(high, 2, high, 2, 2, zs), ALL)
    sizes = dict(inner.shape)
    in_specs = (
        P(ALL, None),
        P(),
        P(ROWS, "z"),
        P(None, ROWS, "z"),
        P("z", ROWS),
        P(),
        P(),
        P(ALL, None, None, None),
        P(ALL, None, None),
        P(ALL, None),
        P(ALL, None),
        P(ALL, None),
    )
    out_specs = (
        P(ALL, None),
        P(ALL, None),
        P(),
        P(ROWS, "z"),
        P(None, ROWS, "z"),
        P("z", ROWS),
        P(),
        P(),
        P(ALL, None, None, None),
        P(ALL, None, None),
    )
    return jax.shard_map(
        functools.partial(local, sizes),
        mesh=inner,
        in_specs=in_specs,
        out_specs=out_specs,
        check_vma=False,
    )
```

```python
import functools
import math

import jax
import jax.numpy as jnp
from jax import lax
from jax.experimental import pallas as pl
from jax.experimental.pallas import tpu as pltpu
from jax.sharding import Mesh
from jax.sharding import PartitionSpec as P

HEAD = 64
EPSILON = 1e-06
ATTN_SCALE = 0.015625
RESIDUAL_SCALE = 0.22
THETA = 10000.0
QUERY_BLOCK = 256
F32 = jnp.float32
BF16 = jnp.bfloat16
SWAP = [(0, 1), (1, 0)]
VMEM_LIMIT = 56 * 1024 * 1024


def lasts(microseconds):
    return pl.CostEstimate(
        flops=int(microseconds * 1.15e9), bytes_accessed=1, transcendentals=0
    )


ROWS = ("yh", "yl", "xh", "xl", "core")
ALL = ROWS + ("z",)


def swap(value, axis):
    return lax.ppermute(value, axis, SWAP)


def dot(a, b, dims):
    return lax.dot_general(a, b, (dims, ((), ())), preferred_element_type=F32)


def rotary_tables(length):
    half_width = HEAD // 2
    frequency = THETA ** (-2.0 * jnp.arange(half_width, dtype=F32) / HEAD)
    angles = jnp.arange(length, dtype=F32)[:, None] * frequency[None, :]
    cosine, sine = jnp.cos(angles), jnp.sin(angles)
    return jnp.tile(cosine, (1, 4)), jnp.tile(jnp.concatenate([-sine, sine], axis=1), (1, 2))


def line_step(value, size):
    return lax.ppermute(value, "z", [(i, (i + 1) % size) for i in range(size)])


def line_pieces(value, size, count=None):
    pieces = [value]
    for _ in range((count or size) - 1):
        pieces.append(line_step(pieces[-1], size))
    return pieces


def line_order(pieces):
    size = len(pieces)
    z = lax.axis_index("z")
    whole = jnp.zeros((size,) + pieces[0].shape, pieces[0].dtype)
    for step, piece in enumerate(pieces):
        whole = lax.dynamic_update_index_in_dim(whole, piece, lax.rem(z + size - step, size), 0)
    return whole


def tie(*values):
    return lax.optimization_barrier(values)


def behind(value, size):
    z = lax.axis_index("z")
    return [
        lax.dynamic_index_in_dim(value, lax.rem(z + size - j, size), 0, False) for j in range(size)
    ]


def spread(pieces, sizes):
    if sizes["yh"] == 1:
        return [piece[None] for piece in pieces]
    return [lax.all_gather(piece, ("yh", "xh"), axis=0, tiled=False) for piece in pieces]


def exchange(value, axes):
    return lax.all_to_all(value, axes, split_axis=0, concat_axis=0, tiled=True)


def share(value, axes, count):
    return exchange(jnp.broadcast_to(value[None], (count,) + value.shape), axes)


def one_hot(place_row, slots):
    rank = lax.broadcasted_iota(jnp.int32, (slots, place_row.shape[1]), 0).astype(F32)
    return jnp.where(rank == place_row, 1.0, 0.0)


def load_weights(sources, gate_up, down, sem):
    step, inner = pl.program_id(0), pl.program_id(1)
    block, half = gate_up.shape[2] // 2, gate_up.shape[3] // 2

    def pairs(k):
        slot = k % 2
        if len(sources[k]) == 2:
            yield sources[k][0], gate_up.at[slot]
            yield sources[k][1], down.at[slot]
            return
        for n, ref in enumerate(sources[k]):
            which, piece = divmod(n, 3)
            if piece == 2:
                yield ref, down.at[slot, pl.ds(which * half, half)]
            else:
                yield ref, gate_up.at[slot, which, pl.ds(piece * block, block)]

    def copies(k):
        for n, (source, target) in enumerate(pairs(k)):
            yield pltpu.make_async_copy(source, target, sem.at[k % 2, n])

    @pl.when((step == 0) & (inner == 0))
    def _():
        for copy in copies(0):
            copy.start()

    for k in range(len(sources)):

        @pl.when((step == k) & (inner == 0))
        def _(k=k):
            for copy in copies(k):
                copy.wait()
            if k + 1 < len(sources):
                for copy in copies(k + 1):
                    copy.start()


def sources_of(refs):
    sources, refs = [], list(refs)
    while refs:
        count = 2 if len(refs[0].shape) == 3 else 6
        sources.append(refs[:count])
        refs = refs[count:]
    return sources


def weight_scratch(width, hidden):
    return [
        pltpu.VMEM((2, 2, width, hidden), BF16),
        pltpu.VMEM((2, hidden, width), BF16),
        pltpu.SemaphoreType.DMA((2, 6)),
    ]


def slot_gates_of(picks, gate_ref, group, number):
    return jnp.concatenate(
        [
            jnp.sum(pick * gate_ref[group, j, pl.ds(number, 1), :], axis=1, keepdims=True)
            for j, pick in enumerate(picks)
        ],
        axis=0,
    )


def forward_kernel(pieces, slots, first, given, *refs):
    x_refs, refs = refs[:pieces], refs[pieces:]
    place_ref, refs = refs[0], refs[1:]
    if first == 0:
        mask_ref, scale_ref, mine_ref, router_ref = refs[:4]
        gate_ref = refs[4 + given + 5]
        weights, outs = sources_of(refs[4 : 4 + given]), refs[4 + given : 4 + given + 5]
    else:
        gate_ref = refs[0]
        weights, outs = sources_of(refs[6 : 6 + given]), refs[6 + given : 6 + given + 5]
    y_ref, xs_ref, dg_ref, du_ref, act_ref = outs
    gate_up, down, sem = refs[-3:]
    step, group = pl.program_id(0), pl.program_id(1)
    number = first + step
    load_weights(weights, gate_up, down, sem)

    if first == 0:

        @pl.when(step == 0)
        def _():
            for j in range(pieces):
                mask = mask_ref[group, j]
                logits = dot(router_ref[...], x_refs[j][0], ((1,), (1,)))
                logits = jnp.where(mask > 0.0, logits, -1e30)
                top = jnp.max(logits, axis=0, keepdims=True)
                exponent = jnp.where(mask > 0.0, jnp.exp(logits - top), 0.0)
                gates = exponent / jnp.sum(exponent, axis=0, keepdims=True) * scale_ref[group, j]
                for e in range(gate_ref.shape[2]):
                    gate_ref[group, j, e : e + 1] = jnp.sum(
                        gates * mine_ref[:, e : e + 1], axis=0, keepdims=True
                    )

    picks = [one_hot(place_ref[group, j, pl.ds(number, 1), :], slots) for j in range(pieces)]
    for j, pick in enumerate(picks):
        rows = dot(pick.astype(BF16), x_refs[j][0], ((1,), (0,)))
        xs_ref[0, j * slots : (j + 1) * slots] = rows.astype(BF16)
    slot_gate = slot_gates_of(picks, gate_ref, group, number)
    now = lax.rem(step, 2)
    x = xs_ref[0]
    gate = dot(x, gate_up[now, 0], ((1,), (0,)))
    up = dot(x, gate_up[now, 1], ((1,), (0,)))
    sigmoid = 1.0 / (1.0 + jnp.exp(-gate))
    silu = gate * sigmoid
    active = (silu * up).astype(BF16)
    act_ref[0] = active
    dg_ref[0] = (up * sigmoid * (1.0 + gate * (1.0 - sigmoid))).astype(BF16)
    du_ref[0] = silu.astype(BF16)
    weighted = (active.astype(F32) * slot_gate).astype(BF16)
    y_ref[0] = dot(weighted, down[now], ((1,), (0,))).astype(BF16)


def backward_kernel(pieces, slots, first, given, *refs):
    g_refs, refs = refs[:pieces], refs[pieces:]
    place_ref, gate_ref, xs_ref, dg_ref, du_ref, act_ref = refs[:6]
    weights, refs = sources_of(refs[6 : 6 + given]), refs[6 + given :]
    experts = len(weights)
    rows_ref, through_ref = refs[:2]
    results = [refs[2 + 6 * k : 8 + 6 * k] for k in range(experts)]
    gate_up, down, sem, gs_ref, stage, stage_down, out_sem = refs[2 + 6 * experts : 9 + 6 * experts]
    sums = refs[9 + 6 * experts :]
    step, group = pl.program_id(0), pl.program_id(1)
    number = first - 2 * step
    load_weights(weights, gate_up, down, sem)
    width = g_refs[0].shape[-1]
    half = down.shape[1] // 2
    now = lax.rem(step, 2)
    last = pl.num_programs(1) - 1

    def stores(k):
        block = width // 2
        for n, ref in enumerate(results[k]):
            which, piece = divmod(n, 3)
            source = stage_down.at[pl.ds(which * half, half)]
            if piece < 2:
                source = stage.at[which, pl.ds(piece * block, block)]
            yield pltpu.make_async_copy(source, ref, out_sem.at[n])

    picks = [one_hot(place_ref[group, j, pl.ds(number, 1), :], slots) for j in range(pieces)]
    for j, pick in enumerate(picks):
        rows = dot(pick.astype(BF16), g_refs[j][0], ((1,), (0,)))
        gs_ref[j * slots : (j + 1) * slots] = rows.astype(BF16)
    slot_gate = slot_gates_of(picks, gate_ref, group, number) * RESIDUAL_SCALE
    grad_active = dot(gs_ref[...], down[now], ((1,), (1,)))
    active = act_ref[0].astype(F32)
    through = jnp.sum(grad_active * active, axis=1, keepdims=True) * RESIDUAL_SCALE
    for j, pick in enumerate(picks):
        through_ref[0, j] = jnp.sum(
            pick * through[j * slots : (j + 1) * slots], axis=0, keepdims=True
        )
    grad_active = grad_active * slot_gate
    grad_gate = (grad_active * dg_ref[0].astype(F32)).astype(BF16)
    grad_up = (grad_active * du_ref[0].astype(F32)).astype(BF16)
    rows = dot(grad_gate, gate_up[now, 0], ((1,), (1,)))
    rows = rows + dot(grad_up, gate_up[now, 1], ((1,), (1,)))
    rows_ref[0] = rows.astype(BF16)
    weighted = (active * slot_gate).astype(BF16)

    for k in range(1, experts):

        @pl.when((step == k) & (group == last))
        def _(k=k):
            for copy in stores(k - 1):
                copy.wait()

    def add(target, total, left, right):
        part = dot(left, right, ((0,), (0,)))
        if total is None:
            target[...] = part.astype(BF16)
            return

        @pl.when(group == 0)
        def _():
            total[...] = part

        @pl.when(group > 0)
        def _():
            total[...] += part

        @pl.when(group == last)
        def _():
            target[...] = total[...].astype(BF16)

    x = xs_ref[0]
    totals = [sums[0].at[0], sums[0].at[1], sums[1]] if sums else [None] * 3
    add(stage.at[0], totals[0], x, grad_gate)
    add(stage.at[1], totals[1], x, grad_up)
    add(stage_down, totals[2], weighted, gs_ref[...])
    for k in range(experts):

        @pl.when((step == k) & (group == last))
        def _(k=k):
            for copy in stores(k):
                copy.start()
            if k == experts - 1:
                for copy in stores(k):
                    copy.wait()


def resident(arrays):
    return [
        pl.BlockSpec(a.shape, lambda e, c, n=a.ndim: (0,) * n, pipeline_mode=pl.Buffered(1))
        for a in arrays
    ]


def piece_spec(piece):
    groups, tokens, width = piece.shape
    mode = pl.Buffered(1) if groups == 1 else None
    return pl.BlockSpec((1, tokens, width), lambda e, c: (c, 0, 0), pipeline_mode=mode)


def experts_forward(first, x_pieces, place, tables, weights, slots, before=None):
    pieces = len(x_pieces)
    groups, tokens, width = x_pieces[0].shape
    hidden = weights[0][0].shape[-1]
    rows = pieces * slots
    experts = place.shape[2]
    anywhere = pl.BlockSpec(memory_space=pl.ANY)
    flat = [array for pair in weights for array in pair]
    before = list(before or [])

    def by_slot(n):
        return pl.BlockSpec((1, rows, n), lambda e, c: (first + e, c, 0))

    gate_shape = (groups, pieces, experts, tokens)
    widths = (width, width, hidden, hidden, hidden)
    out_specs = [by_slot(n) for n in widths]
    out_shape = [jax.ShapeDtypeStruct((experts, groups * rows, n), BF16) for n in widths]
    if first == 0:
        out_specs.append(pl.BlockSpec(gate_shape, lambda e, c: (0, 0, 0, 0)))
        out_shape.append(jax.ShapeDtypeStruct(gate_shape, F32))
    operands = [*x_pieces, place, *tables]
    return pl.pallas_call(
        functools.partial(forward_kernel, pieces, slots, first, len(flat)),
        grid=(len(weights), groups),
        in_specs=[piece_spec(p) for p in x_pieces]
        + resident([place, *tables])
        + [anywhere] * (len(before) + len(flat)),
        out_specs=out_specs,
        out_shape=out_shape,
        input_output_aliases={len(operands) + n: n for n in range(len(before))},
        scratch_shapes=weight_scratch(width, hidden),
        compiler_params=pltpu.CompilerParams(vmem_limit_bytes=VMEM_LIMIT),
        cost_estimate=lasts(8.0 * len(weights)),
        name="experts_forward",
    )(*operands, *before, *flat)


def experts_backward(first, g_pieces, place, gates, saved, weights, slots):
    pieces = len(g_pieces)
    groups, tokens, width = g_pieces[0].shape
    experts = len(weights)
    hidden = weights[0][0].shape[-1]
    rows = pieces * slots
    flat = [array for pair in weights for array in pair]

    def by_slot(n):
        return pl.BlockSpec((1, rows, n), lambda e, c: (first - 2 * e, c, 0))

    anywhere = pl.BlockSpec(memory_space=pl.ANY)
    block = jax.ShapeDtypeStruct((width // 2, hidden), BF16)
    return pl.pallas_call(
        functools.partial(backward_kernel, pieces, slots, first, len(flat)),
        grid=(experts, groups),
        in_specs=[piece_spec(p) for p in g_pieces]
        + resident([place, gates])
        + [by_slot(width)]
        + [by_slot(hidden)] * 3
        + [anywhere] * len(flat),
        out_specs=[
            pl.BlockSpec((1, rows, width), lambda e, c: (e, c, 0)),
            pl.BlockSpec((1, pieces, 1, tokens), lambda e, c: (e, c, 0, 0)),
        ]
        + [anywhere] * (6 * experts),
        out_shape=[
            jax.ShapeDtypeStruct((experts, groups * rows, width), BF16),
            jax.ShapeDtypeStruct((experts, groups * pieces, 1, tokens), F32),
        ]
        + [block, block, jax.ShapeDtypeStruct((hidden // 2, width), BF16)] * (2 * experts),
        scratch_shapes=weight_scratch(width, hidden)
        + [
            pltpu.VMEM((rows, width), BF16),
            pltpu.VMEM((2, width, hidden), BF16),
            pltpu.VMEM((hidden, width), BF16),
            pltpu.SemaphoreType.DMA((6,)),
        ]
        + (
            [pltpu.VMEM((2, width, hidden), F32), pltpu.VMEM((hidden, width), F32)]
            if groups > 1
            else []
        ),
        compiler_params=pltpu.CompilerParams(vmem_limit_bytes=VMEM_LIMIT),
        cost_estimate=lasts(14.5 * experts),
        name="experts_backward",
    )(*g_pieces, place, gates, *saved, *flat)


def extra_rows(expert_count, tokens, width):
    return 16 * -(-(-(-2 * expert_count // 16)) // (width // tokens))


def extra_places(expert_count, tokens, width):
    across = width // tokens
    for block in range(-(-2 * expert_count // 16)):
        yield block, 16 * (block // across), tokens * (block % across)


def combine_kernel(order, slots, extra, pieces, place_ref, *refs):
    parts = 1 + max(which for which, _ in order)
    experts = len(order)
    rows_refs, refs = refs[:parts], refs[parts:]
    if extra:
        through_refs, mine_ref, refs = refs[:parts], refs[parts], refs[parts + 1 :]
    step = pl.program_id(0)
    tokens = place_ref.shape[1]
    lane = lax.broadcasted_iota(jnp.int32, (tokens, experts * slots), 1).astype(F32)
    hit = lane == place_ref[0, :, 0:1]
    for e in range(1, experts):
        hit = hit | (lane == place_ref[0, :, e : e + 1])
    pick = jnp.where(hit, 1.0, 0.0).astype(BF16)
    rows = jnp.concatenate([rows_refs[which][k] for which, k in order], axis=0)
    out = dot(pick, rows, ((1,), (0,)))
    width = out.shape[1]
    more = None
    if extra:
        dense = 0.0
        for e, (which, k) in enumerate(order):
            dense = dense + mine_ref[:, e : e + 1] * through_refs[which][k, 0]
        high = dense.astype(BF16).astype(F32)
        both = jnp.concatenate([high, dense - high], axis=0)
        across = width // tokens
        lines = []
        for start in range(0, both.shape[0], 16 * across):
            line = [both[i : i + 16] for i in range(start, min(start + 16 * across, both.shape[0]), 16)]
            line += [jnp.zeros((16, tokens), F32)] * (across - len(line))
            lines.append(jnp.concatenate(line, axis=1))
        more = jnp.concatenate(lines, axis=0)

    def store(ref):
        if not pieces:
            ref[0, :tokens] = out.astype(BF16)
            if extra:
                ref[0, tokens:] = more.astype(BF16)
            return
        ref[0, :tokens] = (out + refs[0][0, :tokens].astype(F32)).astype(BF16)
        if extra:
            ref[0, tokens:] = (more + refs[0][0, tokens:].astype(F32)).astype(BF16)

    if not pieces:
        store(refs[0])
        return
    for j in range(pieces):

        @pl.when(lax.rem(step, pieces) == j)
        def _(j=j):
            store(refs[1 + j])


def combine(place, parts, order, slots, half, start, count, other=None, through=None, mine=None):
    groups, pieces, tokens, experts = place.shape
    column = pieces // 2
    width = parts[0].shape[-1]
    extra = 0 if through is None else extra_rows(mine.shape[0], tokens, width)

    def at(i):
        return (i // count) * pieces + half * column + (start + i % count) % column

    in_specs = [pl.BlockSpec((1, tokens, experts), lambda i: (at(i), 0, 0))]
    in_specs += [pl.BlockSpec((p.shape[0], slots, width), lambda i: (0, at(i), 0)) for p in parts]
    operands = [place.reshape(groups * pieces, tokens, experts), *parts]
    if extra:
        in_specs += [
            pl.BlockSpec((t.shape[0], 1, 1, tokens), lambda i: (0, at(i), 0, 0)) for t in through
        ]
        in_specs.append(pl.BlockSpec(mine.shape, lambda i: (0, 0)))
        operands += [*through, mine]
    rows = tokens + extra
    by_step = pl.BlockSpec((1, rows, width), lambda i: (i, 0, 0))
    if other is None:
        out_specs, out_shape = by_step, jax.ShapeDtypeStruct((groups * count, rows, width), BF16)
    else:
        in_specs.append(by_step)
        operands.append(other)
        out_specs = [pl.BlockSpec((1, rows, width), lambda i: (i // count, 0, 0))] * count
        out_shape = [jax.ShapeDtypeStruct((groups, rows, width), BF16)] * count
    return pl.pallas_call(
        functools.partial(combine_kernel, order, slots, extra, 0 if other is None else count),
        grid=(groups * count,),
        in_specs=in_specs,
        out_specs=out_specs,
        out_shape=out_shape,
        compiler_params=pltpu.CompilerParams(vmem_limit_bytes=VMEM_LIMIT),
        cost_estimate=lasts(0.1),
        name="combine",
    )(*operands)


def only_own(terms, sizes):
    if sizes["yh"] == 1:
        return [term[0] for term in terms]
    return [
        lax.psum_scatter(term, ("yh", "xh"), scatter_dimension=0, tiled=True)[0] for term in terms
    ]


def packed_specs(width, hidden):
    block = width // 2
    return (
        pl.BlockSpec((1, 1, block, hidden), lambda h, i: (0, h, jnp.minimum(i, 1), 0)),
        pl.BlockSpec((1, hidden // 2, width), lambda h, i: (0, h, 0)),
    )


def take_kernel(gate_ref, down_a_ref, up_ref, down_b_ref, *out_refs):
    step = pl.program_id(0)
    for n in (0, 1):

        @pl.when(step == n)
        def _(n=n):
            out_refs[n][...] = gate_ref[0]
            out_refs[3 + n][...] = up_ref[0]

    @pl.when(step == 2)
    def _():
        out_refs[2][...] = down_a_ref[...]
        out_refs[5][...] = down_b_ref[...]


def take_pieces(gate_up_x, down_x, gate_up_y, down_y):
    _, width, hidden = gate_up_x.shape
    block, half = width // 2, hidden // 2

    def specs(which):
        return [
            pl.BlockSpec((1, block, hidden), lambda i: (which, jnp.minimum(i, 1), 0)),
            pl.BlockSpec((half, width), lambda i: (which, 0)),
        ]

    shapes = [(block, hidden), (block, hidden), (half, width)] * 2
    return pl.pallas_call(
        take_kernel,
        grid=(3,),
        in_specs=specs(0) + specs(1),
        out_specs=[pl.BlockSpec(shape, lambda i: (0, 0)) for shape in shapes],
        out_shape=[jax.ShapeDtypeStruct(shape, BF16) for shape in shapes],
        compiler_params=pltpu.CompilerParams(vmem_limit_bytes=VMEM_LIMIT),
        cost_estimate=lasts(4.0),
        name="take_pieces",
    )(gate_up_x, down_x, gate_up_y, down_y)


def collect_kernel(*refs):
    gate_up_ref, down_ref, wide, deep, sem = refs[-5:]
    step = pl.program_id(0) * 3 + pl.program_id(1)

    def slot(n):
        return deep.at[n // 3] if n % 3 == 2 else wide.at[n % 3]

    def copies(n):
        for k in range(3):
            yield pltpu.make_async_copy(refs[3 * n + k], slot(n).at[k], sem.at[n, k])

    @pl.when(step == 0)
    def _():
        for n in (0, 1, 2, 5):
            for copy in copies(n):
                copy.start()

    for n in range(6):

        @pl.when(step == n)
        def _(n=n):
            for copy in copies(n):
                copy.wait()
            here = slot(n)
            total = here[0].astype(F32) + here[1].astype(F32) + here[2].astype(F32)
            if n % 3 < 2:
                gate_up_ref[0, 0] = total
            else:
                down_ref[0] = total
            if n < 2:
                for copy in copies(n + 3):
                    copy.start()


def collect(pieces, width):
    hidden = pieces[0][0].shape[1]
    gate_up_spec, down_spec = packed_specs(width, hidden)
    return pl.pallas_call(
        collect_kernel,
        grid=(2, 3),
        in_specs=[pl.BlockSpec(memory_space=pl.ANY)] * 18,
        out_specs=[gate_up_spec, down_spec],
        out_shape=[
            jax.ShapeDtypeStruct((1, 2, width, hidden), F32),
            jax.ShapeDtypeStruct((1, hidden, width), F32),
        ],
        scratch_shapes=[
            pltpu.VMEM((2, 3, width // 2, hidden), BF16),
            pltpu.VMEM((2, 3, hidden // 2, width), BF16),
            pltpu.SemaphoreType.DMA((6, 3)),
        ],
        compiler_params=pltpu.CompilerParams(vmem_limit_bytes=VMEM_LIMIT),
        cost_estimate=lasts(9.5),
        name="collect",
    )(*[array for piece in pieces for array in piece])


def inverse_root(values):
    return lax.rsqrt(jnp.mean(values * values, axis=-1, keepdims=True) + EPSILON)


def branch_kernel(place_ref, att_ref, w_ref, hidden_ref, gain_ref, middle_ref, low_ref):
    step = pl.program_id(0)
    weights = w_ref[:, 0].reshape(hidden_ref.shape[1], w_ref.shape[-1])
    part = RESIDUAL_SCALE * dot(att_ref[0], weights, ((1,), (1,)))

    @pl.when(step == 0)
    def _():
        middle_ref[...] = hidden_ref[...] + part

    @pl.when(step > 0)
    def _():
        middle_ref[...] += part

    @pl.when(step == pl.num_programs(0) - 1)
    def _():
        middle = middle_ref[...]
        low_ref[...] = (middle * inverse_root(middle) * gain_ref[...]).astype(BF16)


def out_weights_spec(weights):
    rows, _, height, columns = weights.shape
    return pl.BlockSpec((rows, 1, height, columns), lambda i, p: (0, i, 0, 0))


def branch_norm(places, attended, weights, hidden, gain):
    count, tokens, columns = attended.shape
    width = hidden.shape[1]
    return pl.pallas_call(
        branch_kernel,
        grid_spec=pltpu.PrefetchScalarGridSpec(
            num_scalar_prefetch=1,
            grid=(count,),
            in_specs=[
                pl.BlockSpec((1, tokens, columns), lambda i, p: (p[i], 0, 0)),
                out_weights_spec(weights),
                pl.BlockSpec((tokens, width), lambda i, p: (0, 0)),
                pl.BlockSpec((1, width), lambda i, p: (0, 0)),
            ],
            out_specs=[pl.BlockSpec((tokens, width), lambda i, p: (0, 0))] * 2,
        ),
        out_shape=[
            jax.ShapeDtypeStruct((tokens, width), F32),
            jax.ShapeDtypeStruct((tokens, width), BF16),
        ],
        compiler_params=pltpu.CompilerParams(vmem_limit_bytes=VMEM_LIMIT),
        cost_estimate=lasts(7.0),
        name="branch_norm",
    )(places, attended, weights, hidden, gain.reshape(1, width))


def moe_back_kernel(
    extra, place_ref, own_ref, run_ref, prob_ref, scale_ref, router_ref, low_ref, middle_ref, gain_ref, grad_ref, w_ref,
    grad_middle_ref, branch_ref, attended_ref, sums_ref,
):
    tokens = middle_ref.shape[0]

    @pl.when(pl.program_id(0) == 0)
    def _():
        experts = prob_ref.shape[0]

        def total(rows, columns=slice(None)):
            return own_ref[rows, columns].astype(F32) + run_ref[rows, columns].astype(F32)

        both = jnp.concatenate(
            [
                total(slice(tokens + row, tokens + row + 16), slice(column, column + tokens))
                for _, row, column in extra
            ],
            axis=0,
        )
        scaled = (both[:experts] + both[experts : 2 * experts]) * scale_ref[...]
        prob = prob_ref[...]
        chosen = prob * (scaled - jnp.sum(prob * scaled, axis=0, keepdims=True))
        chosen = chosen.astype(BF16)
        sums_ref[:experts] = dot(chosen, low_ref[...], ((1,), (0,)))
        grad = total(slice(0, tokens)) + dot(chosen, router_ref[...], ((0,), (0,)))
        middle = middle_ref[...]
        inverse = inverse_root(middle)
        scaled = middle * inverse
        sums_ref[experts:] = jnp.zeros((sums_ref.shape[0] - experts, middle.shape[1]), F32)
        sums_ref[experts : experts + 1] = jnp.sum(grad * scaled, axis=0, keepdims=True)
        grad = grad * gain_ref[...]
        mean = jnp.mean(grad * scaled, axis=-1, keepdims=True)
        grad = grad_ref[...] + inverse * (grad - scaled * mean)
        grad_middle_ref[...] = grad
        branch_ref[...] = (RESIDUAL_SCALE * grad).astype(BF16)

    weights = w_ref[:, 0].reshape(middle_ref.shape[1], w_ref.shape[-1])
    attended_ref[0] = dot(branch_ref[...], weights, ((1,), (0,))).astype(BF16)


def moe_back(places, rows, own, run, prob, scale, router, low, middle, gain, grad, weights):
    tokens, width = middle.shape
    experts = prob.shape[0]
    _, count, _, columns = weights.shape
    extra = list(extra_places(experts, tokens, width))
    operands = [own, run, prob, scale, router, low, middle, gain.reshape(1, width), grad]
    return pl.pallas_call(
        functools.partial(moe_back_kernel, extra),
        grid_spec=pltpu.PrefetchScalarGridSpec(
            num_scalar_prefetch=1,
            grid=(count,),
            in_specs=[pl.BlockSpec(a.shape, lambda i, p: (0, 0)) for a in operands]
            + [out_weights_spec(weights)],
            out_specs=[
                pl.BlockSpec((tokens, width), lambda i, p: (0, 0)),
                pl.BlockSpec((tokens, width), lambda i, p: (0, 0)),
                pl.BlockSpec((1, tokens, columns), lambda i, p: (p[i], 0, 0)),
                pl.BlockSpec((rows, width), lambda i, p: (0, 0)),
            ],
        ),
        out_shape=[
            jax.ShapeDtypeStruct((tokens, width), F32),
            jax.ShapeDtypeStruct((tokens, width), BF16),
            jax.ShapeDtypeStruct((count, tokens, columns), BF16),
            jax.ShapeDtypeStruct((rows, width), F32),
        ],
        compiler_params=pltpu.CompilerParams(vmem_limit_bytes=VMEM_LIMIT),
        cost_estimate=lasts(20.0),
        name="moe_back",
    )(places, *operands, weights)


def split_kernel(value_ref, first_ref, rest_ref):
    value = value_ref[...].astype(F32)
    cut, each = first_ref.shape[1], rest_ref.shape[2]
    first_ref[...] = value[:, :cut]
    for k in (0, 1):
        rest_ref[k] = value[:, cut + k * each : cut + (k + 1) * each]


def split_columns(value, cut):
    rows, columns = value.shape
    return pl.pallas_call(
        split_kernel,
        out_shape=[
            jax.ShapeDtypeStruct((rows, cut), F32),
            jax.ShapeDtypeStruct((2, rows, (columns - cut) // 2), F32),
        ],
        cost_estimate=lasts(1.0),
        name="split_columns",
    )(value)


def product_kernel(rows_ref, block_ref, out_ref):
    out_ref[...] = dot(rows_ref[...], block_ref[0], ((0,), (0,))).astype(BF16)


def product_by_blocks(rows, blocks):
    tokens, width = rows.shape
    count, _, columns = blocks.shape
    return pl.pallas_call(
        product_kernel,
        grid=(count,),
        in_specs=[
            pl.BlockSpec((tokens, width), lambda i: (0, 0)),
            pl.BlockSpec((1, tokens, columns), lambda i: (i, 0, 0)),
        ],
        out_specs=pl.BlockSpec((width, columns), lambda i: (0, i)),
        out_shape=jax.ShapeDtypeStruct((width, count * columns), BF16),
        compiler_params=pltpu.CompilerParams(vmem_limit_bytes=VMEM_LIMIT),
        cost_estimate=lasts(15.0),
        name="product_by_blocks",
    )(rows, blocks)


def finish_kernel(own_ref, run_ref, hidden_ref, gain_ref, grad_ref, out_ref):
    grad = own_ref[...].astype(F32) + run_ref[...].astype(F32)
    hidden = hidden_ref[...]
    inverse = inverse_root(hidden)
    scaled = hidden * inverse
    grad = grad * gain_ref[...]
    mean = jnp.mean(grad * scaled, axis=-1, keepdims=True)
    out_ref[...] = grad_ref[...] + inverse * (grad - scaled * mean)


def finish(own, run, hidden, gain, grad):
    tokens, width = hidden.shape
    rows = pl.BlockSpec((tokens // 2, width), lambda i: (i, 0))
    return pl.pallas_call(
        finish_kernel,
        grid=(2,),
        in_specs=[rows, rows, rows, pl.BlockSpec((1, width), lambda i: (0, 0)), rows],
        out_specs=rows,
        out_shape=jax.ShapeDtypeStruct((tokens, width), F32),
        compiler_params=pltpu.CompilerParams(vmem_limit_bytes=VMEM_LIMIT),
        cost_estimate=lasts(3.5),
        name="finish",
    )(own, run, hidden, gain.reshape(1, width), grad)


def causal_mask(scores, start):
    keys, columns = scores.shape
    block = keys - start
    key = lax.broadcasted_iota(jnp.int32, (block, columns), 0)
    query = lax.rem(lax.broadcasted_iota(jnp.int32, (block, columns), 1), block)
    low = jnp.where(key <= query, scores[start:], -1e30)
    return low if start == 0 else jnp.concatenate([scores[:start], low], axis=0)


def head_rows(pair, odd):
    lane = lax.broadcasted_iota(jnp.int32, pair.shape, 1)
    return jnp.where((lane >= HEAD) == odd, pair, jnp.zeros_like(pair))


def both_halves(rows):
    return jnp.concatenate([rows, rows], axis=1)


def attend_kernel(heads, groups, block, qkv_ref, out_ref, lse_ref):
    length = qkv_ref.shape[0]
    each = heads // groups
    at_key = heads * HEAD
    at_value = at_key + groups * HEAD
    for i in range(length // block):
        start, stop = i * block, (i + 1) * block
        parts = []
        for g in range(groups):
            key = both_halves(qkv_ref[:stop, at_key + g * HEAD : at_key + (g + 1) * HEAD])
            value = qkv_ref[:stop, at_value + g * HEAD : at_value + (g + 1) * HEAD]
            query = []
            for h in range(g * each, (g + 1) * each):
                pair = qkv_ref[start:stop, h // 2 * 2 * HEAD : (h // 2 + 1) * 2 * HEAD]
                query.append(head_rows(pair, h % 2 == 1) * ATTN_SCALE)
            query = jnp.concatenate(query, axis=0).astype(BF16)
            scores = causal_mask(dot(key, query, ((1,), (1,))), start)
            top = jnp.max(scores, axis=0, keepdims=True)
            exponent = jnp.exp(scores - top)
            norm = jnp.sum(exponent, axis=0, keepdims=True)
            total = top + jnp.log(norm)
            out = dot(value, exponent.astype(BF16), ((0,), (0,))) / norm
            for k in range(each):
                columns = slice(k * block, (k + 1) * block)
                lse_ref[g * each + k : g * each + k + 1, start:stop] = total[:, columns]
                parts.append(out[:, columns])
        for pair in range(heads // 2):
            rows = jnp.concatenate(parts[2 * pair : 2 * pair + 2], axis=0)
            out_ref[start:stop, pair * 2 * HEAD : (pair + 1) * 2 * HEAD] = rows.T.astype(BF16)


def attend(qkv, heads, groups):
    length = qkv.shape[0]
    return pl.pallas_call(
        functools.partial(attend_kernel, heads, groups, min(QUERY_BLOCK, length)),
        out_shape=[
            jax.ShapeDtypeStruct((length, heads * HEAD), BF16),
            jax.ShapeDtypeStruct((8 * -(-heads // 8), length), F32),
        ],
        compiler_params=pltpu.CompilerParams(vmem_limit_bytes=VMEM_LIMIT),
        cost_estimate=lasts(8.0),
        name="attend",
    )(qkv)


def turn(values, cosine, sine, direction):
    width = values.shape[1]
    lane = lax.broadcasted_iota(jnp.int32, values.shape, 1)
    first = lax.rem(lane, HEAD) < HEAD // 2
    behind_half = pltpu.roll(values, width - HEAD // 2, 1)
    other = jnp.where(first, behind_half, pltpu.roll(values, HEAD // 2, 1))
    repeats = width // cosine.shape[1]
    cosine = jnp.concatenate([cosine] * repeats, axis=1) if repeats > 1 else cosine
    sine = jnp.concatenate([sine] * repeats, axis=1) if repeats > 1 else sine
    return values * cosine + direction * (other * sine)


def attend_back_kernel(
    heads, groups, block, qkv_ref, lse_ref, grad_ref, cos_ref, sin_ref, out_ref, key_sum, value_sum
):
    length = qkv_ref.shape[0]
    each = heads // groups
    at_key = heads * HEAD
    at_value = at_key + groups * HEAD
    for i in reversed(range(length // block)):
        start, stop = i * block, (i + 1) * block
        parts = []
        for g in range(groups):
            key = qkv_ref[:stop, at_key + g * HEAD : at_key + (g + 1) * HEAD]
            value = both_halves(qkv_ref[:stop, at_value + g * HEAD : at_value + (g + 1) * HEAD])
            query, grad, lse = [], [], []
            for h in range(g * each, (g + 1) * each):
                columns = slice(h // 2 * 2 * HEAD, (h // 2 + 1) * 2 * HEAD)
                query.append(head_rows(qkv_ref[start:stop, columns], h % 2 == 1) * ATTN_SCALE)
                grad.append(head_rows(grad_ref[start:stop, columns], h % 2 == 1))
                lse.append(lse_ref[h : h + 1, start:stop])
            query = jnp.concatenate(query, axis=0).astype(BF16)
            grad = jnp.concatenate(grad, axis=0)
            lse = jnp.concatenate(lse, axis=1)
            scores = causal_mask(dot(both_halves(key), query, ((1,), (1,))), start)
            probs = jnp.exp(scores - lse)
            grad_probs = dot(value, grad, ((1,), (1,)))
            weighted = probs * grad_probs
            delta = jnp.sum(weighted, axis=0, keepdims=True)
            grad_scores = (weighted - probs * delta).astype(BF16)
            grad_value = dot(probs.astype(BF16), grad, ((1,), (0,)))
            grad_key = dot(grad_scores, query, ((1,), (0,)))
            if stop == length:
                value_sum[g] = grad_value
                key_sum[g] = grad_key
            else:
                value_sum[g, :stop] += grad_value
                key_sum[g, :stop] += grad_key
            grad_query = dot(key, grad_scores, ((0,), (0,))) * ATTN_SCALE
            for k in range(each):
                parts.append(grad_query[:, k * block : (k + 1) * block])
        cosine, sine = cos_ref[start:stop], sin_ref[start:stop]
        for pair in range(heads // 2):
            rows = jnp.concatenate(parts[2 * pair : 2 * pair + 2], axis=0).T
            rows = turn(rows, cosine, sine, -1.0).astype(BF16)
            out_ref[start:stop, pair * 2 * HEAD : (pair + 1) * 2 * HEAD] = rows
    rows = [key_sum[g][:, :HEAD] + key_sum[g][:, HEAD:] for g in range(groups)]
    rows = turn(jnp.concatenate(rows, axis=1), cos_ref[...], sin_ref[...], -1.0)
    out_ref[:, at_key:at_value] = rows.astype(BF16)
    rows = [value_sum[g][:, :HEAD] + value_sum[g][:, HEAD:] for g in range(groups)]
    out_ref[:, at_value:] = jnp.concatenate(rows, axis=1).astype(BF16)


def attend_back(qkv, lse, grad, cosine, sine, heads, groups):
    length = qkv.shape[0]
    return pl.pallas_call(
        functools.partial(attend_back_kernel, heads, groups, min(QUERY_BLOCK, length)),
        out_shape=jax.ShapeDtypeStruct(qkv.shape, BF16),
        scratch_shapes=[pltpu.VMEM((groups, length, 2 * HEAD), F32)] * 2,
        compiler_params=pltpu.CompilerParams(vmem_limit_bytes=VMEM_LIMIT),
        cost_estimate=lasts(14.0),
        name="attend_back",
    )(qkv, lse, grad, cosine, sine)


def project_kernel(turned, place_ref, x_ref, w_ref, cos_ref, sin_ref, *refs):
    out_ref = refs[-1]
    values = dot(x_ref[...], w_ref[...], ((1,), (0,)))
    out_ref[:, :turned] = turn(values[:, :turned], cos_ref[...], sin_ref[...], 1.0).astype(BF16)
    out_ref[:, turned:] = values[:, turned:].astype(BF16)


def project(place, rows, weights, cosine, sine, turned, before=None):
    tokens, width = rows.shape
    columns = weights.shape[1]
    in_specs = [
        pl.BlockSpec((tokens, width), lambda i, p: (0, 0)),
        pl.BlockSpec((width, columns), lambda i, p: (0, 0)),
        pl.BlockSpec((tokens, cosine.shape[1]), lambda i, p: (p[0], 0)),
        pl.BlockSpec((tokens, sine.shape[1]), lambda i, p: (p[0], 0)),
    ]
    operands = [place.reshape(1), rows, weights, cosine, sine]
    if before is not None:
        in_specs.append(pl.BlockSpec(memory_space=pl.ANY))
        operands.append(before)
    return pl.pallas_call(
        functools.partial(project_kernel, turned),
        grid_spec=pltpu.PrefetchScalarGridSpec(
            num_scalar_prefetch=1,
            grid=(1,),
            in_specs=in_specs,
            out_specs=pl.BlockSpec((tokens, columns), lambda i, p: (p[0], 0)),
        ),
        out_shape=jax.ShapeDtypeStruct((cosine.shape[0], columns), BF16),
        input_output_aliases={} if before is None else {5: 0},
        compiler_params=pltpu.CompilerParams(vmem_limit_bytes=VMEM_LIMIT),
        cost_estimate=lasts(4.0),
        name="project",
    )(*operands)


def project_back_kernel(pieces, place_ref, *refs):
    x_refs = refs[:pieces]
    grad_ref, w_ref, out_ref, gain_ref = refs[pieces:]
    tokens = x_refs[0].shape[0]
    grad = 0.0
    for j in range(pieces):
        start = pl.multiple_of(place_ref[j] * tokens, tokens)
        grad = grad + dot(x_refs[j][...], grad_ref[pl.ds(start, tokens), :], ((0,), (0,)))
    out_ref[...] = grad.astype(BF16)
    ones = jnp.ones((8, w_ref.shape[1]), BF16)
    products = w_ref[...].astype(F32) * grad
    high = products.astype(BF16)
    low = (products - high.astype(F32)).astype(BF16)
    gain_ref[...] = dot(ones, high, ((1,), (1,))) + dot(ones, low, ((1,), (1,)))


def project_back(places, pieces, grad, weights):
    tokens, width = pieces[0].shape
    columns = weights.shape[1]
    cut = width // 3
    return pl.pallas_call(
        functools.partial(project_back_kernel, len(pieces)),
        grid_spec=pltpu.PrefetchScalarGridSpec(
            num_scalar_prefetch=1,
            grid=(3,),
            in_specs=[pl.BlockSpec((tokens, cut), lambda i, p: (0, i))] * len(pieces)
            + [
                pl.BlockSpec(grad.shape, lambda i, p: (0, 0)),
                pl.BlockSpec((cut, columns), lambda i, p: (i, 0)),
            ],
            out_specs=[
                pl.BlockSpec((cut, columns), lambda i, p: (i, 0)),
                pl.BlockSpec((8, cut), lambda i, p: (0, i)),
            ],
        ),
        out_shape=[
            jax.ShapeDtypeStruct((width, columns), BF16),
            jax.ShapeDtypeStruct((8, width), F32),
        ],
        compiler_params=pltpu.CompilerParams(vmem_limit_bytes=VMEM_LIMIT),
        cost_estimate=lasts(9.0),
        name="project_back",
    )(places, *pieces, grad, weights)


def chosen_tables(ids, scale, expert_count):
    lead = (1,) * (ids.ndim - 2)
    numbers = jnp.arange(expert_count, dtype=F32).reshape(lead + (1, expert_count, 1))
    hits = ids[..., :, None, :] == numbers
    mask = jnp.any(hits, axis=-3)
    return mask, jnp.sum(jnp.where(hits, scale[..., :, None, :], 0.0), axis=-3)


def masked_softmax(logits, mask, axis):
    top = jnp.max(jnp.where(mask, logits, -jnp.inf), axis=axis, keepdims=True)
    exponent = jnp.where(mask, jnp.exp(jnp.where(mask, logits - top, 0.0)), 0.0)
    return exponent / jnp.sum(exponent, axis=axis, keepdims=True)


def local(
    sizes,
    hidden_in,
    norm1_gain,
    w_query,
    w_keyvalue,
    w_output,
    norm2_gain,
    w_router,
    w_gate_up,
    w_down,
    expert_ids,
    choice_scale,
    out_grad,
):
    tok_rows, model_width = hidden_in.shape
    pick_count = expert_ids.shape[1]
    expert_count = w_router.shape[1]
    capacity = max(2, (tok_rows * pick_count * 11 + 8 * expert_count - 1) // (8 * expert_count))
    slots = -(-capacity // 16) * 16
    zs, high = sizes["z"], sizes["yh"]
    yl, xl, core, z = (lax.axis_index(a) for a in ("yl", "xl", "core", "z"))
    yh, xh = lax.axis_index("yh"), lax.axis_index("xh")

    packed = jnp.concatenate([w_query, w_keyvalue[0], w_keyvalue[1]], axis=1)
    dp_count = 8 * high * high
    w_in = lax.all_gather(packed, ROWS, axis=0, tiled=True)
    query_width = w_query.shape[1]
    kv_width = w_keyvalue.shape[2]
    normed_low = (hidden_in * inverse_root(hidden_in) * norm1_gain).astype(BF16)
    weights_o = (w_gate_up[0], w_down[0])
    weights_x = tuple(swap(w, "xl") for w in weights_o)
    weights_y = tuple(swap(w, "yl") for w in weights_o)
    w_out = share(w_output.T, "z", zs)
    seq_pieces = [normed_low, line_step(normed_low, zs)]
    w_out = lax.all_gather(w_out, ROWS, axis=0)
    seq_pieces.append(line_step(seq_pieces[1], zs))
    seq_pieces[2], w_in = tie(seq_pieces[2], w_in)
    seq_pieces.append(line_step(seq_pieces[2], zs))
    meta = jnp.concatenate([expert_ids.astype(F32).T, choice_scale.T], axis=0)
    grad_low, meta, seq_pieces[-1] = tie(out_grad.astype(BF16), meta, seq_pieces[-1])
    grad_first = line_step(grad_low, zs)
    meta_all = share(meta, ("yh", "xh", "core", "z"), high * high * 2 * zs)
    meta_all = meta_all.reshape((high * high, 2, zs) + meta.shape)
    meta_all = jnp.where(core == 1, meta_all[:, ::-1], meta_all)
    meta_all = jnp.stack(behind(jnp.moveaxis(meta_all, 2, 0), zs), axis=2)
    meta_all = meta_all.reshape((high * high, 2 * zs) + meta.shape)

    length = zs * tok_rows
    heads = query_width // HEAD
    groups = kv_width // HEAD
    places = lax.rem(z + zs - jnp.arange(zs, dtype=jnp.int32), zs)
    cosine, sine = rotary_tables(length)
    qkv = None
    for j, piece in enumerate(seq_pieces):
        qkv = project(places[j], piece, w_in, cosine, sine, query_width + kv_width, qkv)
    attended, lse = attend(qkv, heads, groups)
    attended = attended.reshape(zs, tok_rows, query_width)
    attended, grad_first = tie(attended, grad_first)
    attended_own = exchange(attended, "z")
    mask_all, scale_all = chosen_tables(
        meta_all[:, :, :pick_count], meta_all[:, :, pick_count:], expert_count
    )
    side = 2 * high
    numbers = []
    for dy, dx in ((0, 0), (0, 1), (1, 0), (1, 1)):
        chip = (yh * 2 + (yl ^ dy)) * side + xh * 2 + (xl ^ dx)
        numbers.append((chip * 2 + core) * zs + z)
    mine = jnp.stack(numbers)[None, :] == jnp.arange(expert_count)[:, None]
    mask_mine = jnp.any(mine[:, :, None] & mask_all[:, :, :, None], axis=2)
    earlier = (jnp.arange(tok_rows)[:, None] < jnp.arange(tok_rows)[None, :]).astype(BF16)
    rank = jnp.einsum(
        "gpes,st->gpet", mask_mine.astype(BF16), earlier, preferred_element_type=F32
    )
    place = jnp.where(mask_mine, rank, -1.0)
    place_of_token = jnp.where(
        mask_mine, rank + (jnp.arange(4, dtype=F32) * slots)[:, None], -1.0
    ).swapaxes(2, 3)

    tables = (place, place_of_token, mask_all.astype(F32), scale_all)
    attended_own, tables = tie(attended_own, tables)
    place, place_of_token, mask_low, scale_all = tables
    middle, normed_two_low = branch_norm(jnp.arange(zs), attended_own, w_out, hidden_in, norm2_gain)

    rows_pieces = [normed_two_low, line_step(normed_two_low, zs)]
    rows_pieces[1], *weights_d = tie(rows_pieces[1], *take_pieces(*weights_x, *weights_y))
    for step in range(3):
        weights_d[step] = swap(weights_d[step], "yl")
        weights_d[3 + step] = swap(weights_d[3 + step], "xl")
        if step < 2:
            rows_pieces.append(line_step(rows_pieces[-1], zs))
            rows_pieces[-1], weights_d[step], weights_d[3 + step] = tie(
                rows_pieces[-1], weights_d[step], weights_d[3 + step]
            )
    grad_first, rows_pieces[-1] = tie(grad_first, rows_pieces[-1])
    grad_next = line_step(grad_first, zs)
    rows_pieces = rows_pieces + [swap(piece, "core") for piece in rows_pieces]
    rows_pieces = spread(rows_pieces, sizes)
    *by_slot, gates = experts_forward(
        0,
        rows_pieces,
        place,
        (mask_low, scale_all, mine.astype(F32), w_router.T),
        (weights_o, weights_x, weights_y),
        slots,
    )
    by_slot[0], grad_next = tie(by_slot[0], grad_next)
    grad_last = line_step(grad_next, zs)
    out_slots, *saved = experts_forward(
        3, rows_pieces, place, (gates,), (weights_d,), slots, by_slot
    )
    out_order = ((0, 0), (0, 1), (0, 2), (0, 3))
    out_parts = [out_slots]

    def out_other(start, count):
        return combine(place_of_token, out_parts, out_order, slots, 1, start, count)

    def out_own(start, count, other):
        return only_own(
            combine(place_of_token, out_parts, out_order, slots, 0, start, count, other), sizes
        )

    out_near, out_far = out_other(1, 1), out_other(2, zs - 1)
    out_near, out_far, grad_last = swap(out_near, "core"), *tie(out_far, grad_last)
    out_far = swap(out_far, "core")
    (term,) = out_own(1, 1, out_near)
    grad_pieces = [grad_low, grad_first, grad_next, grad_last]
    grad_pieces = grad_pieces + [swap(piece, "core") for piece in grad_pieces]
    term, grad_pieces = tie(term, grad_pieces)
    grad_pieces = spread(grad_pieces, sizes)
    out_run = line_step(term, zs)
    rows_dx, gate_dx, *grads = experts_backward(
        3, grad_pieces, place, gates, saved, (weights_d, weights_x), slots
    )
    gd, gx = grads[:6], grads[6:]
    gd[0], gd[3] = swap(gd[0], "yl"), swap(gd[3], "xl")
    gd[1], gd[4] = swap(gd[1], "yl"), swap(gd[4], "xl")
    out_far, out_run, rows_dx = tie(out_far, out_run, rows_dx)
    out_terms = out_own(2, zs - 1, out_far)
    out_run, gates = tie(out_terms[0] + out_run, gates)
    out_run = line_step(out_run, zs)
    rows_yo, gate_yo, *grads = experts_backward(
        2, grad_pieces, place, gates, saved, (weights_y, weights_o), slots
    )
    gy, go = grads[:6], grads[6:]
    out_run, rows_yo, gd[0], gd[3], gd[1], gd[4] = tie(
        out_terms[1] + out_run, rows_yo, gd[0], gd[3], gd[1], gd[4]
    )
    gd[2], gd[5] = swap(gd[2], "yl"), swap(gd[5], "xl")
    moe_parts, moe_order = [rows_dx, rows_yo], ((1, 1), (0, 1), (1, 0), (0, 0))
    more = ((gate_dx, gate_yo), mine.astype(F32))

    def moe_other(start, count):
        return combine(place_of_token, moe_parts, moe_order, slots, 1, start, count, None, *more)

    def moe_own(start, count, other):
        return only_own(
            combine(place_of_token, moe_parts, moe_order, slots, 0, start, count, other, *more),
            sizes,
        )

    moe_near, moe_far = moe_other(1, 1), moe_other(2, zs - 1)
    moe_near, moe_far = swap(moe_near, "core"), swap(moe_far, "core")
    (term,) = moe_own(1, 1, moe_near)
    term, *moe_parts = tie(term, *moe_parts)
    moe_run = line_step(term, zs)
    moe_terms = moe_own(2, zs - 1, moe_far)
    moe_run, gd[2], gd[5] = tie(moe_terms[0] + moe_run, gd[2], gd[5])
    gx[3], gy[0] = swap(gx[3], "xl"), swap(gy[0], "yl")
    moe_run = line_step(moe_run, zs)
    moe_run, gx[3], gy[0] = tie(moe_terms[1] + moe_run, gx[3], gy[0])
    gx[4], gy[1] = swap(gx[4], "xl"), swap(gy[1], "yl")
    moe_run = line_step(moe_run, zs)

    mask_own, scale_own = chosen_tables(meta[:pick_count], meta[pick_count:], expert_count)
    logits_own = dot(w_router, normed_two_low, ((0,), (1,)))
    prob_own = masked_softmax(logits_own, mask_own, 0)
    unit = max(8, dp_count * zs * 128 // math.gcd(model_width, dp_count * zs * 128))
    sum_rows = -(-(expert_count + 2) // unit) * unit
    prob_own, scale_own, moe_terms[1] = tie(prob_own, scale_own, moe_terms[1])
    for i in range(3):
        gx[i], gy[3 + i] = gx[i] + gd[i], gy[3 + i] + gd[3 + i]
    moe_run, gx[4], gy[1], *both = tie(moe_run, gx[4], gy[1], *gx[:3], *gy[3:])
    gx[:3], gy[3:] = both[:3], both[3:]
    gx[5], gy[2] = swap(gx[5], "xl"), swap(gy[2], "yl")
    gx[0], gy[3] = swap(gx[0], "xl"), swap(gy[3], "yl")
    grad_middle, grad_branch, grad_attended, early_sums = moe_back(
        jnp.arange(zs),
        sum_rows,
        moe_terms[2],
        moe_run,
        prob_own,
        scale_own,
        w_router.T,
        normed_two_low,
        middle,
        norm2_gain,
        out_grad,
        w_out,
    )

    grad_w_out = product_by_blocks(grad_branch, attended_own)
    shard_out = lax.psum_scatter(grad_w_out, ROWS, scatter_dimension=0, tiled=True)
    grad_attended = exchange(grad_attended, "z")
    out_run, grad_attended, _, gx[5], gy[2] = tie(
        out_run, grad_attended, grad_w_out, gx[5], gy[2]
    )
    gx[1], gy[4] = swap(gx[1], "xl"), swap(gy[4], "yl")
    out_run = line_step(out_run, zs)
    grad_proj = attend_back(
        qkv, lse, grad_attended.reshape(length, query_width), cosine, sine, heads, groups
    )
    out_run, grad_proj = tie(out_run, grad_proj)
    terms = [
        dot(g, w_in, ((1,), (1,))).astype(BF16)
        for g in behind(grad_proj.reshape(zs, tok_rows, -1), zs)
    ]
    terms[1], grad_proj = tie(terms[1], grad_proj)
    run = line_step(terms[1], zs)
    grad_w_in, gain_rows = project_back(places, seq_pieces, grad_proj, w_in)
    run, grad_w_in, gain_rows, gx[0], gy[3], *terms = tie(
        run, grad_w_in, gain_rows, gx[0], gy[3], *terms
    )
    gx[2], gy[5] = swap(gx[2], "xl"), swap(gy[5], "yl")
    run = line_step(terms[2] + run, zs)

    sums = lax.dynamic_update_slice(early_sums, gain_rows[:1], (expert_count + 1, 0))
    sums = sums.reshape(dp_count * zs, -1, 128)
    shard_out, grad_w_in = tie(shard_out, grad_w_in)
    shard_in = lax.psum_scatter(grad_w_in, ROWS, scatter_dimension=0, tiled=True)
    shard_out = shard_out.reshape(-1, zs, query_width).transpose(1, 0, 2)
    chunks = behind(shard_out, zs)
    for step in range(1, zs):
        chunks[step] = lax.ppermute(
            chunks[step], "z", [(i, (i + zs - step) % zs) for i in range(zs)]
        )
    sums = jnp.sum(exchange(sums, ALL), axis=0)
    output = middle + RESIDUAL_SCALE * (out_terms[2].astype(F32) + out_run.astype(F32))
    run, gx[1], gy[4], gx[2], gy[5], output, *chunks = tie(
        terms[3] + run, gx[1], gy[4], gx[2], gy[5], output, *chunks
    )
    run = line_step(run, zs)
    grad_w_gate_up, grad_w_down = collect(
        [(go[i], gx[i], gy[i]) for i in range(6)], model_width
    )

    sums, grad_w_gate_up, grad_w_down = tie(sums, grad_w_gate_up, grad_w_down)
    sums = share(sums, ALL, dp_count * zs)
    run, grad_w_gate_up, grad_w_down = tie(run, grad_w_gate_up, grad_w_down)
    grad_hidden = finish(terms[0], run, hidden_in, norm1_gain, grad_middle)
    grad_hidden, sums = tie(grad_hidden, sums)
    sums = sums.reshape(sum_rows, model_width)
    shard_output = sum(chunk.astype(F32) for chunk in chunks).T
    shard_query, shard_keyvalue = split_columns(shard_in, query_width)
    return (
        output,
        grad_hidden,
        sums[expert_count + 1] / norm1_gain,
        shard_query,
        shard_keyvalue,
        shard_output,
        sums[expert_count],
        sums[:expert_count].T,
        grad_w_gate_up,
        grad_w_down,
    )


def solution(mesh):
    high = math.isqrt(mesh.shape["dp"] // 2) // 2
    zs = mesh.shape["tensor"]
    inner = Mesh(mesh.devices.reshape(high, 2, high, 2, 2, zs), ALL)
    sizes = dict(inner.shape)
    in_specs = (
        P(ALL, None),
        P(),
        P(ROWS, "z"),
        P(None, ROWS, "z"),
        P("z", ROWS),
        P(),
        P(),
        P(ALL, None, None, None),
        P(ALL, None, None),
        P(ALL, None),
        P(ALL, None),
        P(ALL, None),
    )
    out_specs = (
        P(ALL, None),
        P(ALL, None),
        P(),
        P(ROWS, "z"),
        P(None, ROWS, "z"),
        P("z", ROWS),
        P(),
        P(),
        P(ALL, None, None, None),
        P(ALL, None, None),
    )
    return jax.shard_map(
        functools.partial(local, sizes),
        mesh=inner,
        in_specs=in_specs,
        out_specs=out_specs,
        check_vma=False,
    )
```
